32 devices in a mesh: dp: 4 (over y, x), expert: 8 (over z, core).
Axes of the slice: x: 2, y: 2, z: 4, core: 2. Of those that a mesh axis runs over, the one named last changes fastest.
Arguments:
- grad_out: bfloat16 [4096, 2048], P(('dp', 'expert')), may hold values from -6 to 6
- probs: bfloat16 [4096, 2], P(('dp', 'expert')), may hold values from 0.019897461 to 0.5
- routes: int32 [4096, 2], P(('dp', 'expert')), may hold values from 0 to 7, all different within a row; in each aligned block of 128 rows (0 to 127, 128 to 255, ...) at most 48 rows name the same one
- saved_gate: bfloat16 [4, 8, 8, 48, 768], P('dp', 'expert'), may hold values from -6 to 6
- saved_up: bfloat16 [4, 8, 8, 48, 768], P('dp', 'expert'), may hold values from -6 to 6
- w_down: bfloat16 [8, 768, 2048], P('expert'), may hold values from -0.21875 to 0.21875
Outputs:
- grad_gate: bfloat16 [4, 8, 8, 48, 768], P('dp', 'expert')
- grad_up: bfloat16 [4, 8, 8, 48, 768], P('dp', 'expert')
- grad_weight: float32 [8, 768, 2048], P('expert', 'dp')
- route_grad: float32 [4096, 2], P(('dp', 'expert'))
The draws below stay inside these ranges and needn't reach their ends.
Inputs may be any that keep to these rules, and one draw needn't show every extreme that they name: A token's 2 routes name different experts. Among one device's 128 tokens no expert is named by more than 48 routes, a bound that some block reaches.
All inputs are finite; a program needn't handle non-finite values.
Results may differ from the reference program's by a relative error of at most 0.0049.
Values may be sent and summed in bfloat16 or wider, within the bound.
No kernel may reach another device: no remote copies, remote signals or barrier semaphores. Data moves between devices by JAX's collectives and lax.ppermute only.
A program may use at most 64 MiB of HBM per device.

```python
import math
import jax
import jax.numpy as jnp
import numpy as np
from jax import lax

D = 2048
FF = 768
TOP = 2
TOK_DEV = 128
EXPERTS = 8
CAP = 48
TOKENS = 4096
N_DP = 4
N_EXPERT = 8


def levels(rng, dims, split, least, high):
    def one(dim, shards_of):
        draws = jax.random.uniform(jax.random.fold_in(jax.random.fold_in(rng, 6), dim), (shards_of,), jnp.float32, least / len(split), high / len(split))
        return jnp.repeat(jnp.exp(draws), dims[dim] // shards_of).reshape((-1,) + (1,) * (len(dims) - dim - 1))

    loudness = one(*split[0])
    for cut in split[1:]:
        loudness = loudness * one(*cut)
    return loudness


def routed_block(own_key, own, number, rows, count, top, limit, skew):
    ranking = jax.random.permutation(own_key, count)
    crowded, usual = load_shares(count, rows * top, limit, skew, True), load_shares(count, rows * top, limit, skew, False)
    places = jnp.arange(count)

    def named(sizes, rotation):
        used = int((sizes > 0).sum())
        fixed = max(1, used // 4)
        passed = fixed + (places - fixed + rotation * (used - fixed)) % max(1, count - fixed)
        return jnp.zeros((count,), jnp.int32).at[ranking[jnp.where(places < fixed, places, passed)]].set(jnp.asarray(sizes, jnp.int32))

    sizes = jnp.where(number % 4 == 0, named(crowded, number // 4), named(usual, number - number // 4 - 1))
    mixed = jax.random.permutation(jax.random.fold_in(own, 3), count)
    source_of, receiver = mixed[0:count // 2 * 2:2], mixed[1:count // 2 * 2:2]
    margin = jnp.minimum(sizes[source_of] - 1, limit - sizes[receiver]) // 2
    margin = jnp.where((source_of == ranking[0]) | (receiver == ranking[0]) | (sizes[receiver] == 0), 0, jnp.maximum(margin, 0))
    passed = jax.random.randint(jax.random.fold_in(own, 4), (count // 2,), 0, 1 << 20) % (margin + 1)
    sizes = sizes.at[source_of].add(-passed).at[receiver].add(passed)
    members = jnp.searchsorted(jnp.cumsum(sizes), jnp.arange(rows * top), side="right").astype(jnp.int32)
    table = members.reshape(top, rows).T
    table = table[jax.random.permutation(jax.random.fold_in(own, 1), rows)]
    rotation = jax.random.randint(jax.random.fold_in(own, 2), (rows, 1), 0, top)
    return jnp.take_along_axis(table, (jnp.arange(top)[None, :] + rotation) % top, axis=1)


def load_shares(amount, total, reach, slope, full):
    weights = [(1 << 20) // math.isqrt(grade ** slope) + 1 for grade in range(1, amount + 1)]
    largest = reach if full else min(reach, max(-(-total // amount), total * weights[0] // sum(weights)))
    least = 1 if total - largest >= amount - 1 else 0
    holding, spare = [largest] + [least] * (amount - 1), total - largest - least * (amount - 1)
    while spare > 0:
        candidates = [i for i in range(1, amount) if holding[i] < largest] or [i for i in range(1, amount) if holding[i] < reach]
        pool, left = sum([weights[i] for i in candidates]), spare
        for i in candidates:
            more = min(reach - holding[i], max(1, left * weights[i] // pool), spare)
            holding[i] = holding[i] + more
            spare = spare - more
    return np.array(holding)


def normal_values(own_key, extent, deviation, limit, split=(), kind=jnp.bfloat16):
    drawn = jax.random.normal(own_key, extent, jnp.float32) * deviation
    if len(split) > 0:
        drawn = levels(own_key, extent, split, -0.22, 0.18) * drawn
    return jnp.clip(drawn, min=-limit, max=limit).astype(kind)


def setup_inputs(seed: int = 0) -> dict:
    splits = jax.random.split(jax.random.key(seed), 7)
    grad_out = normal_values(splits[0], (TOKENS, D), 1.0, 6.0, ((0, 32),))
    probs = jnp.clip(jnp.exp(math.log(0.5) - 3.224016 * jax.random.uniform(splits[1], (TOKENS, TOP), jnp.float32) ** levels(splits[1], (TOKENS, TOP), ((0, 32),), -0.2, 0.2)), 0.019897461, 0.5).astype(jnp.bfloat16)
    routes_keys = jax.random.split(jax.random.fold_in(splits[2], 1), TOKENS // TOK_DEV)
    routes_turns = jax.random.permutation(jax.random.fold_in(splits[2], 3), TOKENS // TOK_DEV)
    routes = jax.vmap(lambda own, number: routed_block(jax.random.fold_in(splits[2], 2), own, number, TOK_DEV, EXPERTS, TOP, CAP, 2))(routes_keys, routes_turns).reshape((TOKENS, TOP))
    saved_gate = normal_values(splits[3], (N_DP, EXPERTS, N_EXPERT, CAP, FF), 1.0, 6.0, ((0, 4), (1, 8)))
    saved_up = normal_values(splits[4], (N_DP, EXPERTS, N_EXPERT, CAP, FF), 1.0, 6.0, ((0, 4), (1, 8)))
    w_down = normal_values(splits[5], (EXPERTS, FF, D), FF ** -0.5, 0.21875, ((0, 8),))
    return dict(grad_out=grad_out, probs=probs, routes=routes, saved_gate=saved_gate, saved_up=saved_up, w_down=w_down)


def silu_parts(gate_value):
    sigmoid = jax.nn.sigmoid(gate_value)
    return gate_value * sigmoid, sigmoid * (1.0 + gate_value * (1.0 - sigmoid))


def positions_of(route_block):
    flat_routes = route_block.reshape(-1).astype(jnp.int32)
    onehot = (flat_routes[:, None] == jnp.arange(EXPERTS, dtype=jnp.int32)[None, :]).astype(jnp.int32)
    before = jnp.cumsum(onehot, axis=0) - onehot
    slot_index = jnp.sum(before * onehot, axis=1).astype(jnp.int32)
    return (flat_routes * CAP + slot_index).astype(jnp.int32)


def dispatch(grad_block, prob_block, route_block):
    position = positions_of(route_block)
    repeated = jnp.repeat(grad_block, TOP, axis=0)
    sent_grad = jnp.zeros((EXPERTS * CAP, D), grad_block.dtype).at[position].set(repeated)
    sent_prob = jnp.zeros((EXPERTS * CAP,), prob_block.dtype).at[position].set(prob_block.reshape(-1))
    return sent_grad.reshape(EXPERTS, CAP, D), sent_prob.reshape(EXPERTS, CAP), position


def pick_slots(slot_values, positions):
    return jnp.take(slot_values, positions, axis=0)


def reference(grad_out, probs, routes, saved_gate, saved_up, w_down):
    grad_groups = grad_out.reshape(N_DP, N_EXPERT, TOK_DEV, D)
    prob_groups = probs.reshape(N_DP, N_EXPERT, TOK_DEV, TOP)
    route_groups = routes.reshape(N_DP, N_EXPERT, TOK_DEV, TOP)
    weight = w_down.astype(jnp.float32)

    def group_step(panel_sum, inputs):
        grad_rows, prob_rows, route_rows, gate_group, up_group = inputs
        sent_grad, sent_prob, position = jax.vmap(dispatch)(grad_rows, prob_rows, route_rows)
        sent_grad = jnp.swapaxes(sent_grad, 0, 1)
        sent_prob = jnp.swapaxes(sent_prob, 0, 1)
        gate_value = gate_group.astype(jnp.float32)
        up_value = up_group.astype(jnp.float32)
        activation, gate_slope = silu_parts(gate_value)
        hidden = (activation * up_value).astype(jnp.bfloat16)
        hidden_wide = hidden.astype(jnp.float32)
        grad_wide = sent_grad.astype(jnp.float32)
        expert_out = jnp.einsum("esck,ekd->escd", hidden_wide, weight)
        slot_grad = jnp.sum(grad_wide * expert_out, axis=-1)
        scaled = (sent_prob.astype(jnp.float32)[..., None] * grad_wide).astype(jnp.bfloat16)
        scaled_wide = scaled.astype(jnp.float32)
        grad_hidden = jnp.einsum("escd,ekd->esck", scaled_wide, weight)
        grad_up = (grad_hidden * activation).astype(jnp.bfloat16)
        grad_gate = (grad_hidden * up_value * gate_slope).astype(jnp.bfloat16)
        panel_sum = panel_sum + jnp.einsum("esck,escd->ekd", hidden_wide, scaled_wide)
        per_source = jnp.swapaxes(slot_grad, 0, 1).reshape(N_EXPERT, EXPERTS * CAP)
        route_grad = jax.vmap(pick_slots)(per_source, position)
        return panel_sum, (grad_gate, grad_up, route_grad.reshape(N_EXPERT, TOK_DEV, TOP))

    start_panel = jnp.zeros((EXPERTS, FF, D), jnp.float32)
    grad_weight, outputs = lax.scan(group_step, start_panel, (grad_groups, prob_groups, route_groups, saved_gate, saved_up))
    grad_gate, grad_up, route_grad = outputs
    return grad_gate, grad_up, grad_weight, route_grad.reshape(TOKENS, TOP)
```

```python
import functools

import jax
import jax.numpy as jnp
from jax import lax
from jax.experimental import pallas as pl
from jax.experimental.pallas import tpu as pltpu
from jax.sharding import PartitionSpec as P

LANES = 128
CHUNKS = 4
VMEM_LIMIT = 32 * 1024 * 1024


def params():
    return pltpu.CompilerParams(vmem_limit_bytes=VMEM_LIMIT)


def cost(flops, moved):
    return pl.CostEstimate(flops=flops, bytes_accessed=moved, transcendentals=0)


def silu_parts(gate_value):
    sigmoid = jax.nn.sigmoid(gate_value)
    return (gate_value * sigmoid, sigmoid * (1.0 + gate_value * (1.0 - sigmoid)))


def dispatch_kernel(expert_count, capacity, routes_ref, probs_ref, grad_ref, slot_ref, *sent_refs):
    token_count, top_count = routes_ref.shape
    row_count = expert_count * capacity
    experts = lax.broadcasted_iota(jnp.int32, (token_count, expert_count), 1)
    named = [routes_ref[:, k : k + 1] for k in range(top_count)]
    onehots = [(experts == name).astype(jnp.float32) for name in named]
    earlier = (
        lax.broadcasted_iota(jnp.int32, (token_count, token_count), 0)
        > lax.broadcasted_iota(jnp.int32, (token_count, token_count), 1)
    ).astype(jnp.bfloat16)
    before = jnp.dot(
        earlier, sum(onehots).astype(jnp.bfloat16), preferred_element_type=jnp.float32
    )
    slots = lax.broadcasted_iota(jnp.int32, (token_count, row_count), 1)
    selector = jnp.zeros((token_count, row_count), jnp.float32)
    for k in range(top_count):
        slot = jnp.sum(before * onehots[k], axis=1, keepdims=True).astype(jnp.int32)
        before = before + onehots[k]
        slot_ref[:, k : k + 1] = slot
        prob = probs_ref[:, k : k + 1].astype(jnp.float32)
        selector = selector + jnp.where(slots == named[k] * capacity + slot, prob, 0.0)
    selector = selector.T.astype(jnp.bfloat16)
    start = 0
    for sent_ref in sent_refs:
        width = sent_ref.shape[1]
        sent_ref[...] = jnp.dot(
            selector, grad_ref[:, start : start + width], preferred_element_type=jnp.float32
        ).astype(jnp.bfloat16)
        start += width


def dispatch(routes, probs, grad_out, expert_count, capacity, widths):
    token_count, top_count = routes.shape
    row_count = expert_count * capacity
    model_width = grad_out.shape[1]
    return pl.pallas_call(
        functools.partial(dispatch_kernel, expert_count, capacity),
        out_shape=[jax.ShapeDtypeStruct((token_count, top_count), jnp.int32)]
        + [jax.ShapeDtypeStruct((row_count, width), jnp.bfloat16) for width in widths],
        compiler_params=params(),
        cost_estimate=cost(
            2 * row_count * token_count * model_width, 2 * (row_count + token_count) * model_width
        ),
    )(routes, probs, grad_out)


def hidden_kernel(gate_ref, up_ref, hidden_ref):
    activation, _ = silu_parts(gate_ref[...].astype(jnp.float32))
    hidden = activation * up_ref[...].astype(jnp.float32)
    hidden_ref[...] = hidden.T.astype(jnp.bfloat16)


def hidden_transposed(gate, up):
    row_count, hidden_width = gate.shape
    step = 2 * LANES
    return pl.pallas_call(
        hidden_kernel,
        grid=(hidden_width // step,),
        in_specs=[pl.BlockSpec((row_count, step), lambda i: (0, i))] * 2,
        out_specs=pl.BlockSpec((step, row_count), lambda i: (i, 0)),
        out_shape=jax.ShapeDtypeStruct((hidden_width, row_count), jnp.bfloat16),
        compiler_params=params(),
        cost_estimate=cost(20 * row_count * hidden_width, 6 * row_count * hidden_width),
    )(gate, up)


def panel_kernel(group_count, group_ref, hidden_ref, rows_ref, own_ref, *sent_refs):
    share = own_ref.shape[0]
    rows = rows_ref[...]
    for step in list(range(1, group_count)) + [0]:
        owner = lax.bitwise_xor(group_ref[0], step)
        start = pl.multiple_of(owner * share, share)
        part = jnp.dot(
            hidden_ref[pl.ds(start, share), :], rows, preferred_element_type=jnp.float32
        )
        if step == 0:
            own_ref[...] = part
        else:
            sent_refs[step - 1][...] = part.astype(jnp.bfloat16)


def panel_parts(group, hidden, rows, group_count):
    hidden_width, row_count = hidden.shape
    width = rows.shape[1]
    share = hidden_width // group_count
    vmem = pl.BlockSpec(memory_space=pltpu.VMEM)
    return pl.pallas_call(
        functools.partial(panel_kernel, group_count),
        in_specs=[pl.BlockSpec(memory_space=pltpu.SMEM), vmem, vmem],
        out_shape=[jax.ShapeDtypeStruct((share, width), jnp.float32)]
        + [jax.ShapeDtypeStruct((share, width), jnp.bfloat16)] * (group_count - 1),
        compiler_params=params(),
        cost_estimate=cost(
            2 * hidden_width * row_count * width, 2 * hidden_width * (row_count + width)
        ),
    )(group, hidden, rows)


def total_kernel(own_ref, *refs):
    total = own_ref[...]
    for ref in refs[: len(refs) - 1]:
        total = total + ref[...].astype(jnp.float32)
    refs[-1][...] = total


def total_chunk(held, own, arrived, start, model_width):
    share, width = own.shape
    place = pl.BlockSpec((share, width), lambda i: (0, start // width))
    inputs = [own] + list(arrived)
    specs = [pl.BlockSpec((share, width), lambda i: (0, 0))] * len(inputs)
    kernel = total_kernel
    aliases = {}
    if held is not None:
        inputs = [held] + inputs
        specs = [pl.BlockSpec(memory_space=pl.ANY)] + specs
        aliases = {0: 0}

        def kernel(held_ref, *refs):
            total_kernel(*refs)

    return pl.pallas_call(
        kernel,
        grid=(1,),
        in_specs=specs,
        out_specs=place,
        out_shape=jax.ShapeDtypeStruct((share, model_width), jnp.float32),
        input_output_aliases=aliases,
        compiler_params=params(),
        cost_estimate=cost(4 * share * width, 14 * share * width),
    )(*inputs)


def rows_times_weight(rows_ref, weight_ref):
    return lax.dot_general(
        rows_ref[...],
        weight_ref[...],
        (((1,), (1,)), ((), ())),
        preferred_element_type=jnp.float32,
    )


def first_kernel(rows_ref, weight_ref, sum_ref):
    sum_ref[...] = rows_times_weight(rows_ref, weight_ref)


def middle_kernel(held_ref, rows_ref, weight_ref, sum_ref):
    sum_ref[...] = held_ref[...] + rows_times_weight(rows_ref, weight_ref)


def grad_hidden_step(held, rows, weight, start):
    row_count, width = rows.shape
    hidden_width = weight.shape[0]
    step = 2 * LANES
    block = pl.BlockSpec((row_count, step), lambda i: (0, i))
    specs = [
        pl.BlockSpec((row_count, width), lambda i: (0, 0)),
        pl.BlockSpec((step, width), lambda i: (i, start // width)),
    ]
    return pl.pallas_call(
        first_kernel if held is None else middle_kernel,
        grid=(hidden_width // step,),
        in_specs=specs if held is None else [block] + specs,
        out_specs=block,
        out_shape=jax.ShapeDtypeStruct((row_count, hidden_width), jnp.float32),
        compiler_params=params(),
        cost_estimate=cost(
            2 * row_count * hidden_width * width, 8 * row_count * hidden_width
        ),
    )(*([rows, weight] if held is None else [held, rows, weight]))


def last_kernel(
    capacity,
    held_ref,
    rows_ref,
    weight_ref,
    gate_ref,
    up_ref,
    grad_gate_ref,
    grad_up_ref,
    slot_ref,
    sum_ref,
):
    place = pl.program_id(0)
    grad_hidden = held_ref[...] + rows_times_weight(rows_ref, weight_ref)
    activation, gate_slope = silu_parts(gate_ref[...].astype(jnp.float32))
    up_value = up_ref[...].astype(jnp.float32)
    grad_up_ref[...] = (grad_hidden * activation).astype(jnp.bfloat16)
    grad_gate_ref[...] = (grad_hidden * up_value * gate_slope).astype(jnp.bfloat16)
    hidden = (activation * up_value).astype(jnp.bfloat16).astype(jnp.float32)
    product = hidden * grad_hidden
    folded = product[:, :LANES]
    for start in range(LANES, product.shape[1], LANES):
        folded = folded + product[:, start : start + LANES]

    @pl.when(place == 0)
    def _():
        sum_ref[...] = folded

    @pl.when(place > 0)
    def _():
        sum_ref[...] = sum_ref[...] + folded

    @pl.when(place == pl.num_programs(0) - 1)
    def _():
        line = jnp.sum(sum_ref[...].T, axis=0, keepdims=True)
        slot_ref[...] = jnp.zeros_like(slot_ref)
        for source in range(slot_ref.shape[0]):
            slot_ref[source, 0:1, 0:capacity] = line[:, source * capacity : (source + 1) * capacity]


def grad_hidden_last(held, rows, weight, start, gate, up, expert_count, capacity):
    row_count, width = rows.shape
    hidden_width = weight.shape[0]
    step = 2 * LANES
    lanes = -(-capacity // LANES) * LANES
    block = pl.BlockSpec((row_count, step), lambda i: (0, i))
    return pl.pallas_call(
        functools.partial(last_kernel, capacity),
        grid=(hidden_width // step,),
        in_specs=[
            block,
            pl.BlockSpec((row_count, width), lambda i: (0, 0)),
            pl.BlockSpec((step, width), lambda i: (i, start // width)),
            block,
            block,
        ],
        out_specs=[
            block,
            block,
            pl.BlockSpec((expert_count, 8, lanes), lambda i: (0, 0, 0)),
        ],
        out_shape=[
            jax.ShapeDtypeStruct((row_count, hidden_width), jnp.bfloat16),
            jax.ShapeDtypeStruct((row_count, hidden_width), jnp.bfloat16),
            jax.ShapeDtypeStruct((expert_count, 8, lanes), jnp.float32),
        ],
        scratch_shapes=[pltpu.VMEM((row_count, LANES), jnp.float32)],
        compiler_params=params(),
        cost_estimate=cost(
            2 * row_count * hidden_width * width, 12 * row_count * hidden_width
        ),
    )(held, rows, weight, gate, up)


def route_kernel(returned_ref, routes_ref, slot_ref, probs_ref, out_ref):
    token_count, top_count = routes_ref.shape
    lanes = returned_ref.shape[2]
    places = lax.broadcasted_iota(jnp.int32, (token_count, lanes), 1)
    for k in range(top_count):
        name = routes_ref[:, k : k + 1]
        line = jnp.zeros((token_count, lanes), jnp.float32)
        for expert in range(returned_ref.shape[0]):
            line = jnp.where(name == expert, returned_ref[expert, 0:1, :], line)
        line = jnp.where(places == slot_ref[:, k : k + 1], line, 0.0)
        picked = jnp.sum(line, axis=1, keepdims=True)
        out_ref[:, k : k + 1] = picked / probs_ref[:, k : k + 1].astype(jnp.float32)


def shards(grad_out, probs, routes, saved_gate, saved_up, w_down):
    expert_count = lax.axis_size("expert")
    group_count = lax.axis_size("dp")
    capacity = saved_gate.shape[3]
    hidden_width = saved_gate.shape[4]
    model_width = grad_out.shape[1]
    row_count = expert_count * capacity
    share = hidden_width // group_count
    width = model_width // CHUNKS
    starts = [chunk * width for chunk in range(CHUNKS)]
    direct = share % 16 == 0 and group_count & (group_count - 1) == 0

    slot, *sent = dispatch(routes, probs, grad_out, expert_count, capacity, [width] * CHUNKS)
    gate = saved_gate.reshape(row_count, hidden_width)
    up = saved_up.reshape(row_count, hidden_width)
    weight = w_down[0]
    hidden = hidden_transposed(gate, up)
    group = lax.axis_index("dp").reshape(1)
    held = None
    panel = None
    panels = []
    for chunk, start in enumerate(starts):
        rows = lax.all_to_all(
            sent[chunk].reshape(expert_count, capacity, width),
            "expert",
            split_axis=0,
            concat_axis=0,
            tiled=True,
        ).reshape(row_count, width)
        if direct:
            own, *parts = panel_parts(group, hidden, rows, group_count)
            arrived = [
                lax.ppermute(part, "dp", [(g, g ^ (step + 1)) for g in range(group_count)])
                for step, part in enumerate(parts)
            ]
            panel = total_chunk(panel, own, arrived, start, model_width)
        else:
            whole = jnp.dot(hidden, rows, preferred_element_type=jnp.float32)
            panels.append(lax.psum_scatter(whole, "dp", scatter_dimension=0, tiled=True))
        if chunk + 1 < CHUNKS:
            held = grad_hidden_step(held, rows, weight, start)
        else:
            grad_gate, grad_up, slot_grad = grad_hidden_last(
                held, rows, weight, start, gate, up, expert_count, capacity
            )
    if not direct:
        panel = jnp.concatenate(panels, axis=1)
    returned = lax.all_to_all(slot_grad, "expert", split_axis=0, concat_axis=0, tiled=True)
    route_grad = pl.pallas_call(
        route_kernel,
        out_shape=jax.ShapeDtypeStruct(routes.shape, jnp.float32),
        compiler_params=params(),
        cost_estimate=cost(100000, 100000),
    )(returned, routes, slot, probs)
    return (
        grad_gate.reshape(saved_gate.shape),
        grad_up.reshape(saved_up.shape),
        panel[None],
        route_grad,
    )


def solution(mesh):
    return jax.shard_map(
        shards,
        mesh=mesh,
        in_specs=(
            P(("dp", "expert"), None),
            P(("dp", "expert"), None),
            P(("dp", "expert"), None),
            P("dp", "expert", None, None, None),
            P("dp", "expert", None, None, None),
            P("expert", None, None),
        ),
        out_specs=(
            P("dp", "expert", None, None, None),
            P("dp", "expert", None, None, None),
            P("expert", "dp", None),
            P(("dp", "expert"), None),
        ),
        check_vma=False,
    )
```

```python
import functools

import jax
import jax.numpy as jnp
from jax import lax
from jax.experimental import pallas as pl
from jax.experimental.pallas import tpu as pltpu
from jax.sharding import PartitionSpec as P

LANES = 128
CHUNKS = 4
VMEM_LIMIT = 10 * 1024 * 1024
VMEM = pl.BlockSpec(memory_space=pltpu.VMEM)
ANY = pl.BlockSpec(memory_space=pl.ANY)
SMEM = pl.BlockSpec(memory_space=pltpu.SMEM)


def params():
    return pltpu.CompilerParams(vmem_limit_bytes=VMEM_LIMIT)


def cost(flops, moved):
    return pl.CostEstimate(flops=flops, bytes_accessed=moved, transcendentals=0)


def silu_parts(gate_value):
    sigmoid = jax.nn.sigmoid(gate_value)
    return (gate_value * sigmoid, sigmoid * (1.0 + gate_value * (1.0 - sigmoid)))


def select_kernel(
    expert_count, capacity, place_ref, routes_ref, probs_ref, slot_ref, keep_ref, give_ref
):
    top_count, token_count = routes_ref.shape
    row_count = keep_ref.shape[0]
    names = [
        lax.bitwise_xor(routes_ref[k : k + 1, :], place_ref[0]) for k in range(top_count)
    ]
    experts = lax.broadcasted_iota(jnp.int32, (expert_count, token_count), 0)
    onehots = [(experts == name).astype(jnp.float32) for name in names]
    earlier = (
        lax.broadcasted_iota(jnp.int32, (token_count, token_count), 0)
        < lax.broadcasted_iota(jnp.int32, (token_count, token_count), 1)
    ).astype(jnp.bfloat16)
    before = jnp.dot(
        sum(onehots).astype(jnp.bfloat16), earlier, preferred_element_type=jnp.float32
    )
    slots = lax.broadcasted_iota(jnp.int32, (row_count, token_count), 0)
    keep = jnp.zeros((row_count, token_count), jnp.float32)
    give = jnp.zeros((row_count, token_count), jnp.float32)
    for k in range(top_count):
        slot = jnp.sum(before * onehots[k], axis=0, keepdims=True).astype(jnp.int32)
        before = before + onehots[k]
        slot_ref[k : k + 1, :] = slot
        prob = probs_ref[k : k + 1, :].astype(jnp.float32)
        row = lax.shift_right_logical(names[k], 1) * capacity + slot
        core = lax.bitwise_and(names[k], 1)
        keep = keep + jnp.where(slots == jnp.where(core == 0, row, -1), prob, 0.0)
        give = give + jnp.where(slots == jnp.where(core == 1, row, -1), prob, 0.0)
    keep_ref[...] = keep.astype(jnp.bfloat16)
    give_ref[...] = give.astype(jnp.bfloat16)


def select(place, routes, probs, expert_count, capacity):
    top_count, token_count = routes.shape
    row_count = expert_count // 2 * capacity
    matrix = jax.ShapeDtypeStruct((row_count, token_count), jnp.bfloat16)
    return pl.pallas_call(
        functools.partial(select_kernel, expert_count, capacity),
        in_specs=[SMEM, VMEM, VMEM],
        out_shape=[jax.ShapeDtypeStruct((top_count, token_count), jnp.int32), matrix, matrix],
        compiler_params=params(),
        cost_estimate=cost(20 * row_count * token_count, 8 * row_count * token_count),
    )(place, routes, probs)


def dispatch_kernel(
    capacity, start, width, later_count, keep_ref, own_ref, give_ref, other_ref, *refs
):
    block_refs = refs[later_count:]
    for half, (select_ref, rows_ref) in enumerate(((keep_ref, own_ref), (give_ref, other_ref))):
        rows = jnp.dot(
            select_ref[...],
            rows_ref[:, start : start + width],
            preferred_element_type=jnp.float32,
        ).astype(jnp.bfloat16)
        for step, block_ref in enumerate(block_refs):
            block_ref[half * capacity : (half + 1) * capacity, :] = rows[
                step * capacity : (step + 1) * capacity, :
            ]


def dispatch(keep, own, give, other, capacity, start, width, earlier):
    row_count, token_count = keep.shape
    return pl.pallas_call(
        functools.partial(dispatch_kernel, capacity, start, width, len(earlier)),
        in_specs=[VMEM] * 4 + [ANY] * len(earlier),
        out_shape=[jax.ShapeDtypeStruct((2 * capacity, width), jnp.bfloat16)]
        * (row_count // capacity),
        compiler_params=params(),
        cost_estimate=cost(
            4 * row_count * token_count * width, 4 * (row_count + token_count) * width
        ),
    )(keep, own, give, other, *earlier)


def hidden_kernel(gate_ref, up_ref, hidden_ref):
    activation, _ = silu_parts(gate_ref[...].astype(jnp.float32))
    hidden = activation * up_ref[...].astype(jnp.float32)
    hidden_ref[...] = hidden.T.astype(jnp.bfloat16)


def hidden_transposed(gate, up):
    row_count, hidden_width = gate.shape
    step = 2 * LANES
    return pl.pallas_call(
        hidden_kernel,
        grid=(hidden_width // step,),
        in_specs=[pl.BlockSpec((row_count, step), lambda i: (0, i))] * 2,
        out_specs=pl.BlockSpec((step, row_count), lambda i: (i, 0)),
        out_shape=jax.ShapeDtypeStruct((hidden_width, row_count), jnp.bfloat16),
        compiler_params=params(),
        cost_estimate=cost(20 * row_count * hidden_width, 6 * row_count * hidden_width),
    )(gate, up)


def panel_kernel(line_count, earlier_count, capacity, place_ref, hidden_ref, *refs):
    block_refs = refs[:line_count]
    rows_ref, own_ref, *sent_refs = refs[line_count + earlier_count :]
    group_count = len(sent_refs) + 1
    share = own_ref.shape[0]
    for step, block_ref in enumerate(block_refs):
        for half in range(2):
            source = lax.bitwise_xor(place_ref[0], 2 * step + half)
            start = pl.multiple_of(source * capacity, capacity)
            rows_ref[pl.ds(start, capacity), :] = block_ref[
                half * capacity : (half + 1) * capacity, :
            ]
    rows = rows_ref[...]
    for step in list(range(group_count - 1, -1, -1)):
        owner = lax.bitwise_xor(place_ref[1], step)
        start = pl.multiple_of(owner * share, share)
        part = jnp.dot(
            hidden_ref[pl.ds(start, share), :], rows, preferred_element_type=jnp.float32
        )
        if step == 0:
            own_ref[...] = part
        else:
            sent_refs[step - 1][...] = part.astype(jnp.bfloat16)


def panel_parts(place, hidden, blocks, group_count, earlier):
    hidden_width, row_count = hidden.shape
    width = blocks[0].shape[1]
    share = hidden_width // group_count
    return pl.pallas_call(
        functools.partial(panel_kernel, len(blocks), len(earlier), blocks[0].shape[0] // 2),
        in_specs=[SMEM, VMEM] + [VMEM] * len(blocks) + [ANY] * len(earlier),
        out_shape=[
            jax.ShapeDtypeStruct((row_count, width), jnp.bfloat16),
            jax.ShapeDtypeStruct((share, width), jnp.float32),
        ]
        + [jax.ShapeDtypeStruct((share, width), jnp.bfloat16)] * (group_count - 1),
        compiler_params=params(),
        cost_estimate=cost(
            2 * hidden_width * row_count * width, 2 * hidden_width * (row_count + width)
        ),
    )(place, hidden, *blocks, *earlier)


def total_kernel(own_ref, *refs):
    total = own_ref[...]
    for ref in refs[: len(refs) - 1]:
        total = total + ref[...].astype(jnp.float32)
    refs[-1][...] = total


def total_chunk(held, own, arrived, start, model_width):
    share, width = own.shape
    place = pl.BlockSpec((share, width), lambda i: (0, start // width))
    inputs = [own] + list(arrived)
    specs = [pl.BlockSpec((share, width), lambda i: (0, 0))] * len(inputs)
    kernel = total_kernel
    aliases = {}
    if held is not None:
        inputs = [held] + inputs
        specs = [pl.BlockSpec(memory_space=pl.ANY)] + specs
        aliases = {0: 0}

        def kernel(held_ref, *refs):
            total_kernel(*refs)

    return pl.pallas_call(
        kernel,
        grid=(1,),
        in_specs=specs,
        out_specs=place,
        out_shape=jax.ShapeDtypeStruct((share, model_width), jnp.float32),
        input_output_aliases=aliases,
        compiler_params=params(),
        cost_estimate=cost(4 * share * width, 14 * share * width),
    )(*inputs)


def rows_times_weight(rows_ref, weight_ref):
    return lax.dot_general(
        rows_ref[...],
        weight_ref[...],
        (((1,), (1,)), ((), ())),
        preferred_element_type=jnp.float32,
    )


def first_kernel(rows_ref, weight_ref, sum_ref):
    sum_ref[...] = rows_times_weight(rows_ref, weight_ref)


def middle_kernel(held_ref, rows_ref, weight_ref, sum_ref):
    sum_ref[...] = held_ref[...] + rows_times_weight(rows_ref, weight_ref)


def grad_hidden_step(held, rows, weight, start):
    row_count, width = rows.shape
    hidden_width = weight.shape[0]
    step = 2 * LANES
    block = pl.BlockSpec((row_count, step), lambda i: (0, i))
    specs = [
        pl.BlockSpec((row_count, width), lambda i: (0, 0)),
        pl.BlockSpec((step, width), lambda i: (i, start // width)),
    ]
    return pl.pallas_call(
        first_kernel if held is None else middle_kernel,
        grid=(hidden_width // step,),
        in_specs=specs if held is None else [block] + specs,
        out_specs=block,
        out_shape=jax.ShapeDtypeStruct((row_count, hidden_width), jnp.float32),
        compiler_params=params(),
        cost_estimate=cost(2 * row_count * hidden_width * width, 8 * row_count * hidden_width),
    )(*([rows, weight] if held is None else [held, rows, weight]))


def last_kernel(
    capacity,
    place_ref,
    held_ref,
    rows_ref,
    weight_ref,
    gate_ref,
    up_ref,
    grad_gate_ref,
    grad_up_ref,
    *refs,
):
    slot_refs, sum_ref = refs[:-1], refs[-1]
    grid_place = pl.program_id(0)
    grad_hidden = held_ref[...] + rows_times_weight(rows_ref, weight_ref)
    activation, gate_slope = silu_parts(gate_ref[...].astype(jnp.float32))
    up_value = up_ref[...].astype(jnp.float32)
    grad_up_ref[...] = (grad_hidden * activation).astype(jnp.bfloat16)
    grad_gate_ref[...] = (grad_hidden * up_value * gate_slope).astype(jnp.bfloat16)
    hidden = (activation * up_value).astype(jnp.bfloat16).astype(jnp.float32)
    product = hidden * grad_hidden
    folded = product[:, :LANES]
    for start in range(LANES, product.shape[1], LANES):
        folded = folded + product[:, start : start + LANES]

    @pl.when(grid_place == 0)
    def _():
        sum_ref[...] = folded

    @pl.when(grid_place > 0)
    def _():
        sum_ref[...] = sum_ref[...] + folded

    @pl.when(grid_place == pl.num_programs(0) - 1)
    def _():
        line = jnp.sum(sum_ref[...].T, axis=0, keepdims=True)
        for slot_ref in slot_refs:
            slot_ref[...] = jnp.zeros_like(slot_ref)
        for source in range(2 * len(slot_refs)):
            name = lax.bitwise_xor(place_ref[0], source)
            piece = line[:, source * capacity : (source + 1) * capacity]
            for step, slot_ref in enumerate(slot_refs):
                for half in range(2):

                    @pl.when(name == 2 * step + half)
                    def _(slot_ref=slot_ref, half=half, piece=piece):
                        slot_ref[half, 0:1, 0:capacity] = piece


def grad_hidden_last(place, held, rows, weight, start, gate, up, line_count, capacity):
    row_count, width = rows.shape
    hidden_width = weight.shape[0]
    step = 2 * LANES
    block = pl.BlockSpec((row_count, step), lambda i: (0, i))
    return pl.pallas_call(
        functools.partial(last_kernel, capacity),
        grid=(hidden_width // step,),
        in_specs=[
            SMEM,
            block,
            pl.BlockSpec((row_count, width), lambda i: (0, 0)),
            pl.BlockSpec((step, width), lambda i: (i, start // width)),
            block,
            block,
        ],
        out_specs=[block, block]
        + [pl.BlockSpec((2, 8, LANES), lambda i: (0, 0, 0))] * line_count,
        out_shape=[jax.ShapeDtypeStruct((row_count, hidden_width), jnp.bfloat16)] * 2
        + [jax.ShapeDtypeStruct((2, 8, LANES), jnp.float32)] * line_count,
        scratch_shapes=[pltpu.VMEM((row_count, LANES), jnp.float32)],
        compiler_params=params(),
        cost_estimate=cost(2 * row_count * hidden_width * width, 12 * row_count * hidden_width),
    )(place, held, rows, weight, gate, up)


def forward_kernel(*refs):
    for step, slot_ref in enumerate(refs[:-1]):
        refs[-1][step] = slot_ref[1]


def forward(slot_lines):
    return pl.pallas_call(
        forward_kernel,
        in_specs=[VMEM] * len(slot_lines),
        out_shape=jax.ShapeDtypeStruct((len(slot_lines), 8, LANES), jnp.float32),
        compiler_params=params(),
        cost_estimate=cost(1000, 40000),
    )(*slot_lines)


def route_kernel(line_count, place_ref, routes_ref, probs_ref, slot_ref, other_ref, *refs):
    line_refs, (out_ref, table_ref) = refs[:line_count], refs[line_count:]
    top_count, token_count = routes_ref.shape
    expert_count = 2 * line_count
    for step, line_ref in enumerate(line_refs):
        table_ref[2 * step : 2 * step + 1, :] = line_ref[0, 0:1, :]
        table_ref[2 * step + 1 : 2 * step + 2, :] = other_ref[step, 0:1, :]
    table = table_ref[...]
    slots = lax.broadcasted_iota(jnp.int32, (LANES, token_count), 0)
    experts = lax.broadcasted_iota(jnp.int32, (expert_count, token_count), 0)
    for k in range(top_count):
        chosen = (slots == slot_ref[k : k + 1, :]).astype(jnp.float32)
        spread = jnp.dot(
            table,
            chosen,
            preferred_element_type=jnp.float32,
            precision=lax.Precision.HIGHEST,
        )
        name = lax.bitwise_xor(routes_ref[k : k + 1, :], place_ref[0])
        picked = jnp.sum(jnp.where(experts == name, spread, 0.0), axis=0, keepdims=True)
        out_ref[k : k + 1, :] = picked / probs_ref[k : k + 1, :].astype(jnp.float32)


def route_back(place, routes, probs, slot, other, slot_lines):
    return pl.pallas_call(
        functools.partial(route_kernel, len(slot_lines)),
        in_specs=[SMEM] + [VMEM] * (4 + len(slot_lines)),
        out_shape=jax.ShapeDtypeStruct(routes.shape, jnp.float32),
        scratch_shapes=[pltpu.VMEM((2 * len(slot_lines), LANES), jnp.float32)],
        compiler_params=params(),
        cost_estimate=cost(1000000, 100000),
    )(place, routes, probs, slot, other, *slot_lines)


def swap(value, axis, offset):
    size = lax.axis_size(axis)
    return lax.ppermute(value, axis, [(place, place ^ offset) for place in range(size)])


def line_shards(grad_out, probs, routes, saved_gate, saved_up, w_down):
    expert_count = lax.axis_size("expert")
    group_count = lax.axis_size("dp")
    line_count = expert_count // 2
    capacity = saved_gate.shape[3]
    hidden_width = saved_gate.shape[4]
    model_width = grad_out.shape[1]
    row_count = expert_count * capacity
    width = model_width // CHUNKS
    starts = [chunk * width for chunk in range(CHUNKS)]

    place = jnp.stack([lax.axis_index("expert"), lax.axis_index("dp")]).astype(jnp.int32)
    other_tokens = swap(grad_out, "expert", 1)
    routes, probs = routes.T, probs.T
    slot, keep, give = select(place, routes, probs, expert_count, capacity)
    given = swap(give, "expert", 1)
    gate = saved_gate.reshape(row_count, hidden_width)
    up = saved_up.reshape(row_count, hidden_width)
    weight = w_down[0]
    hidden = hidden_transposed(gate, up)
    held = None
    panel = None
    all_rows, all_arrived = [], []
    for chunk, start in enumerate(starts):
        earlier = all_rows[chunk - 2 : chunk - 1] if chunk > 1 else []
        earlier = earlier + (all_arrived[chunk - 3] if chunk > 2 else [])
        blocks = list(
            dispatch(keep, grad_out, given, other_tokens, capacity, start, width, earlier)
        )
        for step in range(line_count - 1, 0, -1):
            blocks[step] = swap(blocks[step], "expert", 2 * step)
        earlier = all_arrived[chunk - 2] if chunk > 1 else []
        rows, own, *parts = panel_parts(place, hidden, blocks, group_count, earlier)
        arrived = [swap(part, "dp", step + 1) for step, part in enumerate(parts)]
        all_rows.append(rows)
        all_arrived.append(arrived)
        panel = total_chunk(panel, own, arrived, start, model_width)
        if chunk + 1 < CHUNKS:
            held = grad_hidden_step(held, rows, weight, start)
        else:
            grad_gate, grad_up, *slot_lines = grad_hidden_last(
                place, held, rows, weight, start, gate, up, line_count, capacity
            )
    for step in range(line_count - 1, 0, -1):
        slot_lines[step] = swap(slot_lines[step], "expert", 2 * step)
    other = swap(forward(slot_lines), "expert", 1)
    route_grad = route_back(place, routes, probs, slot, other, slot_lines)
    return (
        grad_gate.reshape(saved_gate.shape),
        grad_up.reshape(saved_up.shape),
        panel[None],
        route_grad.T,
    )


def plain_shards(grad_out, probs, routes, saved_gate, saved_up, w_down):
    expert_count = lax.axis_size("expert")
    capacity = saved_gate.shape[3]
    hidden_width = saved_gate.shape[4]
    token_count, top_count = routes.shape
    model_width = grad_out.shape[1]
    row_count = expert_count * capacity
    flat_routes = routes.reshape(-1)
    onehot = (flat_routes[:, None] == jnp.arange(expert_count)[None, :]).astype(jnp.int32)
    before = jnp.cumsum(onehot, axis=0) - onehot
    position = flat_routes * capacity + jnp.sum(before * onehot, axis=1)
    selector = jnp.arange(row_count)[:, None] == position[None, :]
    selector = jnp.where(selector, probs.reshape(-1)[None], 0).reshape(
        row_count, token_count, top_count
    )
    sent = jnp.dot(jnp.sum(selector, axis=2), grad_out, preferred_element_type=jnp.float32)
    rows = lax.all_to_all(
        sent.astype(jnp.bfloat16).reshape(expert_count, capacity, model_width),
        "expert",
        split_axis=0,
        concat_axis=0,
        tiled=True,
    ).reshape(row_count, model_width)
    up_value = saved_up.reshape(row_count, hidden_width).astype(jnp.float32)
    activation, gate_slope = silu_parts(
        saved_gate.reshape(row_count, hidden_width).astype(jnp.float32)
    )
    hidden = (activation * up_value).astype(jnp.bfloat16)
    grad_hidden = lax.dot_general(
        rows, w_down[0], (((1,), (1,)), ((), ())), preferred_element_type=jnp.float32
    )
    slot_grad = jnp.sum(hidden.astype(jnp.float32) * grad_hidden, axis=1)
    grad_up = (grad_hidden * activation).astype(jnp.bfloat16)
    grad_gate = (grad_hidden * up_value * gate_slope).astype(jnp.bfloat16)
    whole_panel = lax.dot_general(
        hidden, rows, (((0,), (0,)), ((), ())), preferred_element_type=jnp.float32
    )
    panel = lax.psum_scatter(whole_panel, "dp", scatter_dimension=0, tiled=True)
    returned = lax.all_to_all(
        slot_grad.reshape(expert_count, capacity), "expert", split_axis=0, concat_axis=0, tiled=True
    )
    route_grad = jnp.take(returned.reshape(-1), position, axis=0).reshape(token_count, top_count)
    return (
        grad_gate.reshape(saved_gate.shape),
        grad_up.reshape(saved_up.shape),
        panel[None],
        route_grad / probs.astype(jnp.float32),
    )


def shards(grad_out, probs, routes, saved_gate, saved_up, w_down):
    expert_count = lax.axis_size("expert")
    group_count = lax.axis_size("dp")
    capacity, hidden_width = saved_gate.shape[3:]
    aligned = (
        expert_count & (expert_count - 1) == 0
        and group_count & (group_count - 1) == 0
        and capacity % 16 == 0
        and capacity <= LANES
        and hidden_width % (16 * group_count) == 0
        and routes.shape[0] % LANES == 0
    )
    run = line_shards if aligned else plain_shards
    return run(grad_out, probs, routes, saved_gate, saved_up, w_down)


def solution(mesh):
    return jax.shard_map(
        shards,
        mesh=mesh,
        in_specs=(
            P(("dp", "expert"), None),
            P(("dp", "expert"), None),
            P(("dp", "expert"), None),
            P("dp", "expert", None, None, None),
            P("dp", "expert", None, None, None),
            P("expert", None, None),
        ),
        out_specs=(
            P("dp", "expert", None, None, None),
            P("dp", "expert", None, None, None),
            P("expert", "dp", None),
            P(("dp", "expert"), None),
        ),
        check_vma=False,
    )
```

```python
import functools

import jax
import jax.numpy as jnp
from jax import lax
from jax.experimental import pallas as pl
from jax.experimental.pallas import tpu as pltpu
from jax.sharding import PartitionSpec as P

LANES = 128
META = 16
OFFSETS = (0, 1, 4, 5)
WIDTHS = (640, 768, 640)
FIRST_PART = WIDTHS[0]
VMEM_LIMIT = 10 * 1024 * 1024
VMEM = pl.BlockSpec(memory_space=pltpu.VMEM)
ANY = pl.BlockSpec(memory_space=pl.ANY)
SMEM = pl.BlockSpec(memory_space=pltpu.SMEM)


def params():
    return pltpu.CompilerParams(vmem_limit_bytes=VMEM_LIMIT)


def cost(flops, moved):
    return pl.CostEstimate(flops=flops // 64, bytes_accessed=moved // 64, transcendentals=0)


def silu_parts(gate_value):
    sigmoid = jax.nn.sigmoid(gate_value)
    return (gate_value * sigmoid, sigmoid * (1.0 + gate_value * (1.0 - sigmoid)))


def tokens_kernel(expert_count, routes_ref, probs_ref, rows_ref, meta_ref, *part_refs):
    top_count, token_count = routes_ref.shape
    names = [routes_ref[k : k + 1, :] for k in range(top_count)]
    experts = lax.broadcasted_iota(jnp.int32, (expert_count, token_count), 0)
    onehots = [(experts == name).astype(jnp.float32) for name in names]
    earlier = (
        lax.broadcasted_iota(jnp.int32, (token_count, token_count), 0)
        < lax.broadcasted_iota(jnp.int32, (token_count, token_count), 1)
    ).astype(jnp.bfloat16)
    before = jnp.dot(
        sum(onehots).astype(jnp.bfloat16), earlier, preferred_element_type=jnp.float32
    )
    lines = [name.astype(jnp.float32) for name in names]
    for onehot in onehots:
        lines.append(jnp.sum(before * onehot, axis=0, keepdims=True))
        before = before + onehot
    for k in range(top_count):
        lines.append(probs_ref[k : k + 1, :].astype(jnp.float32))
    lines.append(jnp.zeros((META - len(lines), token_count), jnp.float32))
    meta = jnp.concatenate(lines, axis=0).astype(jnp.bfloat16)
    meta_ref[...] = meta
    start = 0
    for part, part_ref in enumerate(part_refs):
        width = part_ref.shape[1]
        part_ref[:token_count, :] = rows_ref[:, start : start + width]
        if part == 0:
            part_ref[token_count:, :] = jnp.zeros((META, width), jnp.bfloat16)
            part_ref[token_count:, :token_count] = meta
        start += width


def token_parts(routes, probs, grad_out, expert_count, widths):
    token_count = routes.shape[1]
    return pl.pallas_call(
        functools.partial(tokens_kernel, expert_count),
        in_specs=[VMEM] * 3,
        out_shape=[jax.ShapeDtypeStruct((META, token_count), jnp.bfloat16)]
        + [
            jax.ShapeDtypeStruct((token_count + (0 if part else META), width), jnp.bfloat16)
            for part, width in enumerate(widths)
        ],
        compiler_params=params(),
        cost_estimate=cost(100 * token_count * token_count, 4 * grad_out.size),
    )(routes, probs, grad_out)


def chosen_rows(meta, top_count, capacity, targets):
    token_count = meta.shape[1]
    slots = lax.broadcasted_iota(jnp.int32, (capacity, token_count), 0).astype(jnp.float32)
    parts = []
    for target in targets:
        part = jnp.zeros((capacity, token_count), jnp.float32)
        for k in range(top_count):
            name, slot, prob = (meta[k + top_count * i :][:1, :] for i in range(3))
            slot = jnp.where(name == target, slot, -1.0)
            part = part + jnp.where(slots == slot, prob, 0.0)
        parts.append(part)
    return jnp.concatenate(parts, axis=0).astype(jnp.bfloat16)


def dispatch_kernel(capacity, top_count, starts, first, *refs):
    if first:
        place_ref, own_meta_ref, other_meta_ref, *refs = refs
        row_refs, (local_ref, sent_ref, select_ref) = refs[:4], refs[4:]
        token_count = own_meta_ref.shape[1]
        targets = [
            lax.bitwise_xor(place_ref[0], offset).astype(jnp.float32) for offset in (0, 2)
        ]
        for source in range(4):
            if source < 2:
                meta = (own_meta_ref, other_meta_ref)[source][...]
            else:
                meta = row_refs[source][token_count:, :token_count]
            select_ref[2 * capacity * source : 2 * capacity * (source + 1), :] = chosen_rows(
                meta.astype(jnp.float32), top_count, capacity, targets
            )
    else:
        select_ref, *refs = refs
        row_refs, (local_ref, sent_ref) = refs[:4], refs[4:]
    token_count = select_ref.shape[1]
    width = local_ref.shape[1]
    for source, row_ref in enumerate(row_refs):
        columns = slice(starts[source // 2], starts[source // 2] + width)
        rows = jnp.dot(
            select_ref[2 * capacity * source : 2 * capacity * (source + 1), :],
            row_ref[:token_count, columns],
            preferred_element_type=jnp.float32,
        ).astype(jnp.bfloat16)
        local_ref[source * capacity : (source + 1) * capacity, :] = rows[:capacity, :]
        sent_ref[source * capacity : (source + 1) * capacity, :] = rows[capacity:, :]


def dispatch(lead, rows, capacity, top_count, token_count, starts, width):
    first = len(lead) > 1
    block = jax.ShapeDtypeStruct((4 * capacity, width), jnp.bfloat16)
    chosen = jax.ShapeDtypeStruct((8 * capacity, token_count), jnp.bfloat16)
    return pl.pallas_call(
        functools.partial(dispatch_kernel, capacity, top_count, starts, first),
        in_specs=([SMEM, VMEM, VMEM] if first else [VMEM]) + [VMEM] * 4,
        out_shape=[block, block] + ([chosen] if first else []),
        compiler_params=params(),
        cost_estimate=cost(
            16 * capacity * token_count * width, 4 * (8 * capacity + token_count) * width
        ),
    )(*lead, *rows)


def hidden_kernel(gate_ref, up_ref, turned_ref, hidden_ref, up_scale_ref, gate_scale_ref):
    activation, gate_slope = silu_parts(gate_ref[...].astype(jnp.float32))
    up_value = up_ref[...].astype(jnp.float32)
    hidden = activation * up_value
    turned_ref[...] = hidden.T.astype(jnp.bfloat16)
    hidden_ref[...] = hidden.astype(jnp.bfloat16)
    up_scale_ref[...] = activation
    gate_scale_ref[...] = up_value * gate_slope


def hidden_parts(gate, up):
    row_count, hidden_width = gate.shape
    step = 2 * LANES
    block = pl.BlockSpec((row_count, step), lambda i: (0, i))
    return pl.pallas_call(
        hidden_kernel,
        grid=(hidden_width // step,),
        in_specs=[block] * 2,
        out_specs=[pl.BlockSpec((step, row_count), lambda i: (i, 0))] + [block] * 3,
        out_shape=[
            jax.ShapeDtypeStruct((hidden_width, row_count), jnp.bfloat16),
            jax.ShapeDtypeStruct((row_count, hidden_width), jnp.bfloat16),
            jax.ShapeDtypeStruct((row_count, hidden_width), jnp.float32),
            jax.ShapeDtypeStruct((row_count, hidden_width), jnp.float32),
        ],
        compiler_params=params(),
        cost_estimate=cost(20 * row_count * hidden_width, 16 * row_count * hidden_width),
    )(gate, up)


def panel_kernel(capacity, place_ref, turned_ref, local_ref, near_ref, *refs):
    rows_ref, own_ref, later_ref, sent_ref = refs[-4:]
    share = own_ref.shape[0]
    for source in range(4):
        for offset, block_ref in ((0, local_ref), (2, near_ref)):
            place = lax.bitwise_xor(place_ref[0], OFFSETS[source] + offset)
            start = pl.multiple_of(place * capacity, capacity)
            rows_ref[pl.ds(start, capacity), :] = block_ref[
                source * capacity : (source + 1) * capacity, :
            ]
    rows = rows_ref[...]

    def part(offset):
        owner = lax.bitwise_xor(place_ref[1], offset)
        start = pl.multiple_of(owner * share, share)
        return jnp.dot(turned_ref[pl.ds(start, share), :], rows, preferred_element_type=jnp.float32)

    step = 1 + lax.bitwise_and(place_ref[0], 1)
    sent_ref[:share, :] = part(step).astype(jnp.bfloat16)
    sent_ref[share:, :] = part(3).astype(jnp.bfloat16)
    later_ref[...] = part(3 - step)
    own_ref[...] = part(0)


def panel_parts(place, turned, local, near, capacity, earlier):
    hidden_width, row_count = turned.shape
    width = local.shape[1]
    share = hidden_width // 4
    return pl.pallas_call(
        functools.partial(panel_kernel, capacity),
        in_specs=[SMEM] + [VMEM] * 3 + [ANY] * len(earlier),
        out_shape=[
            jax.ShapeDtypeStruct((row_count, width), jnp.bfloat16),
            jax.ShapeDtypeStruct((share, width), jnp.float32),
            jax.ShapeDtypeStruct((share, width), jnp.float32),
            jax.ShapeDtypeStruct((2 * share, width), jnp.bfloat16),
        ],
        compiler_params=params(),
        cost_estimate=cost(
            2 * hidden_width * row_count * width, 2 * hidden_width * (row_count + width)
        ),
    )(place, turned, local, near, *earlier)


def halve_kernel(own_ref, later_ref, arrived_ref, sum_ref, sent_ref):
    share = own_ref.shape[0]
    sent_ref[...] = (later_ref[...] + arrived_ref[share:, :].astype(jnp.float32)).astype(
        jnp.bfloat16
    )
    sum_ref[...] = own_ref[...] + arrived_ref[:share, :].astype(jnp.float32)


def halve(own, later, arrived):
    return pl.pallas_call(
        halve_kernel,
        in_specs=[VMEM] * 3,
        out_shape=[
            jax.ShapeDtypeStruct(own.shape, jnp.float32),
            jax.ShapeDtypeStruct(own.shape, jnp.bfloat16),
        ],
        compiler_params=params(),
        cost_estimate=cost(4 * own.size, 18 * own.size),
    )(own, later, arrived)


def total_kernel(start, *refs):
    own_ref, arrived_ref, total_ref, sum_ref, semaphore = refs[-5:]
    sum_ref[...] = own_ref[...] + arrived_ref[...].astype(jnp.float32)
    copy = pltpu.make_async_copy(
        sum_ref, total_ref.at[:, start : start + sum_ref.shape[1]], semaphore
    )
    copy.start()
    copy.wait()


def total_chunk(held, own, arrived, start, model_width):
    share, width = own.shape
    first = held is None
    return pl.pallas_call(
        functools.partial(total_kernel, start),
        in_specs=([] if first else [ANY]) + [VMEM] * 2,
        out_specs=ANY,
        out_shape=jax.ShapeDtypeStruct((share, model_width), jnp.float32),
        scratch_shapes=[pltpu.VMEM((share, width), jnp.float32), pltpu.SemaphoreType.DMA],
        input_output_aliases={} if first else {0: 0},
        compiler_params=params(),
        cost_estimate=cost(2 * share * width, 10 * share * width),
    )(*([] if first else [held]), own, arrived)


def rows_times_weight(start, rows_ref, weight_ref):
    return lax.dot_general(
        rows_ref[...],
        weight_ref[:, start : start + rows_ref.shape[1]],
        (((1,), (1,)), ((), ())),
        preferred_element_type=jnp.float32,
    )


def first_kernel(start, rows_ref, weight_ref, sum_ref):
    sum_ref[...] = rows_times_weight(start, rows_ref, weight_ref)


def middle_kernel(start, held_ref, rows_ref, weight_ref, sum_ref):
    sum_ref[...] = held_ref[...] + rows_times_weight(start, rows_ref, weight_ref)


def grad_hidden_step(held, rows, weight, start):
    row_count, width = rows.shape
    hidden_width = weight.shape[0]
    step = 2 * LANES
    block = pl.BlockSpec((row_count, step), lambda i: (0, i))
    specs = [
        pl.BlockSpec((row_count, width), lambda i: (0, 0)),
        pl.BlockSpec((step, weight.shape[1]), lambda i: (i, 0)),
    ]
    return pl.pallas_call(
        functools.partial(first_kernel if held is None else middle_kernel, start),
        grid=(hidden_width // step,),
        in_specs=specs if held is None else [block] + specs,
        out_specs=block,
        out_shape=jax.ShapeDtypeStruct((row_count, hidden_width), jnp.float32),
        compiler_params=params(),
        cost_estimate=cost(2 * row_count * hidden_width * width, 8 * row_count * hidden_width),
    )(*([rows, weight] if held is None else [held, rows, weight]))


def last_kernel(
    capacity,
    start,
    held_ref,
    rows_ref,
    weight_ref,
    hidden_ref,
    up_scale_ref,
    gate_scale_ref,
    grad_gate_ref,
    grad_up_ref,
    slot_ref,
    sum_ref,
):
    grid_place = pl.program_id(0)
    grad_hidden = held_ref[...] + rows_times_weight(start, rows_ref, weight_ref)
    grad_up_ref[...] = (grad_hidden * up_scale_ref[...]).astype(jnp.bfloat16)
    grad_gate_ref[...] = (grad_hidden * gate_scale_ref[...]).astype(jnp.bfloat16)
    product = hidden_ref[...].astype(jnp.float32) * grad_hidden
    folded = product[:, :LANES]
    for column in range(LANES, product.shape[1], LANES):
        folded = folded + product[:, column : column + LANES]

    @pl.when(grid_place == 0)
    def _():
        sum_ref[...] = folded

    @pl.when(grid_place > 0)
    def _():
        sum_ref[...] = sum_ref[...] + folded

    @pl.when(grid_place == pl.num_programs(0) - 1)
    def _():
        line = jnp.sum(sum_ref[...].T, axis=0, keepdims=True)
        slot_ref[...] = jnp.zeros_like(slot_ref)
        for source in range(slot_ref.shape[0]):
            slot_ref[source : source + 1, 0:capacity] = line[
                :, source * capacity : (source + 1) * capacity
            ]


def grad_hidden_last(held, rows, weight, start, hidden, up_scale, gate_scale, capacity):
    row_count, width = rows.shape
    hidden_width = weight.shape[0]
    step = 2 * LANES
    block = pl.BlockSpec((row_count, step), lambda i: (0, i))
    expert_count = row_count // capacity
    return pl.pallas_call(
        functools.partial(last_kernel, capacity, start),
        grid=(hidden_width // step,),
        in_specs=[
            block,
            pl.BlockSpec((row_count, width), lambda i: (0, 0)),
            pl.BlockSpec((step, weight.shape[1]), lambda i: (i, 0)),
            block,
            block,
            block,
        ],
        out_specs=[block, block, pl.BlockSpec((expert_count, LANES), lambda i: (0, 0))],
        out_shape=[jax.ShapeDtypeStruct((row_count, hidden_width), jnp.bfloat16)] * 2
        + [jax.ShapeDtypeStruct((expert_count, LANES), jnp.float32)],
        scratch_shapes=[pltpu.VMEM((row_count, LANES), jnp.float32)],
        compiler_params=params(),
        cost_estimate=cost(2 * row_count * hidden_width * width, 12 * row_count * hidden_width),
    )(held, rows, weight, hidden, up_scale, gate_scale)


def route_kernel(capacity, place_ref, meta_ref, near_ref, far_ref, out_ref, table_ref):
    top_count, token_count = out_ref.shape
    expert_count = table_ref.shape[0]
    half = expert_count // 2
    for offset in range(expert_count):
        block_ref = near_ref if offset < half else far_ref
        row = offset % half * expert_count + place_ref[0]
        table_ref[offset : offset + 1, :] = block_ref[pl.ds(row, 1), :]
    table = table_ref[...].T
    meta = meta_ref[...].astype(jnp.float32)
    slots = lax.broadcasted_iota(jnp.int32, (capacity, token_count), 0).astype(jnp.float32)
    for k in range(top_count):
        name, slot, prob = (meta[k + top_count * i :][:1, :] for i in range(3))
        picked = jnp.zeros((capacity, token_count), jnp.float32)
        for offset in range(expert_count):
            expert = lax.bitwise_xor(place_ref[0], offset).astype(jnp.float32)
            wanted = jnp.where(name == expert, slot, -1.0)
            picked = picked + jnp.where(
                slots == wanted, table[:capacity, offset : offset + 1], 0.0
            )
        out_ref[k : k + 1, :] = jnp.sum(picked, axis=0, keepdims=True) / prob


def route_back(place, meta, near, far, expert_count, top_count, capacity):
    token_count = meta.shape[1]
    return pl.pallas_call(
        functools.partial(route_kernel, capacity),
        in_specs=[SMEM] + [VMEM] * 3,
        out_shape=jax.ShapeDtypeStruct((top_count, token_count), jnp.float32),
        scratch_shapes=[pltpu.VMEM((expert_count, LANES), jnp.float32)],
        compiler_params=params(),
        cost_estimate=cost(1000000, 100000),
    )(place, meta, near, far)


def after_kernel(*refs):
    pass


def after(value, *earlier):
    return pl.pallas_call(
        after_kernel,
        in_specs=[ANY] * (1 + len(earlier)),
        out_specs=ANY,
        out_shape=jax.ShapeDtypeStruct(value.shape, value.dtype),
        input_output_aliases={0: 0},
        compiler_params=params(),
        cost_estimate=cost(64, 64),
    )(value, *earlier)


def swap(value, offset):
    size = lax.axis_size("expert")
    return lax.ppermute(value, "expert", [(place, place ^ offset) for place in range(size)])


def swap_groups(value, later):
    groups, places = lax.axis_size("dp"), lax.axis_size("expert")
    pairs = []
    for group in range(groups):
        for place in range(places):
            other = group ^ (1 + (place & 1) ^ (3 if later else 0))
            pairs.append((group * places + place, other * places + place))
    return lax.ppermute(value, ("dp", "expert"), pairs)


def line_shards(grad_out, probs, routes, saved_gate, saved_up, w_down):
    expert_count = lax.axis_size("expert")
    capacity = saved_gate.shape[3]
    hidden_width = saved_gate.shape[4]
    token_count, model_width = grad_out.shape
    top_count = routes.shape[1]
    row_count = expert_count * capacity

    place = jnp.stack([lax.axis_index("expert"), lax.axis_index("dp")]).astype(jnp.int32)
    part_widths = (FIRST_PART, model_width - FIRST_PART)
    meta, *parts = token_parts(routes.T, probs.T, grad_out, expert_count, part_widths)
    parts = [swap(part, 4) for part in parts]
    other_rows, other_meta = swap(grad_out, 1), swap(meta, 1)
    gate = saved_gate.reshape(row_count, hidden_width)
    up = saved_up.reshape(row_count, hidden_width)
    weight = w_down[0]
    turned, hidden, up_scale, gate_scale = hidden_parts(gate, up)
    lead = [place, meta, other_meta]
    held, panel, start, halves = None, None, 0, []
    for chunk, width in enumerate(WIDTHS):
        part = int(start >= FIRST_PART)
        starts = (start, start - part * FIRST_PART)
        if start == FIRST_PART:
            parts[part] = after(parts[part], sent)
        if start in (0, FIRST_PART):
            other_part = swap(parts[part], 1)
        sources = [grad_out, other_rows, parts[part], other_part]
        local, sent, *select = dispatch(
            lead, sources, capacity, top_count, token_count, starts, width
        )
        lead = select or lead
        earlier = ([held] if chunk > 0 else []) + (halves[chunk - 2 : chunk - 1] if chunk > 1 else [])
        rows, own, later, half = panel_parts(
            place, turned, local, swap(sent, 2), capacity, earlier
        )
        own, half = halve(own, later, swap_groups(half, False))
        half = swap_groups(half, True)
        halves.append(half)
        panel = total_chunk(panel, own, half, start, model_width)
        if chunk + 1 < len(WIDTHS):
            held = grad_hidden_step(held, rows, weight, start)
        else:
            grad_gate, grad_up, lines = grad_hidden_last(
                held, rows, weight, start, hidden, up_scale, gate_scale, capacity
            )
        start += width
    for offset in (1, 2):
        lines = jnp.concatenate([lines, swap(lines, offset)], axis=0)
    route_grad = route_back(
        place, meta, lines, swap(lines, 4), expert_count, top_count, capacity
    )
    return (
        grad_gate.reshape(saved_gate.shape),
        grad_up.reshape(saved_up.shape),
        panel[None],
        route_grad.T,
    )


def plain_shards(grad_out, probs, routes, saved_gate, saved_up, w_down):
    expert_count = lax.axis_size("expert")
    capacity = saved_gate.shape[3]
    hidden_width = saved_gate.shape[4]
    token_count, top_count = routes.shape
    model_width = grad_out.shape[1]
    row_count = expert_count * capacity
    flat_routes = routes.reshape(-1)
    onehot = (flat_routes[:, None] == jnp.arange(expert_count)[None, :]).astype(jnp.int32)
    before = jnp.cumsum(onehot, axis=0) - onehot
    position = flat_routes * capacity + jnp.sum(before * onehot, axis=1)
    selector = jnp.arange(row_count)[:, None] == position[None, :]
    selector = jnp.where(selector, probs.reshape(-1)[None], 0).reshape(
        row_count, token_count, top_count
    )
    sent = jnp.dot(jnp.sum(selector, axis=2), grad_out, preferred_element_type=jnp.float32)
    rows = lax.all_to_all(
        sent.astype(jnp.bfloat16).reshape(expert_count, capacity, model_width),
        "expert",
        split_axis=0,
        concat_axis=0,
        tiled=True,
    ).reshape(row_count, model_width)
    up_value = saved_up.reshape(row_count, hidden_width).astype(jnp.float32)
    activation, gate_slope = silu_parts(
        saved_gate.reshape(row_count, hidden_width).astype(jnp.float32)
    )
    hidden = (activation * up_value).astype(jnp.bfloat16)
    grad_hidden = lax.dot_general(
        rows, w_down[0], (((1,), (1,)), ((), ())), preferred_element_type=jnp.float32
    )
    slot_grad = jnp.sum(hidden.astype(jnp.float32) * grad_hidden, axis=1)
    grad_up = (grad_hidden * activation).astype(jnp.bfloat16)
    grad_gate = (grad_hidden * up_value * gate_slope).astype(jnp.bfloat16)
    whole_panel = lax.dot_general(
        hidden, rows, (((0,), (0,)), ((), ())), preferred_element_type=jnp.float32
    )
    panel = lax.psum_scatter(whole_panel, "dp", scatter_dimension=0, tiled=True)
    returned = lax.all_to_all(
        slot_grad.reshape(expert_count, capacity), "expert", split_axis=0, concat_axis=0, tiled=True
    )
    route_grad = jnp.take(returned.reshape(-1), position, axis=0).reshape(token_count, top_count)
    return (
        grad_gate.reshape(saved_gate.shape),
        grad_up.reshape(saved_up.shape),
        panel[None],
        route_grad / probs.astype(jnp.float32),
    )


def shards(grad_out, probs, routes, saved_gate, saved_up, w_down):
    expert_count = lax.axis_size("expert")
    group_count = lax.axis_size("dp")
    capacity, hidden_width = saved_gate.shape[3:]
    aligned = (
        expert_count == 8
        and group_count == 4
        and capacity % 16 == 0
        and capacity <= LANES
        and hidden_width % (16 * group_count) == 0
        and routes.shape[0] == LANES
        and grad_out.shape[1] == sum(WIDTHS)
    )
    run = line_shards if aligned else plain_shards
    return run(grad_out, probs, routes, saved_gate, saved_up, w_down)


def solution(mesh):
    return jax.shard_map(
        shards,
        mesh=mesh,
        in_specs=(
            P(("dp", "expert"), None),
            P(("dp", "expert"), None),
            P(("dp", "expert"), None),
            P("dp", "expert", None, None, None),
            P("dp", "expert", None, None, None),
            P("expert", None, None),
        ),
        out_specs=(
            P("dp", "expert", None, None, None),
            P("dp", "expert", None, None, None),
            P("expert", "dp", None),
            P(("dp", "expert"), None),
        ),
        check_vma=False,
    )
```

```python
import functools

import jax
import jax.numpy as jnp
from jax import lax
from jax.experimental import pallas as pl
from jax.experimental.pallas import tpu as pltpu
from jax.sharding import PartitionSpec as P

LANES = 128
META = 16
PARTS = ((768,), (640, 640))
VMEM_LIMIT = 10 * 1024 * 1024
VMEM = pl.BlockSpec(memory_space=pltpu.VMEM)
ANY = pl.BlockSpec(memory_space=pl.ANY)
HBM = pl.BlockSpec(memory_space=pltpu.HBM)


def params():
    return pltpu.CompilerParams(vmem_limit_bytes=VMEM_LIMIT)


def cost(flops, moved):
    return pl.CostEstimate(flops=flops // 64, bytes_accessed=moved // 64, transcendentals=0)


def silu_parts(gate_value):
    sigmoid = jax.nn.sigmoid(gate_value)
    return (gate_value * sigmoid, sigmoid * (1.0 + gate_value * (1.0 - sigmoid)))


def tokens_kernel(expert_count, routes_hbm, probs_hbm, rows_hbm, meta_ref, *refs):
    part_refs, (routes_ref, probs_ref, semaphores) = refs[:-3], refs[-3:]
    token_count = rows_hbm.shape[0]
    top_count = routes_ref.shape[0]
    copies = [
        pltpu.make_async_copy(routes_hbm, routes_ref, semaphores.at[0]),
        pltpu.make_async_copy(probs_hbm, probs_ref, semaphores.at[1]),
    ]
    start = 0
    for part, part_ref in enumerate(part_refs):
        width = part_ref.shape[1]
        copies.append(
            pltpu.make_async_copy(
                rows_hbm.at[:, start : start + width],
                part_ref.at[:token_count, :],
                semaphores.at[2 + part],
            )
        )
        start += width
    for copy in copies:
        copy.start()
    for copy in copies[:2]:
        copy.wait()
    names = [routes_ref[k : k + 1, :] for k in range(top_count)]
    experts = lax.broadcasted_iota(jnp.int32, (expert_count, token_count), 0)
    onehots = [(experts == name).astype(jnp.float32) for name in names]
    earlier = (
        lax.broadcasted_iota(jnp.int32, (token_count, token_count), 0)
        < lax.broadcasted_iota(jnp.int32, (token_count, token_count), 1)
    ).astype(jnp.bfloat16)
    before = jnp.dot(
        sum(onehots).astype(jnp.bfloat16), earlier, preferred_element_type=jnp.float32
    )
    lines = [name.astype(jnp.float32) for name in names]
    for onehot in onehots:
        lines.append(jnp.sum(before * onehot, axis=0, keepdims=True))
        before = before + onehot
    for k in range(top_count):
        lines.append(probs_ref[k : k + 1, :].astype(jnp.float32))
    lines.append(jnp.zeros((META - len(lines), token_count), jnp.float32))
    meta = jnp.concatenate(lines, axis=0).astype(jnp.bfloat16)
    meta_ref[...] = meta
    lead_ref = part_refs[0]
    lead_ref[token_count:, :] = jnp.zeros((META, lead_ref.shape[1]), jnp.bfloat16)
    lead_ref[token_count:, :token_count] = meta
    for copy in copies[2:]:
        copy.wait()


def token_parts(routes, probs, grad_out, expert_count):
    token_count = routes.shape[1]
    return pl.pallas_call(
        functools.partial(tokens_kernel, expert_count),
        in_specs=[HBM] * 3,
        out_shape=[jax.ShapeDtypeStruct((META, token_count), jnp.bfloat16)]
        + [
            jax.ShapeDtypeStruct((token_count + (0 if part else META), width), jnp.bfloat16)
            for part, width in enumerate(map(sum, PARTS))
        ],
        scratch_shapes=[
            pltpu.VMEM(routes.shape, routes.dtype),
            pltpu.VMEM(probs.shape, probs.dtype),
            pltpu.SemaphoreType.DMA((2 + len(PARTS),)),
        ],
        compiler_params=params(),
        cost_estimate=cost(100 * token_count * token_count, 4 * grad_out.size),
    )(routes, probs, grad_out)


def chosen_rows(meta, top_count, capacity):
    token_count = meta.shape[1]
    slots = lax.broadcasted_iota(jnp.int32, (capacity, token_count), 0).astype(jnp.float32)
    parts = []
    for offset in (0, 2):
        target = lax.bitwise_xor(lax.axis_index("expert"), offset).astype(jnp.float32)
        part = jnp.zeros((capacity, token_count), jnp.float32)
        for k in range(top_count):
            name, slot, prob = (meta[k + top_count * i :][:1, :] for i in range(3))
            slot = jnp.where(name == target, slot, -1.0)
            part = part + jnp.where(slots == slot, prob, 0.0)
        parts.append(part)
    return jnp.concatenate(parts, axis=0).astype(jnp.bfloat16)


def dispatch_kernel(capacity, top_count, start, *refs):
    meta_refs, row_refs, (local_ref, sent_ref) = refs[:2], refs[2:4], refs[-2:]
    token_count = meta_refs[0].shape[1] if meta_refs[0].shape[0] == META else LANES
    width = local_ref.shape[1]
    for source in range(2):
        first = meta_refs[source].shape[0] - META
        meta = meta_refs[source][first:, :token_count].astype(jnp.float32)
        rows = jnp.dot(
            chosen_rows(meta, top_count, capacity),
            row_refs[source][:token_count, start : start + width],
            preferred_element_type=jnp.float32,
        ).astype(jnp.bfloat16)
        local_ref[source * capacity : (source + 1) * capacity, :] = rows[:capacity, :]
        sent_ref[source * capacity : (source + 1) * capacity, :] = rows[capacity:, :]


def dispatch(metas, rows, capacity, top_count, start, width, earlier=()):
    block = jax.ShapeDtypeStruct((2 * capacity, width), jnp.bfloat16)
    return pl.pallas_call(
        functools.partial(dispatch_kernel, capacity, top_count, start),
        in_specs=[VMEM] * 4 + [ANY] * len(earlier),
        out_shape=[block, block],
        compiler_params=params(),
        cost_estimate=cost(8 * capacity * LANES * width, 8 * capacity * width),
    )(*metas, *rows, *earlier)


def hidden_kernel(gate_ref, up_ref, turned_ref, hidden_ref, up_scale_ref, gate_scale_ref):
    activation, gate_slope = silu_parts(gate_ref[...].astype(jnp.float32))
    up_value = up_ref[...].astype(jnp.float32)
    hidden = activation * up_value
    turned_ref[...] = hidden.T.astype(jnp.bfloat16)
    hidden_ref[...] = hidden.astype(jnp.bfloat16)
    up_scale_ref[...] = activation
    gate_scale_ref[...] = up_value * gate_slope


def hidden_parts(gate, up):
    row_count, hidden_width = gate.shape
    step = 2 * LANES
    block = pl.BlockSpec((row_count, step), lambda i: (0, i))
    return pl.pallas_call(
        hidden_kernel,
        grid=(hidden_width // step,),
        in_specs=[block] * 2,
        out_specs=[pl.BlockSpec((step, row_count), lambda i: (i, 0))] + [block] * 3,
        out_shape=[
            jax.ShapeDtypeStruct((hidden_width, row_count), jnp.bfloat16),
            jax.ShapeDtypeStruct((row_count, hidden_width), jnp.bfloat16),
            jax.ShapeDtypeStruct((row_count, hidden_width), jnp.float32),
            jax.ShapeDtypeStruct((row_count, hidden_width), jnp.float32),
        ],
        compiler_params=params(),
        cost_estimate=cost(20 * row_count * hidden_width, 16 * row_count * hidden_width),
    )(gate, up)


def panel_kernel(capacity, columns, turned_ref, *refs):
    block_refs, (rows_ref, own_ref, later_ref, sent_ref) = refs[:4], refs[-4:]
    share, width = own_ref.shape
    device = lax.axis_index("expert")
    for block, (block_ref, column) in enumerate(zip(block_refs, columns)):
        for half in range(2):
            place = lax.bitwise_xor(device, 2 * block + half)
            row = pl.multiple_of(place * capacity, capacity)
            rows_ref[pl.ds(row, capacity), :] = block_ref[
                half * capacity : (half + 1) * capacity, column : column + width
            ]
    rows = rows_ref[...]

    def part(offset):
        owner = lax.bitwise_xor(lax.axis_index("dp"), offset)
        row = pl.multiple_of(owner * share, share)
        return jnp.dot(turned_ref[pl.ds(row, share), :], rows, preferred_element_type=jnp.float32)

    step = 1 + lax.bitwise_and(device, 1)
    sent_ref[:share, :] = part(step).astype(jnp.bfloat16)
    sent_ref[share:, :] = part(3).astype(jnp.bfloat16)
    later_ref[...] = part(3 - step)
    own_ref[...] = part(0)


def panel_parts(turned, blocks, capacity, width, earlier):
    hidden_width, row_count = turned.shape
    share = hidden_width // 4
    return pl.pallas_call(
        functools.partial(panel_kernel, capacity, [column for _, column in blocks]),
        in_specs=[VMEM] * 5 + [ANY] * len(earlier),
        out_shape=[
            jax.ShapeDtypeStruct((row_count, width), jnp.bfloat16),
            jax.ShapeDtypeStruct((share, width), jnp.float32),
            jax.ShapeDtypeStruct((share, width), jnp.float32),
            jax.ShapeDtypeStruct((2 * share, width), jnp.bfloat16),
        ],
        compiler_params=params(),
        cost_estimate=cost(
            2 * hidden_width * row_count * width, 2 * hidden_width * (row_count + width)
        ),
    )(turned, *[block for block, _ in blocks], *earlier)


def halve_kernel(own_ref, later_ref, arrived_ref, *refs):
    sum_ref, sent_ref = refs[-2:]
    share = own_ref.shape[0]
    sent_ref[...] = (later_ref[...] + arrived_ref[share:, :].astype(jnp.float32)).astype(
        jnp.bfloat16
    )
    sum_ref[...] = own_ref[...] + arrived_ref[:share, :].astype(jnp.float32)


def halve(own, later, arrived, earlier):
    return pl.pallas_call(
        halve_kernel,
        in_specs=[VMEM] * 3 + [ANY] * len(earlier),
        out_shape=[
            jax.ShapeDtypeStruct(own.shape, jnp.float32),
            jax.ShapeDtypeStruct(own.shape, jnp.bfloat16),
        ],
        compiler_params=params(),
        cost_estimate=cost(4 * own.size, 18 * own.size),
    )(own, later, arrived, *earlier)


def total_kernel(count, *refs):
    own_refs, arrived_refs = refs[:count], refs[count : 2 * count]
    total_ref, *sum_refs, semaphores = refs[2 * count :]
    copies = []
    start = 0
    for place, (own_ref, arrived_ref) in enumerate(zip(own_refs, arrived_refs)):
        width = own_ref.shape[1]
        sum_refs[place][...] = own_ref[...] + arrived_ref[...].astype(jnp.float32)
        copies.append(
            pltpu.make_async_copy(
                sum_refs[place], total_ref.at[:, start : start + width], semaphores.at[place]
            )
        )
        copies[-1].start()
        start += width
    for copy in copies:
        copy.wait()


def total(owns, arrived):
    share = owns[0].shape[0]
    size = share * sum(own.shape[1] for own in owns)
    return pl.pallas_call(
        functools.partial(total_kernel, len(owns)),
        in_specs=[VMEM] * (2 * len(owns)),
        out_specs=HBM,
        out_shape=jax.ShapeDtypeStruct((share, size // share), jnp.float32),
        scratch_shapes=[pltpu.VMEM(own.shape, jnp.float32) for own in owns]
        + [pltpu.SemaphoreType.DMA((len(owns),))],
        compiler_params=params(),
        cost_estimate=cost(2 * size, 10 * size),
    )(*owns, *arrived)


def rows_times_weight(start, rows_ref, weight_ref):
    return lax.dot_general(
        rows_ref[...],
        weight_ref[:, start : start + rows_ref.shape[1]],
        (((1,), (1,)), ((), ())),
        preferred_element_type=jnp.float32,
    )


def first_kernel(start, rows_ref, weight_ref, sum_ref):
    sum_ref[...] = rows_times_weight(start, rows_ref, weight_ref)


def middle_kernel(start, held_ref, rows_ref, weight_ref, sum_ref):
    sum_ref[...] = held_ref[...] + rows_times_weight(start, rows_ref, weight_ref)


def grad_hidden_step(held, rows, weight, start):
    row_count, width = rows.shape
    hidden_width = weight.shape[0]
    step = 2 * LANES
    block = pl.BlockSpec((row_count, step), lambda i: (0, i))
    specs = [
        pl.BlockSpec((row_count, width), lambda i: (0, 0)),
        pl.BlockSpec((step, weight.shape[1]), lambda i: (i, 0)),
    ]
    return pl.pallas_call(
        functools.partial(first_kernel if held is None else middle_kernel, start),
        grid=(hidden_width // step,),
        in_specs=specs if held is None else [block] + specs,
        out_specs=block,
        out_shape=jax.ShapeDtypeStruct((row_count, hidden_width), jnp.float32),
        compiler_params=params(),
        cost_estimate=cost(2 * row_count * hidden_width * width, 8 * row_count * hidden_width),
    )(*([rows, weight] if held is None else [held, rows, weight]))


def last_kernel(
    capacity,
    start,
    held_ref,
    rows_ref,
    weight_ref,
    hidden_ref,
    up_scale_ref,
    gate_scale_ref,
    grad_gate_ref,
    grad_up_ref,
    slot_ref,
    sum_ref,
):
    grid_place = pl.program_id(0)
    grad_hidden = held_ref[...] + rows_times_weight(start, rows_ref, weight_ref)
    grad_up_ref[...] = (grad_hidden * up_scale_ref[...]).astype(jnp.bfloat16)
    grad_gate_ref[...] = (grad_hidden * gate_scale_ref[...]).astype(jnp.bfloat16)
    product = hidden_ref[...].astype(jnp.float32) * grad_hidden
    folded = product[:, :LANES]
    for column in range(LANES, product.shape[1], LANES):
        folded = folded + product[:, column : column + LANES]

    @pl.when(grid_place == 0)
    def _():
        sum_ref[...] = folded

    @pl.when(grid_place > 0)
    def _():
        sum_ref[...] = sum_ref[...] + folded

    @pl.when(grid_place == pl.num_programs(0) - 1)
    def _():
        line = jnp.sum(sum_ref[...].T, axis=0, keepdims=True)
        slot_ref[...] = jnp.zeros_like(slot_ref)
        for source in range(slot_ref.shape[0]):
            slot_ref[source : source + 1, 0:capacity] = line[
                :, source * capacity : (source + 1) * capacity
            ]


def grad_hidden_last(held, rows, weight, start, hidden, up_scale, gate_scale, capacity):
    row_count, width = rows.shape
    hidden_width = weight.shape[0]
    step = 2 * LANES
    block = pl.BlockSpec((row_count, step), lambda i: (0, i))
    expert_count = row_count // capacity
    return pl.pallas_call(
        functools.partial(last_kernel, capacity, start),
        grid=(hidden_width // step,),
        in_specs=[
            block,
            pl.BlockSpec((row_count, width), lambda i: (0, 0)),
            pl.BlockSpec((step, weight.shape[1]), lambda i: (i, 0)),
            block,
            block,
            block,
        ],
        out_specs=[block, block, pl.BlockSpec((expert_count, LANES), lambda i: (0, 0))],
        out_shape=[jax.ShapeDtypeStruct((row_count, hidden_width), jnp.bfloat16)] * 2
        + [jax.ShapeDtypeStruct((expert_count, LANES), jnp.float32)],
        scratch_shapes=[pltpu.VMEM((row_count, LANES), jnp.float32)],
        compiler_params=params(),
        cost_estimate=cost(2 * row_count * hidden_width * width, 12 * row_count * hidden_width),
    )(held, rows, weight, hidden, up_scale, gate_scale)


def route_kernel(capacity, meta_ref, near_ref, far_ref, out_ref, table_ref):
    top_count, token_count = out_ref.shape
    expert_count = table_ref.shape[0]
    half = expert_count // 2
    for offset in range(expert_count):
        block_ref = near_ref if offset < half else far_ref
        row = offset % half * expert_count + lax.axis_index("expert")
        table_ref[offset : offset + 1, :] = block_ref[pl.ds(row, 1), :]
    table = table_ref[...].T
    meta = meta_ref[...].astype(jnp.float32)
    slots = lax.broadcasted_iota(jnp.int32, (capacity, token_count), 0).astype(jnp.float32)
    for k in range(top_count):
        name, slot, prob = (meta[k + top_count * i :][:1, :] for i in range(3))
        picked = jnp.zeros((capacity, token_count), jnp.float32)
        for offset in range(expert_count):
            expert = lax.bitwise_xor(lax.axis_index("expert"), offset).astype(jnp.float32)
            wanted = jnp.where(name == expert, slot, -1.0)
            picked = picked + jnp.where(
                slots == wanted, table[:capacity, offset : offset + 1], 0.0
            )
        out_ref[k : k + 1, :] = jnp.sum(picked, axis=0, keepdims=True) / prob


def route_back(meta, near, far, expert_count, top_count, capacity):
    token_count = meta.shape[1]
    return pl.pallas_call(
        functools.partial(route_kernel, capacity),
        in_specs=[VMEM] * 3,
        out_shape=jax.ShapeDtypeStruct((top_count, token_count), jnp.float32),
        scratch_shapes=[pltpu.VMEM((expert_count, LANES), jnp.float32)],
        compiler_params=params(),
        cost_estimate=cost(1000000, 100000),
    )(meta, near, far)


def after_kernel(*refs):
    pass


def after(value, *earlier):
    return pl.pallas_call(
        after_kernel,
        in_specs=[ANY] * (1 + len(earlier)),
        out_specs=ANY,
        out_shape=jax.ShapeDtypeStruct(value.shape, value.dtype),
        input_output_aliases={0: 0},
        compiler_params=params(),
        cost_estimate=cost(64, 64),
    )(value, *earlier)


def swap(value, offset):
    size = lax.axis_size("expert")
    return lax.ppermute(value, "expert", [(place, place ^ offset) for place in range(size)])


def swap_groups(value, later):
    groups, places = lax.axis_size("dp"), lax.axis_size("expert")
    pairs = []
    for group in range(groups):
        for place in range(places):
            other = group ^ (1 + (place & 1) ^ (3 if later else 0))
            pairs.append((group * places + place, other * places + place))
    return lax.ppermute(value, ("dp", "expert"), pairs)


def line_shards(grad_out, probs, routes, saved_gate, saved_up, w_down):
    expert_count = lax.axis_size("expert")
    capacity = saved_gate.shape[3]
    hidden_width = saved_gate.shape[4]
    token_count, model_width = grad_out.shape
    top_count = routes.shape[1]
    row_count = expert_count * capacity

    meta, *parts = token_parts(routes.T, probs.T, grad_out, expert_count)
    parts = [swap(part, 4) for part in parts]
    metas = [meta, swap(meta, 1)]
    local, sent = dispatch(
        metas, [grad_out, swap(grad_out, 1)], capacity, top_count, 0, model_width
    )
    near = swap(sent, 2)
    weight = w_down[0]
    turned, hidden, up_scale, gate_scale = hidden_parts(
        saved_gate.reshape(row_count, hidden_width), saved_up.reshape(row_count, hidden_width)
    )
    held, start = None, 0
    halves, owns, arrived = [], [], []
    for part, widths in enumerate(PARTS):
        part_start, part_width = start, sum(widths)
        parts[part] = after(parts[part], sent)
        other_part = swap(parts[part], 1)
        far_metas = [parts[0], other_part] if part == 0 else far_metas
        far_local, sent = dispatch(
            far_metas,
            [parts[part], other_part],
            capacity,
            top_count,
            0,
            part_width,
            [near] if part == 0 else [],
        )
        far_near = swap(sent, 2)
        for width in widths:
            blocks = [(local, start), (near, start)]
            blocks += [(far_local, start - part_start), (far_near, start - part_start)]
            earlier = ([] if held is None else [held]) + halves[:-1]
            rows, own, later, half = panel_parts(turned, blocks, capacity, width, earlier)
            earlier = []
            if start + width < model_width:
                held = grad_hidden_step(held, rows, weight, start)
            else:
                grad_gate, grad_up, lines = grad_hidden_last(
                    held, rows, weight, start, hidden, up_scale, gate_scale, capacity
                )
                lines = jnp.concatenate([lines, swap(lines, 1)], axis=0)
                earlier = [lines]
            own, half = halve(own, later, swap_groups(half, False), earlier)
            halves.append(half)
            owns.append(own)
            arrived.append(swap_groups(half, True))
            start += width
    lines = jnp.concatenate([lines, swap(lines, 2)], axis=0)
    panel = total(owns, arrived)
    route_grad = route_back(meta, lines, swap(lines, 4), expert_count, top_count, capacity)
    return (
        grad_gate.reshape(saved_gate.shape),
        grad_up.reshape(saved_up.shape),
        panel[None],
        route_grad.T,
    )


def plain_shards(grad_out, probs, routes, saved_gate, saved_up, w_down):
    expert_count = lax.axis_size("expert")
    capacity = saved_gate.shape[3]
    hidden_width = saved_gate.shape[4]
    token_count, top_count = routes.shape
    model_width = grad_out.shape[1]
    row_count = expert_count * capacity
    flat_routes = routes.reshape(-1)
    onehot = (flat_routes[:, None] == jnp.arange(expert_count)[None, :]).astype(jnp.int32)
    before = jnp.cumsum(onehot, axis=0) - onehot
    position = flat_routes * capacity + jnp.sum(before * onehot, axis=1)
    selector = jnp.arange(row_count)[:, None] == position[None, :]
    selector = jnp.where(selector, probs.reshape(-1)[None], 0).reshape(
        row_count, token_count, top_count
    )
    sent = jnp.dot(jnp.sum(selector, axis=2), grad_out, preferred_element_type=jnp.float32)
    rows = lax.all_to_all(
        sent.astype(jnp.bfloat16).reshape(expert_count, capacity, model_width),
        "expert",
        split_axis=0,
        concat_axis=0,
        tiled=True,
    ).reshape(row_count, model_width)
    up_value = saved_up.reshape(row_count, hidden_width).astype(jnp.float32)
    activation, gate_slope = silu_parts(
        saved_gate.reshape(row_count, hidden_width).astype(jnp.float32)
    )
    hidden = (activation * up_value).astype(jnp.bfloat16)
    grad_hidden = lax.dot_general(
        rows, w_down[0], (((1,), (1,)), ((), ())), preferred_element_type=jnp.float32
    )
    slot_grad = jnp.sum(hidden.astype(jnp.float32) * grad_hidden, axis=1)
    grad_up = (grad_hidden * activation).astype(jnp.bfloat16)
    grad_gate = (grad_hidden * up_value * gate_slope).astype(jnp.bfloat16)
    whole_panel = lax.dot_general(
        hidden, rows, (((0,), (0,)), ((), ())), preferred_element_type=jnp.float32
    )
    panel = lax.psum_scatter(whole_panel, "dp", scatter_dimension=0, tiled=True)
    returned = lax.all_to_all(
        slot_grad.reshape(expert_count, capacity), "expert", split_axis=0, concat_axis=0, tiled=True
    )
    route_grad = jnp.take(returned.reshape(-1), position, axis=0).reshape(token_count, top_count)
    return (
        grad_gate.reshape(saved_gate.shape),
        grad_up.reshape(saved_up.shape),
        panel[None],
        route_grad / probs.astype(jnp.float32),
    )


def shards(grad_out, probs, routes, saved_gate, saved_up, w_down):
    expert_count = lax.axis_size("expert")
    group_count = lax.axis_size("dp")
    capacity, hidden_width = saved_gate.shape[3:]
    aligned = (
        expert_count == 8
        and group_count == 4
        and capacity % 16 == 0
        and capacity <= LANES
        and hidden_width % (16 * group_count) == 0
        and routes.shape[0] == LANES
        and grad_out.shape[1] == sum(map(sum, PARTS))
    )
    run = line_shards if aligned else plain_shards
    return run(grad_out, probs, routes, saved_gate, saved_up, w_down)


def solution(mesh):
    return jax.shard_map(
        shards,
        mesh=mesh,
        in_specs=(
            P(("dp", "expert"), None),
            P(("dp", "expert"), None),
            P(("dp", "expert"), None),
            P("dp", "expert", None, None, None),
            P("dp", "expert", None, None, None),
            P("expert", None, None),
        ),
        out_specs=(
            P("dp", "expert", None, None, None),
            P("dp", "expert", None, None, None),
            P("expert", "dp", None),
            P(("dp", "expert"), None),
        ),
        check_vma=False,
    )
```

```python
import functools

import jax
import jax.numpy as jnp
from jax import lax
from jax.experimental import pallas as pl
from jax.experimental.pallas import tpu as pltpu
from jax.sharding import PartitionSpec as P

LANES = 128
META = 16
PARTS = ((896,), (640, 512))
VMEM_LIMIT = 10 * 1024 * 1024
VMEM = pl.BlockSpec(memory_space=pltpu.VMEM)
ANY = pl.BlockSpec(memory_space=pl.ANY)
HBM = pl.BlockSpec(memory_space=pltpu.HBM)


def params():
    return pltpu.CompilerParams(vmem_limit_bytes=VMEM_LIMIT)


def cost(flops, moved):
    return pl.CostEstimate(flops=flops // 64, bytes_accessed=moved // 64, transcendentals=0)


def silu_parts(gate_value):
    sigmoid = jax.nn.sigmoid(gate_value)
    return (gate_value * sigmoid, sigmoid * (1.0 + gate_value * (1.0 - sigmoid)))


def tokens_kernel(expert_count, routes_hbm, probs_hbm, rows_hbm, meta_ref, *refs):
    part_refs, (routes_ref, probs_ref, semaphores) = refs[:-3], refs[-3:]
    token_count = rows_hbm.shape[0]
    top_count = routes_ref.shape[0]
    copies = [
        pltpu.make_async_copy(routes_hbm, routes_ref, semaphores.at[0]),
        pltpu.make_async_copy(probs_hbm, probs_ref, semaphores.at[1]),
    ]
    start = 0
    for part, part_ref in enumerate(part_refs):
        width = part_ref.shape[1]
        copies.append(
            pltpu.make_async_copy(
                rows_hbm.at[:, start : start + width],
                part_ref.at[:token_count, :],
                semaphores.at[2 + part],
            )
        )
        start += width
    for copy in copies:
        copy.start()
    for copy in copies[:2]:
        copy.wait()
    names = [routes_ref[k : k + 1, :] for k in range(top_count)]
    experts = lax.broadcasted_iota(jnp.int32, (expert_count, token_count), 0)
    onehots = [(experts == name).astype(jnp.float32) for name in names]
    earlier = (
        lax.broadcasted_iota(jnp.int32, (token_count, token_count), 0)
        < lax.broadcasted_iota(jnp.int32, (token_count, token_count), 1)
    ).astype(jnp.bfloat16)
    before = jnp.dot(
        sum(onehots).astype(jnp.bfloat16), earlier, preferred_element_type=jnp.float32
    )
    lines = [name.astype(jnp.float32) for name in names]
    for onehot in onehots:
        lines.append(jnp.sum(before * onehot, axis=0, keepdims=True))
        before = before + onehot
    for k in range(top_count):
        lines.append(probs_ref[k : k + 1, :].astype(jnp.float32))
    lines.append(jnp.zeros((META - len(lines), token_count), jnp.float32))
    meta = jnp.concatenate(lines, axis=0).astype(jnp.bfloat16)
    meta_ref[...] = meta
    lead_ref = part_refs[0]
    lead_ref[token_count:, :] = jnp.zeros((META, lead_ref.shape[1]), jnp.bfloat16)
    lead_ref[token_count:, :token_count] = meta
    for copy in copies[2:]:
        copy.wait()


def token_parts(routes, probs, grad_out, expert_count):
    token_count = routes.shape[1]
    return pl.pallas_call(
        functools.partial(tokens_kernel, expert_count),
        in_specs=[HBM] * 3,
        out_shape=[jax.ShapeDtypeStruct((META, token_count), jnp.bfloat16)]
        + [
            jax.ShapeDtypeStruct((token_count + (0 if part else META), width), jnp.bfloat16)
            for part, width in enumerate(map(sum, PARTS))
        ],
        scratch_shapes=[
            pltpu.VMEM(routes.shape, routes.dtype),
            pltpu.VMEM(probs.shape, probs.dtype),
            pltpu.SemaphoreType.DMA((2 + len(PARTS),)),
        ],
        compiler_params=params(),
        cost_estimate=cost(100 * token_count * token_count, 4 * grad_out.size),
    )(routes, probs, grad_out)


def chosen_rows(meta, top_count, capacity):
    token_count = meta.shape[1]
    slots = lax.broadcasted_iota(jnp.int32, (capacity, token_count), 0).astype(jnp.float32)
    parts = []
    for offset in (0, 2):
        target = lax.bitwise_xor(lax.axis_index("expert"), offset).astype(jnp.float32)
        part = jnp.zeros((capacity, token_count), jnp.float32)
        for k in range(top_count):
            name, slot, prob = (meta[k + top_count * i :][:1, :] for i in range(3))
            slot = jnp.where(name == target, slot, -1.0)
            part = part + jnp.where(slots == slot, prob, 0.0)
        parts.append(part)
    return jnp.concatenate(parts, axis=0).astype(jnp.bfloat16)


def dispatch_kernel(capacity, top_count, start, *refs):
    meta_refs, row_refs, (local_ref, sent_ref) = refs[:2], refs[2:4], refs[-2:]
    token_count = meta_refs[0].shape[1] if meta_refs[0].shape[0] == META else LANES
    width = local_ref.shape[1]
    for source in range(2):
        first = meta_refs[source].shape[0] - META
        meta = meta_refs[source][first:, :token_count].astype(jnp.float32)
        rows = jnp.dot(
            chosen_rows(meta, top_count, capacity),
            row_refs[source][:token_count, start : start + width],
            preferred_element_type=jnp.float32,
        ).astype(jnp.bfloat16)
        local_ref[source * capacity : (source + 1) * capacity, :] = rows[:capacity, :]
        sent_ref[source * capacity : (source + 1) * capacity, :] = rows[capacity:, :]


def dispatch(metas, rows, capacity, top_count, start, width, earlier=()):
    block = jax.ShapeDtypeStruct((2 * capacity, width), jnp.bfloat16)
    return pl.pallas_call(
        functools.partial(dispatch_kernel, capacity, top_count, start),
        in_specs=[VMEM] * 4 + [ANY] * len(earlier),
        out_shape=[block, block],
        compiler_params=params(),
        cost_estimate=cost(8 * capacity * LANES * width, 8 * capacity * width),
    )(*metas, *rows, *earlier)


def hidden_kernel(gate_ref, up_ref, turned_ref, hidden_ref, up_scale_ref, gate_scale_ref):
    activation, gate_slope = silu_parts(gate_ref[...].astype(jnp.float32))
    up_value = up_ref[...].astype(jnp.float32)
    hidden = activation * up_value
    turned_ref[...] = hidden.T.astype(jnp.bfloat16)
    hidden_ref[...] = hidden.astype(jnp.bfloat16)
    up_scale_ref[...] = activation
    gate_scale_ref[...] = up_value * gate_slope


def hidden_parts(gate, up):
    row_count, hidden_width = gate.shape
    step = 2 * LANES
    block = pl.BlockSpec((row_count, step), lambda i: (0, i))
    return pl.pallas_call(
        hidden_kernel,
        grid=(hidden_width // step,),
        in_specs=[block] * 2,
        out_specs=[pl.BlockSpec((step, row_count), lambda i: (i, 0))] + [block] * 3,
        out_shape=[
            jax.ShapeDtypeStruct((hidden_width, row_count), jnp.bfloat16),
            jax.ShapeDtypeStruct((row_count, hidden_width), jnp.bfloat16),
            jax.ShapeDtypeStruct((row_count, hidden_width), jnp.float32),
            jax.ShapeDtypeStruct((row_count, hidden_width), jnp.float32),
        ],
        compiler_params=params(),
        cost_estimate=cost(20 * row_count * hidden_width, 16 * row_count * hidden_width),
    )(gate, up)


def panel_kernel(capacity, columns, turned_ref, *refs):
    block_refs, (rows_ref, own_ref, later_ref, sent_ref) = refs[:4], refs[-4:]
    share, width = own_ref.shape
    device = lax.axis_index("expert")
    for block, (block_ref, column) in enumerate(zip(block_refs, columns)):
        for half in range(2):
            place = lax.bitwise_xor(device, 2 * block + half)
            row = pl.multiple_of(place * capacity, capacity)
            rows_ref[pl.ds(row, capacity), :] = block_ref[
                half * capacity : (half + 1) * capacity, column : column + width
            ]
    rows = rows_ref[...]

    def part(offset):
        owner = lax.bitwise_xor(lax.axis_index("dp"), offset)
        row = pl.multiple_of(owner * share, share)
        return jnp.dot(turned_ref[pl.ds(row, share), :], rows, preferred_element_type=jnp.float32)

    step = 1 + lax.bitwise_and(device, 1)
    sent_ref[:share, :] = part(step).astype(jnp.bfloat16)
    sent_ref[share:, :] = part(3).astype(jnp.bfloat16)
    later_ref[...] = part(3 - step)
    own_ref[...] = part(0)


def panel_parts(turned, blocks, capacity, width, earlier):
    hidden_width, row_count = turned.shape
    share = hidden_width // 4
    return pl.pallas_call(
        functools.partial(panel_kernel, capacity, [column for _, column in blocks]),
        in_specs=[VMEM] * 5 + [ANY] * len(earlier),
        out_shape=[
            jax.ShapeDtypeStruct((row_count, width), jnp.bfloat16),
            jax.ShapeDtypeStruct((share, width), jnp.float32),
            jax.ShapeDtypeStruct((share, width), jnp.float32),
            jax.ShapeDtypeStruct((2 * share, width), jnp.bfloat16),
        ],
        compiler_params=params(),
        cost_estimate=cost(
            2 * hidden_width * row_count * width, 2 * hidden_width * (row_count + width)
        ),
    )(turned, *[block for block, _ in blocks], *earlier)


def halve_kernel(own_ref, later_ref, arrived_ref, *refs):
    sum_ref, sent_ref = refs[-2:]
    share = own_ref.shape[0]
    sent_ref[...] = (later_ref[...] + arrived_ref[share:, :].astype(jnp.float32)).astype(
        jnp.bfloat16
    )
    sum_ref[...] = own_ref[...] + arrived_ref[:share, :].astype(jnp.float32)


def halve(own, later, arrived, earlier):
    return pl.pallas_call(
        halve_kernel,
        in_specs=[VMEM] * 3 + [ANY] * len(earlier),
        out_shape=[
            jax.ShapeDtypeStruct(own.shape, jnp.float32),
            jax.ShapeDtypeStruct(own.shape, jnp.bfloat16),
        ],
        compiler_params=params(),
        cost_estimate=cost(4 * own.size, 18 * own.size),
    )(own, later, arrived, *earlier)


def total_kernel(count, *refs):
    own_refs, arrived_refs = refs[:count], refs[count : 2 * count]
    total_ref, *sum_refs, semaphores = refs[-2 - count :]
    copies = []
    start = 0
    for place, (own_ref, arrived_ref) in enumerate(zip(own_refs, arrived_refs)):
        width = own_ref.shape[1]
        sum_refs[place][...] = own_ref[...] + arrived_ref[...].astype(jnp.float32)
        copies.append(
            pltpu.make_async_copy(
                sum_refs[place], total_ref.at[:, start : start + width], semaphores.at[place]
            )
        )
        copies[-1].start()
        start += width
    for copy in copies:
        copy.wait()


def total(owns, arrived, earlier):
    share = owns[0].shape[0]
    size = share * sum(own.shape[1] for own in owns)
    return pl.pallas_call(
        functools.partial(total_kernel, len(owns)),
        in_specs=[VMEM] * (2 * len(owns)) + [ANY] * len(earlier),
        out_specs=HBM,
        out_shape=jax.ShapeDtypeStruct((share, size // share), jnp.float32),
        scratch_shapes=[pltpu.VMEM(own.shape, jnp.float32) for own in owns]
        + [pltpu.SemaphoreType.DMA((len(owns),))],
        compiler_params=params(),
        cost_estimate=cost(2 * size, 10 * size),
    )(*owns, *arrived, *earlier)


def rows_times_weight(start, rows_ref, weight_ref):
    return lax.dot_general(
        rows_ref[...],
        weight_ref[:, start : start + rows_ref.shape[1]],
        (((1,), (1,)), ((), ())),
        preferred_element_type=jnp.float32,
    )


def first_kernel(start, rows_ref, weight_ref, sum_ref):
    sum_ref[...] = rows_times_weight(start, rows_ref, weight_ref)


def middle_kernel(start, held_ref, rows_ref, weight_ref, sum_ref):
    sum_ref[...] = held_ref[...] + rows_times_weight(start, rows_ref, weight_ref)


def grad_hidden_step(held, rows, weight, start):
    row_count, width = rows.shape
    hidden_width = weight.shape[0]
    step = 2 * LANES
    block = pl.BlockSpec((row_count, step), lambda i: (0, i))
    specs = [
        pl.BlockSpec((row_count, width), lambda i: (0, 0)),
        pl.BlockSpec((step, weight.shape[1]), lambda i: (i, 0)),
    ]
    return pl.pallas_call(
        functools.partial(first_kernel if held is None else middle_kernel, start),
        grid=(hidden_width // step,),
        in_specs=specs if held is None else [block] + specs,
        out_specs=block,
        out_shape=jax.ShapeDtypeStruct((row_count, hidden_width), jnp.float32),
        compiler_params=params(),
        cost_estimate=cost(2 * row_count * hidden_width * width, 8 * row_count * hidden_width),
    )(*([rows, weight] if held is None else [held, rows, weight]))


def last_kernel(
    capacity,
    start,
    held_ref,
    rows_ref,
    weight_ref,
    hidden_ref,
    up_scale_ref,
    gate_scale_ref,
    grad_gate_ref,
    grad_up_ref,
    slot_ref,
    sum_ref,
):
    grid_place = pl.program_id(0)
    grad_hidden = held_ref[...] + rows_times_weight(start, rows_ref, weight_ref)
    grad_up_ref[...] = (grad_hidden * up_scale_ref[...]).astype(jnp.bfloat16)
    grad_gate_ref[...] = (grad_hidden * gate_scale_ref[...]).astype(jnp.bfloat16)
    product = hidden_ref[...].astype(jnp.float32) * grad_hidden
    folded = product[:, :LANES]
    for column in range(LANES, product.shape[1], LANES):
        folded = folded + product[:, column : column + LANES]

    @pl.when(grid_place == 0)
    def _():
        sum_ref[...] = folded

    @pl.when(grid_place > 0)
    def _():
        sum_ref[...] = sum_ref[...] + folded

    @pl.when(grid_place == pl.num_programs(0) - 1)
    def _():
        line = jnp.sum(sum_ref[...].T, axis=0, keepdims=True)
        slot_ref[...] = jnp.zeros_like(slot_ref)
        for source in range(slot_ref.shape[0]):
            slot_ref[source : source + 1, 0:capacity] = line[
                :, source * capacity : (source + 1) * capacity
            ]


def grad_hidden_last(held, rows, weight, start, hidden, up_scale, gate_scale, capacity):
    row_count, width = rows.shape
    hidden_width = weight.shape[0]
    step = 2 * LANES
    block = pl.BlockSpec((row_count, step), lambda i: (0, i))
    expert_count = row_count // capacity
    return pl.pallas_call(
        functools.partial(last_kernel, capacity, start),
        grid=(hidden_width // step,),
        in_specs=[
            block,
            pl.BlockSpec((row_count, width), lambda i: (0, 0)),
            pl.BlockSpec((step, weight.shape[1]), lambda i: (i, 0)),
            block,
            block,
            block,
        ],
        out_specs=[block, block, pl.BlockSpec((expert_count, LANES), lambda i: (0, 0))],
        out_shape=[jax.ShapeDtypeStruct((row_count, hidden_width), jnp.bfloat16)] * 2
        + [jax.ShapeDtypeStruct((expert_count, LANES), jnp.float32)],
        scratch_shapes=[pltpu.VMEM((row_count, LANES), jnp.float32)],
        compiler_params=params(),
        cost_estimate=cost(2 * row_count * hidden_width * width, 12 * row_count * hidden_width),
    )(held, rows, weight, hidden, up_scale, gate_scale)


def route_kernel(capacity, meta_ref, near_ref, far_ref, out_ref, table_ref):
    top_count, token_count = out_ref.shape
    expert_count = table_ref.shape[0]
    half = expert_count // 2
    for offset in range(expert_count):
        block_ref = near_ref if offset < half else far_ref
        row = offset % half * expert_count + lax.axis_index("expert")
        table_ref[offset : offset + 1, :] = block_ref[pl.ds(row, 1), :]
    table = table_ref[...].T
    meta = meta_ref[...].astype(jnp.float32)
    slots = lax.broadcasted_iota(jnp.int32, (capacity, token_count), 0).astype(jnp.float32)
    for k in range(top_count):
        name, slot, prob = (meta[k + top_count * i :][:1, :] for i in range(3))
        picked = jnp.zeros((capacity, token_count), jnp.float32)
        for offset in range(expert_count):
            expert = lax.bitwise_xor(lax.axis_index("expert"), offset).astype(jnp.float32)
            wanted = jnp.where(name == expert, slot, -1.0)
            picked = picked + jnp.where(
                slots == wanted, table[:capacity, offset : offset + 1], 0.0
            )
        out_ref[k : k + 1, :] = jnp.sum(picked, axis=0, keepdims=True) / prob


def route_back(meta, near, far, expert_count, top_count, capacity):
    token_count = meta.shape[1]
    return pl.pallas_call(
        functools.partial(route_kernel, capacity),
        in_specs=[VMEM] * 3,
        out_shape=jax.ShapeDtypeStruct((top_count, token_count), jnp.float32),
        scratch_shapes=[pltpu.VMEM((expert_count, LANES), jnp.float32)],
        compiler_params=params(),
        cost_estimate=cost(1000000, 100000),
    )(meta, near, far)


def after_kernel(*refs):
    pass


def after(value, *earlier):
    return pl.pallas_call(
        after_kernel,
        in_specs=[ANY] * (1 + len(earlier)),
        out_specs=ANY,
        out_shape=jax.ShapeDtypeStruct(value.shape, value.dtype),
        input_output_aliases={0: 0},
        compiler_params=params(),
        cost_estimate=cost(64, 64),
    )(value, *earlier)


def swap(value, offset):
    size = lax.axis_size("expert")
    return lax.ppermute(value, "expert", [(place, place ^ offset) for place in range(size)])


def swap_groups(value, later):
    groups, places = lax.axis_size("dp"), lax.axis_size("expert")
    pairs = []
    for group in range(groups):
        for place in range(places):
            other = group ^ (1 + (place & 1) ^ (3 if later else 0))
            pairs.append((group * places + place, other * places + place))
    return lax.ppermute(value, ("dp", "expert"), pairs)


def line_shards(grad_out, probs, routes, saved_gate, saved_up, w_down):
    expert_count = lax.axis_size("expert")
    capacity = saved_gate.shape[3]
    hidden_width = saved_gate.shape[4]
    token_count, model_width = grad_out.shape
    top_count = routes.shape[1]
    row_count = expert_count * capacity

    meta, *parts = token_parts(routes.T, probs.T, grad_out, expert_count)
    parts = [swap(part, 4) for part in parts]
    metas = [meta, swap(meta, 1)]
    near_rows = [grad_out, swap(grad_out, 1)]
    weight = w_down[0]
    turned, hidden, up_scale, gate_scale = hidden_parts(
        saved_gate.reshape(row_count, hidden_width), saved_up.reshape(row_count, hidden_width)
    )
    held, start, far_sent = None, 0, None
    owns, arrived = [], []
    for part, widths in enumerate(PARTS):
        part_width = sum(widths)
        local, sent = dispatch(
            metas,
            near_rows,
            capacity,
            top_count,
            start,
            part_width,
            [] if far_sent is None else [far_sent],
        )
        near = swap(sent, 2)
        parts[part] = after(parts[part], near)
        other_part = swap(parts[part], 1)
        far_metas = [parts[0], other_part] if part == 0 else far_metas
        far_local, far_sent = dispatch(
            far_metas,
            [parts[part], other_part],
            capacity,
            top_count,
            0,
            part_width,
        )
        far_near = swap(far_sent, 2)
        column = 0
        for width in widths:
            blocks = [(block, column) for block in (local, near, far_local, far_near)]
            earlier = [] if held is None else [held]
            rows, own, later, half = panel_parts(turned, blocks, capacity, width, earlier)
            own, half = halve(own, later, swap_groups(half, False), arrived[-1:])
            owns.append(own)
            arrived.append(swap_groups(half, True))
            if start + width < model_width:
                held = grad_hidden_step(held, rows, weight, start)
            else:
                grad_gate, grad_up, lines = grad_hidden_last(
                    held, rows, weight, start, hidden, up_scale, gate_scale, capacity
                )
            start += width
            column += width
    for offset in (1, 2):
        lines = jnp.concatenate([lines, swap(lines, offset)], axis=0)
    route_grad = route_back(meta, lines, swap(lines, 4), expert_count, top_count, capacity)
    panel = total(owns, arrived, [route_grad])
    return (
        grad_gate.reshape(saved_gate.shape),
        grad_up.reshape(saved_up.shape),
        panel[None],
        route_grad.T,
    )


def plain_shards(grad_out, probs, routes, saved_gate, saved_up, w_down):
    expert_count = lax.axis_size("expert")
    capacity = saved_gate.shape[3]
    hidden_width = saved_gate.shape[4]
    token_count, top_count = routes.shape
    model_width = grad_out.shape[1]
    row_count = expert_count * capacity
    flat_routes = routes.reshape(-1)
    onehot = (flat_routes[:, None] == jnp.arange(expert_count)[None, :]).astype(jnp.int32)
    before = jnp.cumsum(onehot, axis=0) - onehot
    position = flat_routes * capacity + jnp.sum(before * onehot, axis=1)
    selector = jnp.arange(row_count)[:, None] == position[None, :]
    selector = jnp.where(selector, probs.reshape(-1)[None], 0).reshape(
        row_count, token_count, top_count
    )
    sent = jnp.dot(jnp.sum(selector, axis=2), grad_out, preferred_element_type=jnp.float32)
    rows = lax.all_to_all(
        sent.astype(jnp.bfloat16).reshape(expert_count, capacity, model_width),
        "expert",
        split_axis=0,
        concat_axis=0,
        tiled=True,
    ).reshape(row_count, model_width)
    up_value = saved_up.reshape(row_count, hidden_width).astype(jnp.float32)
    activation, gate_slope = silu_parts(
        saved_gate.reshape(row_count, hidden_width).astype(jnp.float32)
    )
    hidden = (activation * up_value).astype(jnp.bfloat16)
    grad_hidden = lax.dot_general(
        rows, w_down[0], (((1,), (1,)), ((), ())), preferred_element_type=jnp.float32
    )
    slot_grad = jnp.sum(hidden.astype(jnp.float32) * grad_hidden, axis=1)
    grad_up = (grad_hidden * activation).astype(jnp.bfloat16)
    grad_gate = (grad_hidden * up_value * gate_slope).astype(jnp.bfloat16)
    whole_panel = lax.dot_general(
        hidden, rows, (((0,), (0,)), ((), ())), preferred_element_type=jnp.float32
    )
    panel = lax.psum_scatter(whole_panel, "dp", scatter_dimension=0, tiled=True)
    returned = lax.all_to_all(
        slot_grad.reshape(expert_count, capacity), "expert", split_axis=0, concat_axis=0, tiled=True
    )
    route_grad = jnp.take(returned.reshape(-1), position, axis=0).reshape(token_count, top_count)
    return (
        grad_gate.reshape(saved_gate.shape),
        grad_up.reshape(saved_up.shape),
        panel[None],
        route_grad / probs.astype(jnp.float32),
    )


def shards(grad_out, probs, routes, saved_gate, saved_up, w_down):
    expert_count = lax.axis_size("expert")
    group_count = lax.axis_size("dp")
    capacity, hidden_width = saved_gate.shape[3:]
    aligned = (
        expert_count == 8
        and group_count == 4
        and capacity % 16 == 0
        and capacity <= LANES
        and hidden_width % (16 * group_count) == 0
        and routes.shape[0] == LANES
        and grad_out.shape[1] == sum(map(sum, PARTS))
    )
    run = line_shards if aligned else plain_shards
    return run(grad_out, probs, routes, saved_gate, saved_up, w_down)


def solution(mesh):
    return jax.shard_map(
        shards,
        mesh=mesh,
        in_specs=(
            P(("dp", "expert"), None),
            P(("dp", "expert"), None),
            P(("dp", "expert"), None),
            P("dp", "expert", None, None, None),
            P("dp", "expert", None, None, None),
            P("expert", None, None),
        ),
        out_specs=(
            P("dp", "expert", None, None, None),
            P("dp", "expert", None, None, None),
            P("expert", "dp", None),
            P(("dp", "expert"), None),
        ),
        check_vma=False,
    )
```

```python
import functools

import jax
import jax.numpy as jnp
from jax import lax
from jax.experimental import pallas as pl
from jax.experimental.pallas import tpu as pltpu
from jax.sharding import PartitionSpec as P

LANES = 128
META = 16
WIDTHS = (768, 1280)
VMEM_LIMIT = 10 * 1024 * 1024
VMEM = pl.BlockSpec(memory_space=pltpu.VMEM)
ANY = pl.BlockSpec(memory_space=pl.ANY)


def params():
    return pltpu.CompilerParams(vmem_limit_bytes=VMEM_LIMIT)


def cost(flops, moved):
    return pl.CostEstimate(flops=flops // 64, bytes_accessed=moved // 64, transcendentals=0)


def silu_parts(gate_value):
    sigmoid = jax.nn.sigmoid(gate_value)
    return (gate_value * sigmoid, sigmoid * (1.0 + gate_value * (1.0 - sigmoid)))


def tokens_kernel(expert_count, routes_ref, probs_ref, meta_ref):
    top_count, token_count = routes_ref.shape
    names = [routes_ref[k : k + 1, :] for k in range(top_count)]
    experts = lax.broadcasted_iota(jnp.int32, (expert_count, token_count), 0)
    onehots = [(experts == name).astype(jnp.float32) for name in names]
    earlier = (
        lax.broadcasted_iota(jnp.int32, (token_count, token_count), 0)
        < lax.broadcasted_iota(jnp.int32, (token_count, token_count), 1)
    ).astype(jnp.bfloat16)
    before = jnp.dot(
        sum(onehots).astype(jnp.bfloat16), earlier, preferred_element_type=jnp.float32
    )
    lines = [name.astype(jnp.float32) for name in names]
    for onehot in onehots:
        lines.append(jnp.sum(before * onehot, axis=0, keepdims=True))
        before = before + onehot
    for k in range(top_count):
        lines.append(probs_ref[k : k + 1, :].astype(jnp.float32))
    lines.append(jnp.zeros((META - len(lines), token_count), jnp.float32))
    meta_ref[...] = jnp.concatenate(lines, axis=0).astype(jnp.bfloat16)


def token_lines(routes, probs, expert_count):
    token_count = routes.shape[1]
    return pl.pallas_call(
        functools.partial(tokens_kernel, expert_count),
        in_specs=[VMEM] * 2,
        out_shape=jax.ShapeDtypeStruct((META, token_count), jnp.bfloat16),
        compiler_params=params(),
        cost_estimate=cost(100 * token_count * token_count, 4 * token_count * META),
    )(routes, probs)


def far_offset():
    return 4 + 2 * lax.bitwise_and(lax.axis_index("expert"), 1)


def chosen_rows(meta, top_count, capacity):
    token_count = meta.shape[1]
    slots = lax.broadcasted_iota(jnp.int32, (capacity, token_count), 0).astype(jnp.float32)
    parts = []
    for offset in (0, 2, far_offset(), far_offset() + 1):
        target = lax.bitwise_xor(lax.axis_index("expert"), offset).astype(jnp.float32)
        part = jnp.zeros((capacity, token_count), jnp.float32)
        for k in range(top_count):
            name, slot, prob = (meta[k + top_count * i :][:1, :] for i in range(3))
            slot = jnp.where(name == target, slot, -1.0)
            part = part + jnp.where(slots == slot, prob, 0.0)
        parts.append(part)
    return jnp.concatenate(parts, axis=0).astype(jnp.bfloat16)


def dispatch_kernel(capacity, top_count, start, *refs):
    meta_refs, row_refs, (local_ref, near_ref, far_ref) = refs[:2], refs[2:4], refs[-3:]
    width = local_ref.shape[1]
    for source in range(2):
        rows = jnp.dot(
            chosen_rows(meta_refs[source][...].astype(jnp.float32), top_count, capacity),
            row_refs[source][:, start : start + width],
            preferred_element_type=jnp.float32,
        ).astype(jnp.bfloat16)
        places = [(local_ref, source), (near_ref, source), (far_ref, source), (far_ref, source + 2)]
        for step, (block_ref, place) in enumerate(places):
            block_ref[place * capacity : (place + 1) * capacity, :] = rows[
                step * capacity : (step + 1) * capacity, :
            ]


def dispatch(metas, rows, capacity, top_count, start, width, earlier):
    return pl.pallas_call(
        functools.partial(dispatch_kernel, capacity, top_count, start),
        in_specs=[VMEM] * 4 + [ANY] * len(earlier),
        out_shape=[
            jax.ShapeDtypeStruct((count * capacity, width), jnp.bfloat16) for count in (2, 2, 4)
        ],
        compiler_params=params(),
        cost_estimate=cost(16 * capacity * LANES * width, 16 * capacity * width),
    )(*metas, *rows, *earlier)


def hidden_kernel(gate_ref, up_ref, turned_ref, hidden_ref, up_scale_ref, gate_scale_ref):
    activation, gate_slope = silu_parts(gate_ref[...].astype(jnp.float32))
    up_value = up_ref[...].astype(jnp.float32)
    hidden = activation * up_value
    turned_ref[...] = hidden.T.astype(jnp.bfloat16)
    hidden_ref[...] = hidden.astype(jnp.bfloat16)
    up_scale_ref[...] = activation
    gate_scale_ref[...] = up_value * gate_slope


def hidden_parts(gate, up):
    row_count, hidden_width = gate.shape
    step = 2 * LANES
    block = pl.BlockSpec((row_count, step), lambda i: (0, i))
    return pl.pallas_call(
        hidden_kernel,
        grid=(hidden_width // step,),
        in_specs=[block] * 2,
        out_specs=[pl.BlockSpec((step, row_count), lambda i: (i, 0))] + [block] * 3,
        out_shape=[
            jax.ShapeDtypeStruct((hidden_width, row_count), jnp.bfloat16),
            jax.ShapeDtypeStruct((row_count, hidden_width), jnp.bfloat16),
            jax.ShapeDtypeStruct((row_count, hidden_width), jnp.float32),
            jax.ShapeDtypeStruct((row_count, hidden_width), jnp.float32),
        ],
        compiler_params=params(),
        cost_estimate=cost(20 * row_count * hidden_width, 16 * row_count * hidden_width),
    )(gate, up)


def panel_kernel(capacity, turned_ref, *refs):
    block_refs, (rows_ref, own_ref, later_ref, sent_ref) = refs[:4], refs[-4:]
    share = own_ref.shape[0]
    device = lax.axis_index("expert")
    far = far_offset()
    offsets = ((0, 1), (2, 3), (far, far + 1), (11 - far, 10 - far))
    for block, block_ref in enumerate(block_refs):
        first = 2 * capacity if block == 3 else 0
        for half in range(2):
            place = lax.bitwise_xor(device, offsets[block][half])
            row = pl.multiple_of(place * capacity, capacity)
            rows_ref[pl.ds(row, capacity), :] = block_ref[
                first + half * capacity : first + (half + 1) * capacity, :
            ]
    rows = rows_ref[...]

    def part(offset):
        owner = lax.bitwise_xor(lax.axis_index("dp"), offset)
        row = pl.multiple_of(owner * share, share)
        return jnp.dot(turned_ref[pl.ds(row, share), :], rows, preferred_element_type=jnp.float32)

    step = 1 + lax.bitwise_and(device, 1)
    sent_ref[:share, :] = part(step).astype(jnp.bfloat16)
    sent_ref[share:, :] = part(3).astype(jnp.bfloat16)
    later_ref[...] = part(3 - step)
    own_ref[...] = part(0)


def panel_parts(turned, blocks, capacity, earlier):
    hidden_width, row_count = turned.shape
    width = blocks[0].shape[1]
    share = hidden_width // 4
    return pl.pallas_call(
        functools.partial(panel_kernel, capacity),
        in_specs=[VMEM] * 5 + [ANY] * len(earlier),
        out_shape=[
            jax.ShapeDtypeStruct((row_count, width), jnp.bfloat16),
            jax.ShapeDtypeStruct((share, width), jnp.float32),
            jax.ShapeDtypeStruct((share, width), jnp.float32),
            jax.ShapeDtypeStruct((2 * share, width), jnp.bfloat16),
        ],
        compiler_params=params(),
        cost_estimate=cost(
            2 * hidden_width * row_count * width, 2 * hidden_width * (row_count + width)
        ),
    )(turned, *blocks, *earlier)


def halve_kernel(own_ref, later_ref, arrived_ref, *refs):
    sum_ref, sent_ref = refs[-2:]
    share = own_ref.shape[0]
    sent_ref[...] = (later_ref[...] + arrived_ref[share:, :].astype(jnp.float32)).astype(
        jnp.bfloat16
    )
    sum_ref[...] = own_ref[...] + arrived_ref[:share, :].astype(jnp.float32)


def halve(own, later, arrived, earlier):
    return pl.pallas_call(
        halve_kernel,
        in_specs=[VMEM] * 3 + [ANY] * len(earlier),
        out_shape=[
            jax.ShapeDtypeStruct(own.shape, jnp.float32),
            jax.ShapeDtypeStruct(own.shape, jnp.bfloat16),
        ],
        compiler_params=params(),
        cost_estimate=cost(4 * own.size, 18 * own.size),
    )(own, later, arrived, *earlier)


def total_kernel(count, *refs):
    own_refs, arrived_refs = refs[:count], refs[count : 2 * count]
    total_ref, *sum_refs, semaphores = refs[-2 - count :]
    copies = []
    start = 0
    for place, (own_ref, arrived_ref) in enumerate(zip(own_refs, arrived_refs)):
        width = own_ref.shape[1]
        sum_refs[place][...] = own_ref[...] + arrived_ref[...].astype(jnp.float32)
        copies.append(
            pltpu.make_async_copy(
                sum_refs[place], total_ref.at[:, start : start + width], semaphores.at[place]
            )
        )
        copies[-1].start()
        start += width
    for copy in copies:
        copy.wait()


def total(owns, arrived, earlier):
    share = owns[0].shape[0]
    size = share * sum(own.shape[1] for own in owns)
    return pl.pallas_call(
        functools.partial(total_kernel, len(owns)),
        in_specs=[VMEM] * (2 * len(owns)) + [ANY] * len(earlier),
        out_specs=ANY,
        out_shape=jax.ShapeDtypeStruct((share, size // share), jnp.float32),
        scratch_shapes=[pltpu.VMEM(own.shape, jnp.float32) for own in owns]
        + [pltpu.SemaphoreType.DMA((len(owns),))],
        compiler_params=params(),
        cost_estimate=cost(2 * size, 10 * size),
    )(*owns, *arrived, *earlier)


def rows_times_weight(start, rows_ref, weight_ref):
    return lax.dot_general(
        rows_ref[...],
        weight_ref[:, start : start + rows_ref.shape[1]],
        (((1,), (1,)), ((), ())),
        preferred_element_type=jnp.float32,
    )


def first_kernel(start, rows_ref, weight_ref, sum_ref):
    sum_ref[...] = rows_times_weight(start, rows_ref, weight_ref)


def middle_kernel(start, held_ref, rows_ref, weight_ref, sum_ref):
    sum_ref[...] = held_ref[...] + rows_times_weight(start, rows_ref, weight_ref)


def grad_hidden_step(held, rows, weight, start):
    row_count, width = rows.shape
    hidden_width = weight.shape[0]
    step = 2 * LANES
    block = pl.BlockSpec((row_count, step), lambda i: (0, i))
    specs = [
        pl.BlockSpec((row_count, width), lambda i: (0, 0)),
        pl.BlockSpec((step, weight.shape[1]), lambda i: (i, 0)),
    ]
    return pl.pallas_call(
        functools.partial(first_kernel if held is None else middle_kernel, start),
        grid=(hidden_width // step,),
        in_specs=specs if held is None else [block] + specs,
        out_specs=block,
        out_shape=jax.ShapeDtypeStruct((row_count, hidden_width), jnp.float32),
        compiler_params=params(),
        cost_estimate=cost(2 * row_count * hidden_width * width, 8 * row_count * hidden_width),
    )(*([rows, weight] if held is None else [held, rows, weight]))


def last_kernel(
    capacity,
    start,
    held_ref,
    rows_ref,
    weight_ref,
    hidden_ref,
    up_scale_ref,
    gate_scale_ref,
    grad_gate_ref,
    grad_up_ref,
    slot_ref,
    sum_ref,
):
    grid_place = pl.program_id(0)
    grad_hidden = held_ref[...] + rows_times_weight(start, rows_ref, weight_ref)
    grad_up_ref[...] = (grad_hidden * up_scale_ref[...]).astype(jnp.bfloat16)
    grad_gate_ref[...] = (grad_hidden * gate_scale_ref[...]).astype(jnp.bfloat16)
    product = hidden_ref[...].astype(jnp.float32) * grad_hidden
    folded = product[:, :LANES]
    for column in range(LANES, product.shape[1], LANES):
        folded = folded + product[:, column : column + LANES]

    @pl.when(grid_place == 0)
    def _():
        sum_ref[...] = folded

    @pl.when(grid_place > 0)
    def _():
        sum_ref[...] = sum_ref[...] + folded

    @pl.when(grid_place == pl.num_programs(0) - 1)
    def _():
        line = jnp.sum(sum_ref[...].T, axis=0, keepdims=True)
        slot_ref[...] = jnp.zeros_like(slot_ref)
        for source in range(slot_ref.shape[0]):
            slot_ref[source : source + 1, 0:capacity] = line[
                :, source * capacity : (source + 1) * capacity
            ]


def grad_hidden_last(held, rows, weight, start, hidden, up_scale, gate_scale, capacity):
    row_count, width = rows.shape
    hidden_width = weight.shape[0]
    step = 2 * LANES
    block = pl.BlockSpec((row_count, step), lambda i: (0, i))
    expert_count = row_count // capacity
    return pl.pallas_call(
        functools.partial(last_kernel, capacity, start),
        grid=(hidden_width // step,),
        in_specs=[
            block,
            pl.BlockSpec((row_count, width), lambda i: (0, 0)),
            pl.BlockSpec((step, weight.shape[1]), lambda i: (i, 0)),
            block,
            block,
            block,
        ],
        out_specs=[block, block, pl.BlockSpec((expert_count, LANES), lambda i: (0, 0))],
        out_shape=[jax.ShapeDtypeStruct((row_count, hidden_width), jnp.bfloat16)] * 2
        + [jax.ShapeDtypeStruct((expert_count, LANES), jnp.float32)],
        scratch_shapes=[pltpu.VMEM((row_count, LANES), jnp.float32)],
        compiler_params=params(),
        cost_estimate=cost(2 * row_count * hidden_width * width, 12 * row_count * hidden_width),
    )(held, rows, weight, hidden, up_scale, gate_scale)


def route_kernel(capacity, meta_ref, near_ref, far_ref, out_ref, table_ref):
    top_count, token_count = out_ref.shape
    expert_count = table_ref.shape[0]
    half = expert_count // 2
    for offset in range(expert_count):
        block_ref = near_ref if offset < half else far_ref
        row = offset % half * expert_count + lax.axis_index("expert")
        table_ref[offset : offset + 1, :] = block_ref[pl.ds(row, 1), :]
    table = table_ref[...].T
    meta = meta_ref[...].astype(jnp.float32)
    slots = lax.broadcasted_iota(jnp.int32, (capacity, token_count), 0).astype(jnp.float32)
    for k in range(top_count):
        name, slot, prob = (meta[k + top_count * i :][:1, :] for i in range(3))
        picked = jnp.zeros((capacity, token_count), jnp.float32)
        for offset in range(expert_count):
            expert = lax.bitwise_xor(lax.axis_index("expert"), offset).astype(jnp.float32)
            wanted = jnp.where(name == expert, slot, -1.0)
            picked = picked + jnp.where(
                slots == wanted, table[:capacity, offset : offset + 1], 0.0
            )
        out_ref[k : k + 1, :] = jnp.sum(picked, axis=0, keepdims=True) / prob


def route_back(meta, near, far, expert_count, top_count, capacity):
    token_count = meta.shape[1]
    return pl.pallas_call(
        functools.partial(route_kernel, capacity),
        in_specs=[VMEM] * 3,
        out_shape=jax.ShapeDtypeStruct((top_count, token_count), jnp.float32),
        scratch_shapes=[pltpu.VMEM((expert_count, LANES), jnp.float32)],
        compiler_params=params(),
        cost_estimate=cost(1000000, 100000),
    )(meta, near, far)


def after_kernel(*refs):
    pass


def after(value, *earlier):
    return pl.pallas_call(
        after_kernel,
        in_specs=[ANY] * (1 + len(earlier)),
        out_specs=ANY,
        out_shape=jax.ShapeDtypeStruct(value.shape, value.dtype),
        input_output_aliases={0: 0},
        compiler_params=params(),
        cost_estimate=cost(64, 64),
    )(value, *earlier)


def swap(value, offset):
    size = lax.axis_size("expert")
    return lax.ppermute(value, "expert", [(place, place ^ offset) for place in range(size)])


def swap_far(value):
    size = lax.axis_size("expert")
    pairs = [(place, place ^ (4 + 2 * (place & 1))) for place in range(size)]
    return lax.ppermute(value, "expert", pairs)


def swap_groups(value, later):
    groups, places = lax.axis_size("dp"), lax.axis_size("expert")
    pairs = []
    for group in range(groups):
        for place in range(places):
            other = group ^ (1 + (place & 1) ^ (3 if later else 0))
            pairs.append((group * places + place, other * places + place))
    return lax.ppermute(value, ("dp", "expert"), pairs)


def line_shards(grad_out, probs, routes, saved_gate, saved_up, w_down):
    expert_count = lax.axis_size("expert")
    capacity = saved_gate.shape[3]
    hidden_width = saved_gate.shape[4]
    token_count, model_width = grad_out.shape
    top_count = routes.shape[1]
    row_count = expert_count * capacity

    meta = token_lines(routes.T, probs.T, expert_count)
    metas = [meta, swap(meta, 1)]
    near_rows = [grad_out, swap(grad_out, 1)]
    weight = w_down[0]
    turned, hidden, up_scale, gate_scale = hidden_parts(
        saved_gate.reshape(row_count, hidden_width), saved_up.reshape(row_count, hidden_width)
    )
    held, start = None, 0
    all_rows, owns, arrived = [], [], []
    for chunk, width in enumerate(WIDTHS):
        earlier = all_rows[chunk - 2 : chunk - 1] if chunk > 1 else []
        local, near, far = dispatch(metas, near_rows, capacity, top_count, start, width, earlier)
        near = swap(near, 2)
        far = after(swap_far(far), near, *all_rows[-1:])
        blocks = [local, near, far, swap(far, 1)]
        earlier = [] if held is None else [held, own]
        rows, own, later, half = panel_parts(turned, blocks, capacity, earlier)
        all_rows.append(rows)
        own, half = halve(own, later, swap_groups(half, False), arrived[-1:])
        owns.append(own)
        arrived.append(swap_groups(half, True))
        if chunk + 1 < len(WIDTHS):
            held = grad_hidden_step(held, rows, weight, start)
        else:
            grad_gate, grad_up, lines = grad_hidden_last(
                held, rows, weight, start, hidden, up_scale, gate_scale, capacity
            )
        start += width
    for offset in (1, 2):
        lines = jnp.concatenate([lines, swap(lines, offset)], axis=0)
    far_lines = swap(lines, 4)
    panel = total(owns, arrived, [far_lines])
    route_grad = route_back(meta, lines, far_lines, expert_count, top_count, capacity)
    return (
        grad_gate.reshape(saved_gate.shape),
        grad_up.reshape(saved_up.shape),
        panel[None],
        route_grad.T,
    )


def plain_shards(grad_out, probs, routes, saved_gate, saved_up, w_down):
    expert_count = lax.axis_size("expert")
    capacity = saved_gate.shape[3]
    hidden_width = saved_gate.shape[4]
    token_count, top_count = routes.shape
    model_width = grad_out.shape[1]
    row_count = expert_count * capacity
    flat_routes = routes.reshape(-1)
    onehot = (flat_routes[:, None] == jnp.arange(expert_count)[None, :]).astype(jnp.int32)
    before = jnp.cumsum(onehot, axis=0) - onehot
    position = flat_routes * capacity + jnp.sum(before * onehot, axis=1)
    selector = jnp.arange(row_count)[:, None] == position[None, :]
    selector = jnp.where(selector, probs.reshape(-1)[None], 0).reshape(
        row_count, token_count, top_count
    )
    sent = jnp.dot(jnp.sum(selector, axis=2), grad_out, preferred_element_type=jnp.float32)
    rows = lax.all_to_all(
        sent.astype(jnp.bfloat16).reshape(expert_count, capacity, model_width),
        "expert",
        split_axis=0,
        concat_axis=0,
        tiled=True,
    ).reshape(row_count, model_width)
    up_value = saved_up.reshape(row_count, hidden_width).astype(jnp.float32)
    activation, gate_slope = silu_parts(
        saved_gate.reshape(row_count, hidden_width).astype(jnp.float32)
    )
    hidden = (activation * up_value).astype(jnp.bfloat16)
    grad_hidden = lax.dot_general(
        rows, w_down[0], (((1,), (1,)), ((), ())), preferred_element_type=jnp.float32
    )
    slot_grad = jnp.sum(hidden.astype(jnp.float32) * grad_hidden, axis=1)
    grad_up = (grad_hidden * activation).astype(jnp.bfloat16)
    grad_gate = (grad_hidden * up_value * gate_slope).astype(jnp.bfloat16)
    whole_panel = lax.dot_general(
        hidden, rows, (((0,), (0,)), ((), ())), preferred_element_type=jnp.float32
    )
    panel = lax.psum_scatter(whole_panel, "dp", scatter_dimension=0, tiled=True)
    returned = lax.all_to_all(
        slot_grad.reshape(expert_count, capacity), "expert", split_axis=0, concat_axis=0, tiled=True
    )
    route_grad = jnp.take(returned.reshape(-1), position, axis=0).reshape(token_count, top_count)
    return (
        grad_gate.reshape(saved_gate.shape),
        grad_up.reshape(saved_up.shape),
        panel[None],
        route_grad / probs.astype(jnp.float32),
    )


def shards(grad_out, probs, routes, saved_gate, saved_up, w_down):
    expert_count = lax.axis_size("expert")
    group_count = lax.axis_size("dp")
    capacity, hidden_width = saved_gate.shape[3:]
    aligned = (
        expert_count == 8
        and group_count == 4
        and capacity % 16 == 0
        and capacity <= LANES
        and hidden_width % (16 * group_count) == 0
        and routes.shape[0] == LANES
        and grad_out.shape[1] == sum(WIDTHS)
    )
    run = line_shards if aligned else plain_shards
    return run(grad_out, probs, routes, saved_gate, saved_up, w_down)


def solution(mesh):
    return jax.shard_map(
        shards,
        mesh=mesh,
        in_specs=(
            P(("dp", "expert"), None),
            P(("dp", "expert"), None),
            P(("dp", "expert"), None),
            P("dp", "expert", None, None, None),
            P("dp", "expert", None, None, None),
            P("expert", None, None),
        ),
        out_specs=(
            P("dp", "expert", None, None, None),
            P("dp", "expert", None, None, None),
            P("expert", "dp", None),
            P(("dp", "expert"), None),
        ),
        check_vma=False,
    )
```

```python
import functools

import jax
import jax.numpy as jnp
from jax import lax
from jax.experimental import pallas as pl
from jax.experimental.pallas import tpu as pltpu
from jax.sharding import PartitionSpec as P

LANES = 128
META = 16
WIDTHS = (1280, 768)
VMEM_LIMIT = 10 * 1024 * 1024
VMEM = pl.BlockSpec(memory_space=pltpu.VMEM)
ANY = pl.BlockSpec(memory_space=pl.ANY)


def params():
    return pltpu.CompilerParams(vmem_limit_bytes=VMEM_LIMIT)


def cost(flops, moved):
    return pl.CostEstimate(flops=flops // 64, bytes_accessed=moved // 64, transcendentals=0)


def silu_parts(gate_value):
    sigmoid = jax.nn.sigmoid(gate_value)
    return (gate_value * sigmoid, sigmoid * (1.0 + gate_value * (1.0 - sigmoid)))


def tokens_kernel(expert_count, routes_ref, probs_ref, meta_ref):
    top_count, token_count = routes_ref.shape
    names = [routes_ref[k : k + 1, :] for k in range(top_count)]
    experts = lax.broadcasted_iota(jnp.int32, (expert_count, token_count), 0)
    onehots = [(experts == name).astype(jnp.float32) for name in names]
    earlier = (
        lax.broadcasted_iota(jnp.int32, (token_count, token_count), 0)
        < lax.broadcasted_iota(jnp.int32, (token_count, token_count), 1)
    ).astype(jnp.bfloat16)
    before = jnp.dot(
        sum(onehots).astype(jnp.bfloat16), earlier, preferred_element_type=jnp.float32
    )
    lines = [name.astype(jnp.float32) for name in names]
    for onehot in onehots:
        lines.append(jnp.sum(before * onehot, axis=0, keepdims=True))
        before = before + onehot
    for k in range(top_count):
        lines.append(probs_ref[k : k + 1, :].astype(jnp.float32))
    lines.append(jnp.zeros((META - len(lines), token_count), jnp.float32))
    meta_ref[...] = jnp.concatenate(lines, axis=0).astype(jnp.bfloat16)


def token_lines(routes, probs, expert_count):
    token_count = routes.shape[1]
    return pl.pallas_call(
        functools.partial(tokens_kernel, expert_count),
        in_specs=[VMEM] * 2,
        out_shape=jax.ShapeDtypeStruct((META, token_count), jnp.bfloat16),
        compiler_params=params(),
        cost_estimate=cost(100 * token_count * token_count, 4 * token_count * META),
    )(routes, probs)


def far_offset():
    return 4 + 2 * lax.bitwise_and(lax.axis_index("expert"), 1)


def chosen_rows(meta, top_count, capacity):
    token_count = meta.shape[1]
    slots = lax.broadcasted_iota(jnp.int32, (capacity, token_count), 0).astype(jnp.float32)
    parts = []
    for offset in (0, 2, far_offset(), far_offset() + 1):
        target = lax.bitwise_xor(lax.axis_index("expert"), offset).astype(jnp.float32)
        part = jnp.zeros((capacity, token_count), jnp.float32)
        for k in range(top_count):
            name, slot, prob = (meta[k + top_count * i :][:1, :] for i in range(3))
            slot = jnp.where(name == target, slot, -1.0)
            part = part + jnp.where(slots == slot, prob, 0.0)
        parts.append(part)
    return jnp.concatenate(parts, axis=0).astype(jnp.bfloat16)


def dispatch_kernel(capacity, top_count, start, *refs):
    meta_refs, row_refs, (local_ref, near_ref, far_ref) = refs[:2], refs[2:4], refs[-3:]
    width = local_ref.shape[1]
    for source in range(2):
        rows = jnp.dot(
            chosen_rows(meta_refs[source][...].astype(jnp.float32), top_count, capacity),
            row_refs[source][:, start : start + width],
            preferred_element_type=jnp.float32,
        ).astype(jnp.bfloat16)
        places = [(local_ref, source), (near_ref, source), (far_ref, source), (far_ref, source + 2)]
        for step, (block_ref, place) in enumerate(places):
            block_ref[place * capacity : (place + 1) * capacity, :] = rows[
                step * capacity : (step + 1) * capacity, :
            ]


def dispatch(metas, rows, capacity, top_count, start, width, earlier):
    return pl.pallas_call(
        functools.partial(dispatch_kernel, capacity, top_count, start),
        in_specs=[VMEM] * 4 + [ANY] * len(earlier),
        out_shape=[
            jax.ShapeDtypeStruct((count * capacity, width), jnp.bfloat16) for count in (2, 2, 4)
        ],
        compiler_params=params(),
        cost_estimate=cost(16 * capacity * LANES * width, 16 * capacity * width),
    )(*metas, *rows, *earlier)


def hidden_kernel(gate_ref, up_ref, turned_ref, hidden_ref, up_scale_ref, gate_scale_ref):
    activation, gate_slope = silu_parts(gate_ref[...].astype(jnp.float32))
    up_value = up_ref[...].astype(jnp.float32)
    hidden = activation * up_value
    turned_ref[...] = hidden.T.astype(jnp.bfloat16)
    hidden_ref[...] = hidden.astype(jnp.bfloat16)
    up_scale_ref[...] = activation
    gate_scale_ref[...] = up_value * gate_slope


def hidden_parts(gate, up):
    row_count, hidden_width = gate.shape
    step = 2 * LANES
    block = pl.BlockSpec((row_count, step), lambda i: (0, i))
    return pl.pallas_call(
        hidden_kernel,
        grid=(hidden_width // step,),
        in_specs=[block] * 2,
        out_specs=[pl.BlockSpec((step, row_count), lambda i: (i, 0))] + [block] * 3,
        out_shape=[
            jax.ShapeDtypeStruct((hidden_width, row_count), jnp.bfloat16),
            jax.ShapeDtypeStruct((row_count, hidden_width), jnp.bfloat16),
            jax.ShapeDtypeStruct((row_count, hidden_width), jnp.float32),
            jax.ShapeDtypeStruct((row_count, hidden_width), jnp.float32),
        ],
        compiler_params=params(),
        cost_estimate=cost(20 * row_count * hidden_width, 16 * row_count * hidden_width),
    )(gate, up)


def panel_kernel(capacity, turned_ref, *refs):
    block_refs, (rows_ref, own_ref, later_ref, sent_ref) = refs[:4], refs[-4:]
    share = own_ref.shape[0]
    device = lax.axis_index("expert")
    far = far_offset()
    offsets = ((0, 1), (2, 3), (far, far + 1), (11 - far, 10 - far))
    for block, block_ref in enumerate(block_refs):
        first = 2 * capacity if block == 3 else 0
        for half in range(2):
            place = lax.bitwise_xor(device, offsets[block][half])
            row = pl.multiple_of(place * capacity, capacity)
            rows_ref[pl.ds(row, capacity), :] = block_ref[
                first + half * capacity : first + (half + 1) * capacity, :
            ]
    rows = rows_ref[...]

    def part(offset):
        owner = lax.bitwise_xor(lax.axis_index("dp"), offset)
        row = pl.multiple_of(owner * share, share)
        return jnp.dot(turned_ref[pl.ds(row, share), :], rows, preferred_element_type=jnp.float32)

    step = 1 + lax.bitwise_and(device, 1)
    sent_ref[:share, :] = part(step).astype(jnp.bfloat16)
    sent_ref[share:, :] = part(3).astype(jnp.bfloat16)
    later_ref[...] = part(3 - step)
    own_ref[...] = part(0)


def panel_parts(turned, blocks, capacity, earlier):
    hidden_width, row_count = turned.shape
    width = blocks[0].shape[1]
    share = hidden_width // 4
    return pl.pallas_call(
        functools.partial(panel_kernel, capacity),
        in_specs=[VMEM] * 5 + [ANY] * len(earlier),
        out_shape=[
            jax.ShapeDtypeStruct((row_count, width), jnp.bfloat16),
            jax.ShapeDtypeStruct((share, width), jnp.float32),
            jax.ShapeDtypeStruct((share, width), jnp.float32),
            jax.ShapeDtypeStruct((2 * share, width), jnp.bfloat16),
        ],
        compiler_params=params(),
        cost_estimate=cost(
            2 * hidden_width * row_count * width, 2 * hidden_width * (row_count + width)
        ),
    )(turned, *blocks, *earlier)


def halve_kernel(own_ref, later_ref, arrived_ref, *refs):
    sum_ref, sent_ref = refs[-2:]
    share = own_ref.shape[0]
    sent_ref[...] = (later_ref[...] + arrived_ref[share:, :].astype(jnp.float32)).astype(
        jnp.bfloat16
    )
    sum_ref[...] = own_ref[...] + arrived_ref[:share, :].astype(jnp.float32)


def halve(own, later, arrived, earlier):
    return pl.pallas_call(
        halve_kernel,
        in_specs=[VMEM] * 3 + [ANY] * len(earlier),
        out_shape=[
            jax.ShapeDtypeStruct(own.shape, jnp.float32),
            jax.ShapeDtypeStruct(own.shape, jnp.bfloat16),
        ],
        compiler_params=params(),
        cost_estimate=cost(4 * own.size, 18 * own.size),
    )(own, later, arrived, *earlier)


def total_kernel(count, *refs):
    own_refs, arrived_refs = refs[:count], refs[count : 2 * count]
    total_ref, *sum_refs, semaphores = refs[-2 - count :]
    copies = []
    start = 0
    for place, (own_ref, arrived_ref) in enumerate(zip(own_refs, arrived_refs)):
        width = own_ref.shape[1]
        sum_refs[place][...] = own_ref[...] + arrived_ref[...].astype(jnp.float32)
        copies.append(
            pltpu.make_async_copy(
                sum_refs[place], total_ref.at[:, start : start + width], semaphores.at[place]
            )
        )
        copies[-1].start()
        start += width
    for copy in copies:
        copy.wait()


def total(owns, arrived, earlier):
    share = owns[0].shape[0]
    size = share * sum(own.shape[1] for own in owns)
    return pl.pallas_call(
        functools.partial(total_kernel, len(owns)),
        in_specs=[VMEM] * (2 * len(owns)) + [ANY] * len(earlier),
        out_specs=ANY,
        out_shape=jax.ShapeDtypeStruct((share, size // share), jnp.float32),
        scratch_shapes=[pltpu.VMEM(own.shape, jnp.float32) for own in owns]
        + [pltpu.SemaphoreType.DMA((len(owns),))],
        compiler_params=params(),
        cost_estimate=cost(2 * size, 10 * size),
    )(*owns, *arrived, *earlier)


def rows_times_weight(start, rows_ref, weight_ref):
    return lax.dot_general(
        rows_ref[...],
        weight_ref[:, start : start + rows_ref.shape[1]],
        (((1,), (1,)), ((), ())),
        preferred_element_type=jnp.float32,
    )


def first_kernel(start, rows_ref, weight_ref, sum_ref):
    sum_ref[...] = rows_times_weight(start, rows_ref, weight_ref)


def middle_kernel(start, held_ref, rows_ref, weight_ref, sum_ref):
    sum_ref[...] = held_ref[...] + rows_times_weight(start, rows_ref, weight_ref)


def grad_hidden_step(held, rows, weight, start):
    row_count, width = rows.shape
    hidden_width = weight.shape[0]
    step = 2 * LANES
    block = pl.BlockSpec((row_count, step), lambda i: (0, i))
    specs = [
        pl.BlockSpec((row_count, width), lambda i: (0, 0)),
        pl.BlockSpec((step, weight.shape[1]), lambda i: (i, 0)),
    ]
    return pl.pallas_call(
        functools.partial(first_kernel if held is None else middle_kernel, start),
        grid=(hidden_width // step,),
        in_specs=specs if held is None else [block] + specs,
        out_specs=block,
        out_shape=jax.ShapeDtypeStruct((row_count, hidden_width), jnp.float32),
        compiler_params=params(),
        cost_estimate=cost(2 * row_count * hidden_width * width, 8 * row_count * hidden_width),
    )(*([rows, weight] if held is None else [held, rows, weight]))


def last_kernel(
    capacity,
    start,
    held_ref,
    rows_ref,
    weight_ref,
    hidden_ref,
    up_scale_ref,
    gate_scale_ref,
    grad_gate_ref,
    grad_up_ref,
    slot_ref,
    sum_ref,
):
    grid_place = pl.program_id(0)
    grad_hidden = held_ref[...] + rows_times_weight(start, rows_ref, weight_ref)
    grad_up_ref[...] = (grad_hidden * up_scale_ref[...]).astype(jnp.bfloat16)
    grad_gate_ref[...] = (grad_hidden * gate_scale_ref[...]).astype(jnp.bfloat16)
    product = hidden_ref[...].astype(jnp.float32) * grad_hidden
    folded = product[:, :LANES]
    for column in range(LANES, product.shape[1], LANES):
        folded = folded + product[:, column : column + LANES]

    @pl.when(grid_place == 0)
    def _():
        sum_ref[...] = folded

    @pl.when(grid_place > 0)
    def _():
        sum_ref[...] = sum_ref[...] + folded

    @pl.when(grid_place == pl.num_programs(0) - 1)
    def _():
        line = jnp.sum(sum_ref[...].T, axis=0, keepdims=True)
        slot_ref[...] = jnp.zeros_like(slot_ref)
        for source in range(slot_ref.shape[0]):
            slot_ref[source : source + 1, 0:capacity] = line[
                :, source * capacity : (source + 1) * capacity
            ]


def grad_hidden_last(held, rows, weight, start, hidden, up_scale, gate_scale, capacity):
    row_count, width = rows.shape
    hidden_width = weight.shape[0]
    step = 2 * LANES
    block = pl.BlockSpec((row_count, step), lambda i: (0, i))
    expert_count = row_count // capacity
    return pl.pallas_call(
        functools.partial(last_kernel, capacity, start),
        grid=(hidden_width // step,),
        in_specs=[
            block,
            pl.BlockSpec((row_count, width), lambda i: (0, 0)),
            pl.BlockSpec((step, weight.shape[1]), lambda i: (i, 0)),
            block,
            block,
            block,
        ],
        out_specs=[block, block, pl.BlockSpec((expert_count, LANES), lambda i: (0, 0))],
        out_shape=[jax.ShapeDtypeStruct((row_count, hidden_width), jnp.bfloat16)] * 2
        + [jax.ShapeDtypeStruct((expert_count, LANES), jnp.float32)],
        scratch_shapes=[pltpu.VMEM((row_count, LANES), jnp.float32)],
        compiler_params=params(),
        cost_estimate=cost(2 * row_count * hidden_width * width, 12 * row_count * hidden_width),
    )(held, rows, weight, hidden, up_scale, gate_scale)


def route_kernel(capacity, meta_ref, near_ref, far_ref, out_ref, table_ref):
    top_count, token_count = out_ref.shape
    expert_count = table_ref.shape[0]
    half = expert_count // 2
    for offset in range(expert_count):
        block_ref = near_ref if offset < half else far_ref
        row = offset % half * expert_count + lax.axis_index("expert")
        table_ref[offset : offset + 1, :] = block_ref[pl.ds(row, 1), :]
    table = table_ref[...].T
    meta = meta_ref[...].astype(jnp.float32)
    slots = lax.broadcasted_iota(jnp.int32, (capacity, token_count), 0).astype(jnp.float32)
    for k in range(top_count):
        name, slot, prob = (meta[k + top_count * i :][:1, :] for i in range(3))
        picked = jnp.zeros((capacity, token_count), jnp.float32)
        for offset in range(expert_count):
            expert = lax.bitwise_xor(lax.axis_index("expert"), offset).astype(jnp.float32)
            wanted = jnp.where(name == expert, slot, -1.0)
            picked = picked + jnp.where(
                slots == wanted, table[:capacity, offset : offset + 1], 0.0
            )
        out_ref[k : k + 1, :] = jnp.sum(picked, axis=0, keepdims=True) / prob


def route_back(meta, near, far, expert_count, top_count, capacity):
    token_count = meta.shape[1]
    return pl.pallas_call(
        functools.partial(route_kernel, capacity),
        in_specs=[VMEM] * 3,
        out_shape=jax.ShapeDtypeStruct((top_count, token_count), jnp.float32),
        scratch_shapes=[pltpu.VMEM((expert_count, LANES), jnp.float32)],
        compiler_params=params(),
        cost_estimate=cost(1000000, 100000),
    )(meta, near, far)


def after_kernel(*refs):
    pass


def after(value, *earlier):
    return pl.pallas_call(
        after_kernel,
        in_specs=[ANY] * (1 + len(earlier)),
        out_specs=ANY,
        out_shape=jax.ShapeDtypeStruct(value.shape, value.dtype),
        input_output_aliases={0: 0},
        compiler_params=params(),
        cost_estimate=cost(64, 64),
    )(value, *earlier)


def swap(value, offset):
    size = lax.axis_size("expert")
    return lax.ppermute(value, "expert", [(place, place ^ offset) for place in range(size)])


def swap_far(value):
    size = lax.axis_size("expert")
    pairs = [(place, place ^ (4 + 2 * (place & 1))) for place in range(size)]
    return lax.ppermute(value, "expert", pairs)


def swap_groups(value, later):
    groups, places = lax.axis_size("dp"), lax.axis_size("expert")
    pairs = []
    for group in range(groups):
        for place in range(places):
            other = group ^ (1 + (place & 1) ^ (3 if later else 0))
            pairs.append((group * places + place, other * places + place))
    return lax.ppermute(value, ("dp", "expert"), pairs)


def line_shards(grad_out, probs, routes, saved_gate, saved_up, w_down):
    expert_count = lax.axis_size("expert")
    capacity = saved_gate.shape[3]
    hidden_width = saved_gate.shape[4]
    token_count, model_width = grad_out.shape
    top_count = routes.shape[1]
    row_count = expert_count * capacity

    meta = token_lines(routes.T, probs.T, expert_count)
    metas = [meta, swap(meta, 1)]
    near_rows = [grad_out, swap(grad_out, 1)]
    weight = w_down[0]
    turned, hidden, up_scale, gate_scale = hidden_parts(
        saved_gate.reshape(row_count, hidden_width), saved_up.reshape(row_count, hidden_width)
    )
    held, start = None, 0
    all_rows, owns, arrived = [], [], []
    for chunk, width in enumerate(WIDTHS):
        earlier = all_rows[: max(0, chunk - 1)]
        local, near, far = dispatch(metas, near_rows, capacity, top_count, start, width, earlier)
        near = swap(near, 2)
        far = after(swap_far(far), near, *owns[-1:])
        blocks = [local, near, far, swap(far, 1)]
        earlier = [] if held is None else [held, *arrived]
        rows, own, later, half = panel_parts(turned, blocks, capacity, earlier)
        all_rows.append(rows)
        earlier = arrived[-1:]
        if chunk + 1 < len(WIDTHS):
            held = grad_hidden_step(held, rows, weight, start)
        else:
            grad_gate, grad_up, lines = grad_hidden_last(
                held, rows, weight, start, hidden, up_scale, gate_scale, capacity
            )
            for offset in (1, 2):
                lines = jnp.concatenate([lines, swap(lines, offset)], axis=0)
            earlier = earlier + [lines]
        own, half = halve(own, later, swap_groups(half, False), earlier)
        owns.append(own)
        arrived.append(swap_groups(half, True))
        start += width
    far_lines = swap(lines, 4)
    panel = total(owns, arrived, [far_lines])
    route_grad = route_back(meta, lines, far_lines, expert_count, top_count, capacity)
    return (
        grad_gate.reshape(saved_gate.shape),
        grad_up.reshape(saved_up.shape),
        panel[None],
        route_grad.T,
    )


def plain_shards(grad_out, probs, routes, saved_gate, saved_up, w_down):
    expert_count = lax.axis_size("expert")
    capacity = saved_gate.shape[3]
    hidden_width = saved_gate.shape[4]
    token_count, top_count = routes.shape
    model_width = grad_out.shape[1]
    row_count = expert_count * capacity
    flat_routes = routes.reshape(-1)
    onehot = (flat_routes[:, None] == jnp.arange(expert_count)[None, :]).astype(jnp.int32)
    before = jnp.cumsum(onehot, axis=0) - onehot
    position = flat_routes * capacity + jnp.sum(before * onehot, axis=1)
    selector = jnp.arange(row_count)[:, None] == position[None, :]
    selector = jnp.where(selector, probs.reshape(-1)[None], 0).reshape(
        row_count, token_count, top_count
    )
    sent = jnp.dot(jnp.sum(selector, axis=2), grad_out, preferred_element_type=jnp.float32)
    rows = lax.all_to_all(
        sent.astype(jnp.bfloat16).reshape(expert_count, capacity, model_width),
        "expert",
        split_axis=0,
        concat_axis=0,
        tiled=True,
    ).reshape(row_count, model_width)
    up_value = saved_up.reshape(row_count, hidden_width).astype(jnp.float32)
    activation, gate_slope = silu_parts(
        saved_gate.reshape(row_count, hidden_width).astype(jnp.float32)
    )
    hidden = (activation * up_value).astype(jnp.bfloat16)
    grad_hidden = lax.dot_general(
        rows, w_down[0], (((1,), (1,)), ((), ())), preferred_element_type=jnp.float32
    )
    slot_grad = jnp.sum(hidden.astype(jnp.float32) * grad_hidden, axis=1)
    grad_up = (grad_hidden * activation).astype(jnp.bfloat16)
    grad_gate = (grad_hidden * up_value * gate_slope).astype(jnp.bfloat16)
    whole_panel = lax.dot_general(
        hidden, rows, (((0,), (0,)), ((), ())), preferred_element_type=jnp.float32
    )
    panel = lax.psum_scatter(whole_panel, "dp", scatter_dimension=0, tiled=True)
    returned = lax.all_to_all(
        slot_grad.reshape(expert_count, capacity), "expert", split_axis=0, concat_axis=0, tiled=True
    )
    route_grad = jnp.take(returned.reshape(-1), position, axis=0).reshape(token_count, top_count)
    return (
        grad_gate.reshape(saved_gate.shape),
        grad_up.reshape(saved_up.shape),
        panel[None],
        route_grad / probs.astype(jnp.float32),
    )


def shards(grad_out, probs, routes, saved_gate, saved_up, w_down):
    expert_count = lax.axis_size("expert")
    group_count = lax.axis_size("dp")
    capacity, hidden_width = saved_gate.shape[3:]
    aligned = (
        expert_count == 8
        and group_count == 4
        and capacity % 16 == 0
        and capacity <= LANES
        and hidden_width % (16 * group_count) == 0
        and routes.shape[0] == LANES
        and grad_out.shape[1] == sum(WIDTHS)
    )
    run = line_shards if aligned else plain_shards
    return run(grad_out, probs, routes, saved_gate, saved_up, w_down)


def solution(mesh):
    return jax.shard_map(
        shards,
        mesh=mesh,
        in_specs=(
            P(("dp", "expert"), None),
            P(("dp", "expert"), None),
            P(("dp", "expert"), None),
            P("dp", "expert", None, None, None),
            P("dp", "expert", None, None, None),
            P("expert", None, None),
        ),
        out_specs=(
            P("dp", "expert", None, None, None),
            P("dp", "expert", None, None, None),
            P("expert", "dp", None),
            P(("dp", "expert"), None),
        ),
        check_vma=False,
    )
```

```python
import functools

import jax
import jax.numpy as jnp
from jax import lax
from jax.experimental import pallas as pl
from jax.experimental.pallas import tpu as pltpu
from jax.sharding import PartitionSpec as P

LANES = 128
META = 16
WIDTHS = (1280, 768)
VMEM_LIMIT = 10 * 1024 * 1024
VMEM = pl.BlockSpec(memory_space=pltpu.VMEM)
ANY = pl.BlockSpec(memory_space=pl.ANY)


def params():
    return pltpu.CompilerParams(vmem_limit_bytes=VMEM_LIMIT)


def cost(flops, moved):
    return pl.CostEstimate(flops=flops // 64, bytes_accessed=moved // 64, transcendentals=0)


def silu_parts(gate_value):
    sigmoid = jax.nn.sigmoid(gate_value)
    return (gate_value * sigmoid, sigmoid * (1.0 + gate_value * (1.0 - sigmoid)))


def tokens_kernel(expert_count, routes_ref, probs_ref, meta_ref):
    top_count, token_count = routes_ref.shape
    names = [routes_ref[k : k + 1, :] for k in range(top_count)]
    experts = lax.broadcasted_iota(jnp.int32, (expert_count, token_count), 0)
    onehots = [(experts == name).astype(jnp.float32) for name in names]
    earlier = (
        lax.broadcasted_iota(jnp.int32, (token_count, token_count), 0)
        < lax.broadcasted_iota(jnp.int32, (token_count, token_count), 1)
    ).astype(jnp.bfloat16)
    before = jnp.dot(
        sum(onehots).astype(jnp.bfloat16), earlier, preferred_element_type=jnp.float32
    )
    lines = [name.astype(jnp.float32) for name in names]
    for onehot in onehots:
        lines.append(jnp.sum(before * onehot, axis=0, keepdims=True))
        before = before + onehot
    for k in range(top_count):
        lines.append(probs_ref[k : k + 1, :].astype(jnp.float32))
    lines.append(jnp.zeros((META - len(lines), token_count), jnp.float32))
    meta_ref[...] = jnp.concatenate(lines, axis=0).astype(jnp.bfloat16)


def token_lines(routes, probs, expert_count):
    token_count = routes.shape[1]
    return pl.pallas_call(
        functools.partial(tokens_kernel, expert_count),
        in_specs=[VMEM] * 2,
        out_shape=jax.ShapeDtypeStruct((META, token_count), jnp.bfloat16),
        compiler_params=params(),
        cost_estimate=cost(100 * token_count * token_count, 4 * token_count * META),
    )(routes, probs)


def far_offset():
    return 4 + 2 * lax.bitwise_and(lax.axis_index("expert"), 1)


def chosen_rows(meta, top_count, capacity, offsets):
    token_count = meta.shape[1]
    slots = lax.broadcasted_iota(jnp.int32, (capacity, token_count), 0).astype(jnp.float32)
    parts = []
    for offset in offsets:
        target = lax.bitwise_xor(lax.axis_index("expert"), offset).astype(jnp.float32)
        part = jnp.zeros((capacity, token_count), jnp.float32)
        for k in range(top_count):
            name, slot, prob = (meta[k + top_count * i :][:1, :] for i in range(3))
            slot = jnp.where(name == target, slot, -1.0)
            part = part + jnp.where(slots == slot, prob, 0.0)
        parts.append(part)
    return jnp.concatenate(parts, axis=0).astype(jnp.bfloat16)


def dispatch_kernel(capacity, top_count, start, far, *refs):
    meta_refs, row_refs, block_refs = refs[:2], refs[2:4], refs[4:]
    if far:
        offsets = (far_offset(), far_offset() + 1)
        block_refs = refs[-1:] * 2
    else:
        offsets = (0, 2)
        block_refs = refs[-2:]
    width = block_refs[0].shape[1]
    for source in range(2):
        meta = meta_refs[source][...].astype(jnp.float32)
        rows = jnp.dot(
            chosen_rows(meta, top_count, capacity, offsets),
            row_refs[source][:, start : start + width],
            preferred_element_type=jnp.float32,
        ).astype(jnp.bfloat16)
        for step, block_ref in enumerate(block_refs):
            place = source + (2 * step if far else 0)
            block_ref[place * capacity : (place + 1) * capacity, :] = rows[
                step * capacity : (step + 1) * capacity, :
            ]


def dispatch(metas, rows, capacity, top_count, start, width, far):
    counts = (4,) if far else (2, 2)
    return pl.pallas_call(
        functools.partial(dispatch_kernel, capacity, top_count, start, far),
        in_specs=[VMEM] * 4,
        out_shape=[
            jax.ShapeDtypeStruct((count * capacity, width), jnp.bfloat16) for count in counts
        ],
        compiler_params=params(),
        cost_estimate=cost(8 * capacity * LANES * width, 8 * capacity * width),
    )(*metas, *rows)


def hidden_kernel(gate_ref, up_ref, turned_ref, hidden_ref, up_scale_ref, gate_scale_ref):
    activation, gate_slope = silu_parts(gate_ref[...].astype(jnp.float32))
    up_value = up_ref[...].astype(jnp.float32)
    hidden = activation * up_value
    turned_ref[...] = hidden.T.astype(jnp.bfloat16)
    hidden_ref[...] = hidden.astype(jnp.bfloat16)
    up_scale_ref[...] = activation
    gate_scale_ref[...] = up_value * gate_slope


def hidden_parts(gate, up):
    row_count, hidden_width = gate.shape
    step = 2 * LANES
    block = pl.BlockSpec((row_count, step), lambda i: (0, i))
    return pl.pallas_call(
        hidden_kernel,
        grid=(hidden_width // step,),
        in_specs=[block] * 2,
        out_specs=[pl.BlockSpec((step, row_count), lambda i: (i, 0))] + [block] * 3,
        out_shape=[
            jax.ShapeDtypeStruct((hidden_width, row_count), jnp.bfloat16),
            jax.ShapeDtypeStruct((row_count, hidden_width), jnp.bfloat16),
            jax.ShapeDtypeStruct((row_count, hidden_width), jnp.float32),
            jax.ShapeDtypeStruct((row_count, hidden_width), jnp.float32),
        ],
        compiler_params=params(),
        cost_estimate=cost(20 * row_count * hidden_width, 16 * row_count * hidden_width),
    )(gate, up)


def panel_kernel(capacity, start, turned_ref, *refs):
    block_refs, (rows_ref, own_ref, later_ref, sent_ref) = refs[:4], refs[-4:]
    share, width = own_ref.shape
    device = lax.axis_index("expert")
    far = far_offset()
    offsets = ((0, 1), (2, 3), (far, far + 1), (11 - far, 10 - far))
    for block, block_ref in enumerate(block_refs):
        first = 2 * capacity if block == 3 else 0
        column = start if block < 2 else 0
        for half in range(2):
            place = lax.bitwise_xor(device, offsets[block][half])
            row = pl.multiple_of(place * capacity, capacity)
            rows_ref[pl.ds(row, capacity), :] = block_ref[
                first + half * capacity : first + (half + 1) * capacity, column : column + width
            ]
    rows = rows_ref[...]

    def part(offset):
        owner = lax.bitwise_xor(lax.axis_index("dp"), offset)
        row = pl.multiple_of(owner * share, share)
        return jnp.dot(turned_ref[pl.ds(row, share), :], rows, preferred_element_type=jnp.float32)

    step = 1 + lax.bitwise_and(device, 1)
    sent_ref[:share, :] = part(step).astype(jnp.bfloat16)
    sent_ref[share:, :] = part(3).astype(jnp.bfloat16)
    later_ref[...] = part(3 - step)
    own_ref[...] = part(0)


def panel_parts(turned, blocks, capacity, start, earlier):
    hidden_width, row_count = turned.shape
    width = blocks[-1].shape[1]
    share = hidden_width // 4
    return pl.pallas_call(
        functools.partial(panel_kernel, capacity, start),
        in_specs=[VMEM] * 5 + [ANY] * len(earlier),
        out_shape=[
            jax.ShapeDtypeStruct((row_count, width), jnp.bfloat16),
            jax.ShapeDtypeStruct((share, width), jnp.float32),
            jax.ShapeDtypeStruct((share, width), jnp.float32),
            jax.ShapeDtypeStruct((2 * share, width), jnp.bfloat16),
        ],
        compiler_params=params(),
        cost_estimate=cost(
            2 * hidden_width * row_count * width, 2 * hidden_width * (row_count + width)
        ),
    )(turned, *blocks, *earlier)


def halve_kernel(own_ref, later_ref, arrived_ref, *refs):
    sum_ref, sent_ref = refs[-2:]
    share = own_ref.shape[0]
    sent_ref[...] = (later_ref[...] + arrived_ref[share:, :].astype(jnp.float32)).astype(
        jnp.bfloat16
    )
    sum_ref[...] = own_ref[...] + arrived_ref[:share, :].astype(jnp.float32)


def halve(own, later, arrived, earlier):
    return pl.pallas_call(
        halve_kernel,
        in_specs=[VMEM] * 3 + [ANY] * len(earlier),
        out_shape=[
            jax.ShapeDtypeStruct(own.shape, jnp.float32),
            jax.ShapeDtypeStruct(own.shape, jnp.bfloat16),
        ],
        compiler_params=params(),
        cost_estimate=cost(4 * own.size, 18 * own.size),
    )(own, later, arrived, *earlier)


def total_kernel(count, *refs):
    own_refs, arrived_refs = refs[:count], refs[count : 2 * count]
    total_ref, *sum_refs, semaphores = refs[-2 - count :]
    copies = []
    start = 0
    for place, (own_ref, arrived_ref) in enumerate(zip(own_refs, arrived_refs)):
        width = own_ref.shape[1]
        sum_refs[place][...] = own_ref[...] + arrived_ref[...].astype(jnp.float32)
        copies.append(
            pltpu.make_async_copy(
                sum_refs[place], total_ref.at[:, start : start + width], semaphores.at[place]
            )
        )
        copies[-1].start()
        start += width
    for copy in copies:
        copy.wait()


def total(owns, arrived, earlier):
    share = owns[0].shape[0]
    size = share * sum(own.shape[1] for own in owns)
    return pl.pallas_call(
        functools.partial(total_kernel, len(owns)),
        in_specs=[VMEM] * (2 * len(owns)) + [ANY] * len(earlier),
        out_specs=ANY,
        out_shape=jax.ShapeDtypeStruct((share, size // share), jnp.float32),
        scratch_shapes=[pltpu.VMEM(own.shape, jnp.float32) for own in owns]
        + [pltpu.SemaphoreType.DMA((len(owns),))],
        compiler_params=params(),
        cost_estimate=cost(2 * size, 10 * size),
    )(*owns, *arrived, *earlier)


def rows_times_weight(start, rows_ref, weight_ref):
    return lax.dot_general(
        rows_ref[...],
        weight_ref[:, start : start + rows_ref.shape[1]],
        (((1,), (1,)), ((), ())),
        preferred_element_type=jnp.float32,
    )


def first_kernel(start, rows_ref, weight_ref, sum_ref):
    sum_ref[...] = rows_times_weight(start, rows_ref, weight_ref)


def middle_kernel(start, held_ref, rows_ref, weight_ref, sum_ref):
    sum_ref[...] = held_ref[...] + rows_times_weight(start, rows_ref, weight_ref)


def grad_hidden_step(held, rows, weight, start):
    row_count, width = rows.shape
    hidden_width = weight.shape[0]
    step = 2 * LANES
    block = pl.BlockSpec((row_count, step), lambda i: (0, i))
    specs = [
        pl.BlockSpec((row_count, width), lambda i: (0, 0)),
        pl.BlockSpec((step, weight.shape[1]), lambda i: (i, 0)),
    ]
    return pl.pallas_call(
        functools.partial(first_kernel if held is None else middle_kernel, start),
        grid=(hidden_width // step,),
        in_specs=specs if held is None else [block] + specs,
        out_specs=block,
        out_shape=jax.ShapeDtypeStruct((row_count, hidden_width), jnp.float32),
        compiler_params=params(),
        cost_estimate=cost(2 * row_count * hidden_width * width, 8 * row_count * hidden_width),
    )(*([rows, weight] if held is None else [held, rows, weight]))


def last_kernel(
    capacity, start, held_ref, rows_ref, weight_ref, hidden_ref, grad_ref, slot_ref, sum_ref
):
    grid_place = pl.program_id(0)
    grad_hidden = held_ref[...] + rows_times_weight(start, rows_ref, weight_ref)
    grad_ref[...] = grad_hidden
    product = hidden_ref[...].astype(jnp.float32) * grad_hidden
    folded = product[:, :LANES]
    for column in range(LANES, product.shape[1], LANES):
        folded = folded + product[:, column : column + LANES]

    @pl.when(grid_place == 0)
    def _():
        sum_ref[...] = folded

    @pl.when(grid_place > 0)
    def _():
        sum_ref[...] = sum_ref[...] + folded

    @pl.when(grid_place == pl.num_programs(0) - 1)
    def _():
        line = jnp.sum(sum_ref[...].T, axis=0, keepdims=True)
        slot_ref[...] = jnp.zeros_like(slot_ref)
        for source in range(slot_ref.shape[0]):
            slot_ref[source : source + 1, 0:capacity] = line[
                :, source * capacity : (source + 1) * capacity
            ]


def grad_hidden_last(held, rows, weight, start, hidden, capacity):
    row_count, width = rows.shape
    hidden_width = weight.shape[0]
    step = 2 * LANES
    block = pl.BlockSpec((row_count, step), lambda i: (0, i))
    expert_count = row_count // capacity
    return pl.pallas_call(
        functools.partial(last_kernel, capacity, start),
        grid=(hidden_width // step,),
        in_specs=[
            block,
            pl.BlockSpec((row_count, width), lambda i: (0, 0)),
            pl.BlockSpec((step, weight.shape[1]), lambda i: (i, 0)),
            block,
        ],
        out_specs=[block, pl.BlockSpec((expert_count, LANES), lambda i: (0, 0))],
        out_shape=[
            jax.ShapeDtypeStruct((row_count, hidden_width), jnp.float32),
            jax.ShapeDtypeStruct((expert_count, LANES), jnp.float32),
        ],
        scratch_shapes=[pltpu.VMEM((row_count, LANES), jnp.float32)],
        compiler_params=params(),
        cost_estimate=cost(2 * row_count * hidden_width * width, 12 * row_count * hidden_width),
    )(held, rows, weight, hidden)


def scale_kernel(grad_ref, up_scale_ref, gate_scale_ref, *refs):
    grad_gate_ref, grad_up_ref = refs[-2:]
    grad_up_ref[...] = (grad_ref[...] * up_scale_ref[...]).astype(jnp.bfloat16)
    grad_gate_ref[...] = (grad_ref[...] * gate_scale_ref[...]).astype(jnp.bfloat16)


def scaled_grads(grad_hidden, up_scale, gate_scale, earlier):
    row_count, hidden_width = grad_hidden.shape
    step = 2 * LANES
    block = pl.BlockSpec((row_count, step), lambda i: (0, i))
    return pl.pallas_call(
        scale_kernel,
        grid=(hidden_width // step,),
        in_specs=[block] * 3 + [ANY] * len(earlier),
        out_specs=[block, block],
        out_shape=[jax.ShapeDtypeStruct((row_count, hidden_width), jnp.bfloat16)] * 2,
        compiler_params=params(),
        cost_estimate=cost(2 * row_count * hidden_width, 16 * row_count * hidden_width),
    )(grad_hidden, up_scale, gate_scale, *earlier)


def route_kernel(capacity, meta_ref, near_ref, far_ref, out_ref, table_ref):
    top_count, token_count = out_ref.shape
    expert_count = table_ref.shape[0]
    half = expert_count // 2
    for offset in range(expert_count):
        block_ref = near_ref if offset < half else far_ref
        row = offset % half * expert_count + lax.axis_index("expert")
        table_ref[offset : offset + 1, :] = block_ref[pl.ds(row, 1), :]
    table = table_ref[...].T
    meta = meta_ref[...].astype(jnp.float32)
    slots = lax.broadcasted_iota(jnp.int32, (capacity, token_count), 0).astype(jnp.float32)
    for k in range(top_count):
        name, slot, prob = (meta[k + top_count * i :][:1, :] for i in range(3))
        picked = jnp.zeros((capacity, token_count), jnp.float32)
        for offset in range(expert_count):
            expert = lax.bitwise_xor(lax.axis_index("expert"), offset).astype(jnp.float32)
            wanted = jnp.where(name == expert, slot, -1.0)
            picked = picked + jnp.where(
                slots == wanted, table[:capacity, offset : offset + 1], 0.0
            )
        out_ref[k : k + 1, :] = jnp.sum(picked, axis=0, keepdims=True) / prob


def route_back(meta, near, far, expert_count, top_count, capacity):
    token_count = meta.shape[1]
    return pl.pallas_call(
        functools.partial(route_kernel, capacity),
        in_specs=[VMEM] * 3,
        out_shape=jax.ShapeDtypeStruct((top_count, token_count), jnp.float32),
        scratch_shapes=[pltpu.VMEM((expert_count, LANES), jnp.float32)],
        compiler_params=params(),
        cost_estimate=cost(1000000, 100000),
    )(meta, near, far)


def after_kernel(*refs):
    pass


def after(value, *earlier):
    return pl.pallas_call(
        after_kernel,
        in_specs=[ANY] * (1 + len(earlier)),
        out_specs=ANY,
        out_shape=jax.ShapeDtypeStruct(value.shape, value.dtype),
        input_output_aliases={0: 0},
        compiler_params=params(),
        cost_estimate=cost(64, 64),
    )(value, *earlier)


def swap(value, offset):
    size = lax.axis_size("expert")
    return lax.ppermute(value, "expert", [(place, place ^ offset) for place in range(size)])


def swap_far(value):
    size = lax.axis_size("expert")
    pairs = [(place, place ^ (4 + 2 * (place & 1))) for place in range(size)]
    return lax.ppermute(value, "expert", pairs)


def swap_groups(value, later):
    groups, places = lax.axis_size("dp"), lax.axis_size("expert")
    pairs = []
    for group in range(groups):
        for place in range(places):
            other = group ^ (1 + (place & 1) ^ (3 if later else 0))
            pairs.append((group * places + place, other * places + place))
    return lax.ppermute(value, ("dp", "expert"), pairs)


def line_shards(grad_out, probs, routes, saved_gate, saved_up, w_down):
    expert_count = lax.axis_size("expert")
    capacity = saved_gate.shape[3]
    hidden_width = saved_gate.shape[4]
    token_count, model_width = grad_out.shape
    top_count = routes.shape[1]
    row_count = expert_count * capacity

    meta = token_lines(routes.T, probs.T, expert_count)
    metas = [meta, swap(meta, 1)]
    near_rows = [grad_out, swap(grad_out, 1)]
    weight = w_down[0]
    turned, hidden, up_scale, gate_scale = hidden_parts(
        saved_gate.reshape(row_count, hidden_width), saved_up.reshape(row_count, hidden_width)
    )
    held, start = None, 0
    owns, arrived = [], []
    for chunk, width in enumerate(WIDTHS):
        far = swap_far(dispatch(metas, near_rows, capacity, top_count, start, width, True)[0])
        if chunk == 0:
            local, near = dispatch(metas, near_rows, capacity, top_count, 0, model_width, False)
            near = swap(near, 2)
        far = after(far, near, *owns)
        earlier = [] if held is None else [held]
        rows, own, later, half = panel_parts(
            turned, [local, near, far, swap(far, 1)], capacity, start, earlier
        )
        earlier = arrived[-1:]
        if chunk + 1 < len(WIDTHS):
            held = grad_hidden_step(held, rows, weight, start)
        else:
            grad_hidden, lines = grad_hidden_last(held, rows, weight, start, hidden, capacity)
            lines = jnp.concatenate([lines, swap(lines, 1)], axis=0)
            grad_gate, grad_up = scaled_grads(grad_hidden, up_scale, gate_scale, [lines])
            lines = jnp.concatenate([lines, swap(lines, 2)], axis=0)
            earlier = earlier + [lines]
        own, half = halve(own, later, swap_groups(half, False), earlier)
        owns.append(own)
        arrived.append(swap_groups(half, True))
        start += width
    far_lines = swap(lines, 4)
    panel = total(owns, arrived, [far_lines])
    route_grad = route_back(meta, lines, far_lines, expert_count, top_count, capacity)
    return (
        grad_gate.reshape(saved_gate.shape),
        grad_up.reshape(saved_up.shape),
        panel[None],
        route_grad.T,
    )


def plain_shards(grad_out, probs, routes, saved_gate, saved_up, w_down):
    expert_count = lax.axis_size("expert")
    capacity = saved_gate.shape[3]
    hidden_width = saved_gate.shape[4]
    token_count, top_count = routes.shape
    model_width = grad_out.shape[1]
    row_count = expert_count * capacity
    flat_routes = routes.reshape(-1)
    onehot = (flat_routes[:, None] == jnp.arange(expert_count)[None, :]).astype(jnp.int32)
    before = jnp.cumsum(onehot, axis=0) - onehot
    position = flat_routes * capacity + jnp.sum(before * onehot, axis=1)
    selector = jnp.arange(row_count)[:, None] == position[None, :]
    selector = jnp.where(selector, probs.reshape(-1)[None], 0).reshape(
        row_count, token_count, top_count
    )
    sent = jnp.dot(jnp.sum(selector, axis=2), grad_out, preferred_element_type=jnp.float32)
    rows = lax.all_to_all(
        sent.astype(jnp.bfloat16).reshape(expert_count, capacity, model_width),
        "expert",
        split_axis=0,
        concat_axis=0,
        tiled=True,
    ).reshape(row_count, model_width)
    up_value = saved_up.reshape(row_count, hidden_width).astype(jnp.float32)
    activation, gate_slope = silu_parts(
        saved_gate.reshape(row_count, hidden_width).astype(jnp.float32)
    )
    hidden = (activation * up_value).astype(jnp.bfloat16)
    grad_hidden = lax.dot_general(
        rows, w_down[0], (((1,), (1,)), ((), ())), preferred_element_type=jnp.float32
    )
    slot_grad = jnp.sum(hidden.astype(jnp.float32) * grad_hidden, axis=1)
    grad_up = (grad_hidden * activation).astype(jnp.bfloat16)
    grad_gate = (grad_hidden * up_value * gate_slope).astype(jnp.bfloat16)
    whole_panel = lax.dot_general(
        hidden, rows, (((0,), (0,)), ((), ())), preferred_element_type=jnp.float32
    )
    panel = lax.psum_scatter(whole_panel, "dp", scatter_dimension=0, tiled=True)
    returned = lax.all_to_all(
        slot_grad.reshape(expert_count, capacity), "expert", split_axis=0, concat_axis=0, tiled=True
    )
    route_grad = jnp.take(returned.reshape(-1), position, axis=0).reshape(token_count, top_count)
    return (
        grad_gate.reshape(saved_gate.shape),
        grad_up.reshape(saved_up.shape),
        panel[None],
        route_grad / probs.astype(jnp.float32),
    )


def shards(grad_out, probs, routes, saved_gate, saved_up, w_down):
    expert_count = lax.axis_size("expert")
    group_count = lax.axis_size("dp")
    capacity, hidden_width = saved_gate.shape[3:]
    aligned = (
        expert_count == 8
        and group_count == 4
        and capacity % 16 == 0
        and capacity <= LANES
        and hidden_width % (16 * group_count) == 0
        and routes.shape[0] == LANES
        and grad_out.shape[1] == sum(WIDTHS)
    )
    run = line_shards if aligned else plain_shards
    return run(grad_out, probs, routes, saved_gate, saved_up, w_down)


def solution(mesh):
    return jax.shard_map(
        shards,
        mesh=mesh,
        in_specs=(
            P(("dp", "expert"), None),
            P(("dp", "expert"), None),
            P(("dp", "expert"), None),
            P("dp", "expert", None, None, None),
            P("dp", "expert", None, None, None),
            P("expert", None, None),
        ),
        out_specs=(
            P("dp", "expert", None, None, None),
            P("dp", "expert", None, None, None),
            P("expert", "dp", None),
            P(("dp", "expert"), None),
        ),
        check_vma=False,
    )
```

```python
import functools

import jax
import jax.numpy as jnp
from jax import lax
from jax.experimental import pallas as pl
from jax.experimental.pallas import tpu as pltpu
from jax.sharding import PartitionSpec as P

LANES = 128
META = 16
WIDTHS = (1152, 896)
VMEM_LIMIT = 10 * 1024 * 1024
VMEM = pl.BlockSpec(memory_space=pltpu.VMEM)
ANY = pl.BlockSpec(memory_space=pl.ANY)


def params():
    return pltpu.CompilerParams(vmem_limit_bytes=VMEM_LIMIT)


def cost(flops, moved):
    return pl.CostEstimate(flops=flops // 64, bytes_accessed=moved // 64, transcendentals=0)


def silu_parts(gate_value):
    sigmoid = jax.nn.sigmoid(gate_value)
    return (gate_value * sigmoid, sigmoid * (1.0 + gate_value * (1.0 - sigmoid)))


def tokens_kernel(expert_count, routes_ref, probs_ref, meta_ref):
    top_count, token_count = routes_ref.shape
    names = [routes_ref[k : k + 1, :] for k in range(top_count)]
    experts = lax.broadcasted_iota(jnp.int32, (expert_count, token_count), 0)
    onehots = [(experts == name).astype(jnp.float32) for name in names]
    earlier = (
        lax.broadcasted_iota(jnp.int32, (token_count, token_count), 0)
        < lax.broadcasted_iota(jnp.int32, (token_count, token_count), 1)
    ).astype(jnp.bfloat16)
    before = jnp.dot(
        sum(onehots).astype(jnp.bfloat16), earlier, preferred_element_type=jnp.float32
    )
    lines = [name.astype(jnp.float32) for name in names]
    for onehot in onehots:
        lines.append(jnp.sum(before * onehot, axis=0, keepdims=True))
        before = before + onehot
    for k in range(top_count):
        lines.append(probs_ref[k : k + 1, :].astype(jnp.float32))
    lines.append(jnp.zeros((META - len(lines), token_count), jnp.float32))
    meta_ref[...] = jnp.concatenate(lines, axis=0).astype(jnp.bfloat16)


def token_lines(routes, probs, expert_count):
    token_count = routes.shape[1]
    return pl.pallas_call(
        functools.partial(tokens_kernel, expert_count),
        in_specs=[VMEM] * 2,
        out_shape=jax.ShapeDtypeStruct((META, token_count), jnp.bfloat16),
        compiler_params=params(),
        cost_estimate=cost(100 * token_count * token_count, 4 * token_count * META),
    )(routes, probs)


def far_offset():
    return 4 + 2 * lax.bitwise_and(lax.axis_index("expert"), 1)


def chosen_rows(meta, top_count, capacity, offsets):
    token_count = meta.shape[1]
    slots = lax.broadcasted_iota(jnp.int32, (capacity, token_count), 0).astype(jnp.float32)
    parts = []
    for offset in offsets:
        target = lax.bitwise_xor(lax.axis_index("expert"), offset).astype(jnp.float32)
        part = jnp.zeros((capacity, token_count), jnp.float32)
        for k in range(top_count):
            name, slot, prob = (meta[k + top_count * i :][:1, :] for i in range(3))
            slot = jnp.where(name == target, slot, -1.0)
            part = part + jnp.where(slots == slot, prob, 0.0)
        parts.append(part)
    return jnp.concatenate(parts, axis=0).astype(jnp.bfloat16)


def dispatch_kernel(capacity, top_count, start, far, *refs):
    meta_refs, row_refs, block_refs = refs[:2], refs[2:4], refs[4:]
    if far:
        offsets = (far_offset(), far_offset() + 1)
        block_refs = refs[-1:] * 2
    else:
        offsets = (0, 2)
        block_refs = refs[-2:]
    width = block_refs[0].shape[1]
    for source in range(2):
        meta = meta_refs[source][...].astype(jnp.float32)
        rows = jnp.dot(
            chosen_rows(meta, top_count, capacity, offsets),
            row_refs[source][:, start : start + width],
            preferred_element_type=jnp.float32,
        ).astype(jnp.bfloat16)
        for step, block_ref in enumerate(block_refs):
            place = source + (2 * step if far else 0)
            block_ref[place * capacity : (place + 1) * capacity, :] = rows[
                step * capacity : (step + 1) * capacity, :
            ]


def dispatch(metas, rows, capacity, top_count, start, width, far):
    counts = (4,) if far else (2, 2)
    return pl.pallas_call(
        functools.partial(dispatch_kernel, capacity, top_count, start, far),
        in_specs=[VMEM] * 4,
        out_shape=[
            jax.ShapeDtypeStruct((count * capacity, width), jnp.bfloat16) for count in counts
        ],
        compiler_params=params(),
        cost_estimate=cost(8 * capacity * LANES * width, 8 * capacity * width),
    )(*metas, *rows)


def hidden_kernel(gate_ref, up_ref, turned_ref, hidden_ref, up_scale_ref, gate_scale_ref):
    activation, gate_slope = silu_parts(gate_ref[...].astype(jnp.float32))
    up_value = up_ref[...].astype(jnp.float32)
    hidden = activation * up_value
    turned_ref[...] = hidden.T.astype(jnp.bfloat16)
    hidden_ref[...] = hidden.astype(jnp.bfloat16)
    up_scale_ref[...] = activation
    gate_scale_ref[...] = up_value * gate_slope


def hidden_parts(gate, up):
    row_count, hidden_width = gate.shape
    step = 2 * LANES
    block = pl.BlockSpec((row_count, step), lambda i: (0, i))
    return pl.pallas_call(
        hidden_kernel,
        grid=(hidden_width // step,),
        in_specs=[block] * 2,
        out_specs=[pl.BlockSpec((step, row_count), lambda i: (i, 0))] + [block] * 3,
        out_shape=[
            jax.ShapeDtypeStruct((hidden_width, row_count), jnp.bfloat16),
            jax.ShapeDtypeStruct((row_count, hidden_width), jnp.bfloat16),
            jax.ShapeDtypeStruct((row_count, hidden_width), jnp.float32),
            jax.ShapeDtypeStruct((row_count, hidden_width), jnp.float32),
        ],
        compiler_params=params(),
        cost_estimate=cost(20 * row_count * hidden_width, 16 * row_count * hidden_width),
    )(gate, up)


def panel_kernel(capacity, start, turned_ref, *refs):
    block_refs, (rows_ref, own_ref, later_ref, sent_ref) = refs[:4], refs[-4:]
    share, width = own_ref.shape
    device = lax.axis_index("expert")
    far = far_offset()
    offsets = ((0, 1), (2, 3), (far, far + 1), (11 - far, 10 - far))
    for block, block_ref in enumerate(block_refs):
        first = 2 * capacity if block == 3 else 0
        column = start if block < 2 else 0
        for half in range(2):
            place = lax.bitwise_xor(device, offsets[block][half])
            row = pl.multiple_of(place * capacity, capacity)
            rows_ref[pl.ds(row, capacity), :] = block_ref[
                first + half * capacity : first + (half + 1) * capacity, column : column + width
            ]
    rows = rows_ref[...]

    def part(offset):
        owner = lax.bitwise_xor(lax.axis_index("dp"), offset)
        row = pl.multiple_of(owner * share, share)
        return jnp.dot(turned_ref[pl.ds(row, share), :], rows, preferred_element_type=jnp.float32)

    step = 1 + lax.bitwise_and(device, 1)
    sent_ref[:share, :] = part(step).astype(jnp.bfloat16)
    sent_ref[share:, :] = part(3).astype(jnp.bfloat16)
    later_ref[...] = part(3 - step)
    own_ref[...] = part(0)


def panel_parts(turned, blocks, capacity, start, earlier):
    hidden_width, row_count = turned.shape
    width = blocks[-1].shape[1]
    share = hidden_width // 4
    return pl.pallas_call(
        functools.partial(panel_kernel, capacity, start),
        in_specs=[VMEM] * 5 + [ANY] * len(earlier),
        out_shape=[
            jax.ShapeDtypeStruct((row_count, width), jnp.bfloat16),
            jax.ShapeDtypeStruct((share, width), jnp.float32),
            jax.ShapeDtypeStruct((share, width), jnp.float32),
            jax.ShapeDtypeStruct((2 * share, width), jnp.bfloat16),
        ],
        compiler_params=params(),
        cost_estimate=cost(
            2 * hidden_width * row_count * width, 2 * hidden_width * (row_count + width)
        ),
    )(turned, *blocks, *earlier)


def halve_kernel(own_ref, later_ref, arrived_ref, *refs):
    sum_ref, sent_ref = refs[-2:]
    share = own_ref.shape[0]
    sent_ref[...] = (later_ref[...] + arrived_ref[share:, :].astype(jnp.float32)).astype(
        jnp.bfloat16
    )
    sum_ref[...] = own_ref[...] + arrived_ref[:share, :].astype(jnp.float32)


def halve(own, later, arrived, earlier):
    return pl.pallas_call(
        halve_kernel,
        in_specs=[VMEM] * 3 + [ANY] * len(earlier),
        out_shape=[
            jax.ShapeDtypeStruct(own.shape, jnp.float32),
            jax.ShapeDtypeStruct(own.shape, jnp.bfloat16),
        ],
        compiler_params=params(),
        cost_estimate=cost(4 * own.size, 18 * own.size),
    )(own, later, arrived, *earlier)


def total_kernel(count, *refs):
    own_refs, arrived_refs = refs[:count], refs[count : 2 * count]
    total_ref, *sum_refs, semaphores = refs[-2 - count :]
    copies = []
    start = 0
    for place, (own_ref, arrived_ref) in enumerate(zip(own_refs, arrived_refs)):
        width = own_ref.shape[1]
        sum_refs[place][...] = own_ref[...] + arrived_ref[...].astype(jnp.float32)
        copies.append(
            pltpu.make_async_copy(
                sum_refs[place], total_ref.at[:, start : start + width], semaphores.at[place]
            )
        )
        copies[-1].start()
        start += width
    for copy in copies:
        copy.wait()


def total(owns, arrived, earlier):
    share = owns[0].shape[0]
    size = share * sum(own.shape[1] for own in owns)
    return pl.pallas_call(
        functools.partial(total_kernel, len(owns)),
        in_specs=[VMEM] * (2 * len(owns)) + [ANY] * len(earlier),
        out_specs=ANY,
        out_shape=jax.ShapeDtypeStruct((share, size // share), jnp.float32),
        scratch_shapes=[pltpu.VMEM(own.shape, jnp.float32) for own in owns]
        + [pltpu.SemaphoreType.DMA((len(owns),))],
        compiler_params=params(),
        cost_estimate=cost(2 * size, 10 * size),
    )(*owns, *arrived, *earlier)


def rows_times_weight(start, rows_ref, weight_ref):
    return lax.dot_general(
        rows_ref[...],
        weight_ref[:, start : start + rows_ref.shape[1]],
        (((1,), (1,)), ((), ())),
        preferred_element_type=jnp.float32,
    )


def first_kernel(start, rows_ref, weight_ref, sum_ref):
    sum_ref[...] = rows_times_weight(start, rows_ref, weight_ref)


def middle_kernel(start, held_ref, rows_ref, weight_ref, sum_ref):
    sum_ref[...] = held_ref[...] + rows_times_weight(start, rows_ref, weight_ref)


def grad_hidden_step(held, rows, weight, start):
    row_count, width = rows.shape
    hidden_width = weight.shape[0]
    step = 2 * LANES
    block = pl.BlockSpec((row_count, step), lambda i: (0, i))
    specs = [
        pl.BlockSpec((row_count, width), lambda i: (0, 0)),
        pl.BlockSpec((step, weight.shape[1]), lambda i: (i, 0)),
    ]
    return pl.pallas_call(
        functools.partial(first_kernel if held is None else middle_kernel, start),
        grid=(hidden_width // step,),
        in_specs=specs if held is None else [block] + specs,
        out_specs=block,
        out_shape=jax.ShapeDtypeStruct((row_count, hidden_width), jnp.float32),
        compiler_params=params(),
        cost_estimate=cost(2 * row_count * hidden_width * width, 8 * row_count * hidden_width),
    )(*([rows, weight] if held is None else [held, rows, weight]))


def last_kernel(
    capacity, start, held_ref, rows_ref, weight_ref, hidden_ref, grad_ref, slot_ref, sum_ref
):
    grid_place = pl.program_id(0)
    grad_hidden = held_ref[...] + rows_times_weight(start, rows_ref, weight_ref)
    grad_ref[...] = grad_hidden
    product = hidden_ref[...].astype(jnp.float32) * grad_hidden
    folded = product[:, :LANES]
    for column in range(LANES, product.shape[1], LANES):
        folded = folded + product[:, column : column + LANES]

    @pl.when(grid_place == 0)
    def _():
        sum_ref[...] = folded

    @pl.when(grid_place > 0)
    def _():
        sum_ref[...] = sum_ref[...] + folded

    @pl.when(grid_place == pl.num_programs(0) - 1)
    def _():
        line = jnp.sum(sum_ref[...].T, axis=0, keepdims=True)
        slot_ref[...] = jnp.zeros_like(slot_ref)
        for source in range(slot_ref.shape[0]):
            slot_ref[source : source + 1, 0:capacity] = line[
                :, source * capacity : (source + 1) * capacity
            ]


def grad_hidden_last(held, rows, weight, start, hidden, capacity):
    row_count, width = rows.shape
    hidden_width = weight.shape[0]
    step = 2 * LANES
    block = pl.BlockSpec((row_count, step), lambda i: (0, i))
    expert_count = row_count // capacity
    return pl.pallas_call(
        functools.partial(last_kernel, capacity, start),
        grid=(hidden_width // step,),
        in_specs=[
            block,
            pl.BlockSpec((row_count, width), lambda i: (0, 0)),
            pl.BlockSpec((step, weight.shape[1]), lambda i: (i, 0)),
            block,
        ],
        out_specs=[block, pl.BlockSpec((expert_count, LANES), lambda i: (0, 0))],
        out_shape=[
            jax.ShapeDtypeStruct((row_count, hidden_width), jnp.float32),
            jax.ShapeDtypeStruct((expert_count, LANES), jnp.float32),
        ],
        scratch_shapes=[pltpu.VMEM((row_count, LANES), jnp.float32)],
        compiler_params=params(),
        cost_estimate=cost(2 * row_count * hidden_width * width, 12 * row_count * hidden_width),
    )(held, rows, weight, hidden)


def scale_kernel(grad_ref, up_scale_ref, gate_scale_ref, *refs):
    grad_gate_ref, grad_up_ref = refs[-2:]
    grad_up_ref[...] = (grad_ref[...] * up_scale_ref[...]).astype(jnp.bfloat16)
    grad_gate_ref[...] = (grad_ref[...] * gate_scale_ref[...]).astype(jnp.bfloat16)


def scaled_grads(grad_hidden, up_scale, gate_scale, earlier):
    row_count, hidden_width = grad_hidden.shape
    step = 2 * LANES
    block = pl.BlockSpec((row_count, step), lambda i: (0, i))
    return pl.pallas_call(
        scale_kernel,
        grid=(hidden_width // step,),
        in_specs=[block] * 3 + [ANY] * len(earlier),
        out_specs=[block, block],
        out_shape=[jax.ShapeDtypeStruct((row_count, hidden_width), jnp.bfloat16)] * 2,
        compiler_params=params(),
        cost_estimate=cost(2 * row_count * hidden_width, 16 * row_count * hidden_width),
    )(grad_hidden, up_scale, gate_scale, *earlier)


def route_kernel(capacity, meta_ref, near_ref, far_ref, out_ref, table_ref):
    top_count, token_count = out_ref.shape
    expert_count = table_ref.shape[0]
    half = expert_count // 2
    for offset in range(expert_count):
        block_ref = near_ref if offset < half else far_ref
        row = offset % half * expert_count + lax.axis_index("expert")
        table_ref[offset : offset + 1, :] = block_ref[pl.ds(row, 1), :]
    table = table_ref[...].T
    meta = meta_ref[...].astype(jnp.float32)
    slots = lax.broadcasted_iota(jnp.int32, (capacity, token_count), 0).astype(jnp.float32)
    for k in range(top_count):
        name, slot, prob = (meta[k + top_count * i :][:1, :] for i in range(3))
        picked = jnp.zeros((capacity, token_count), jnp.float32)
        for offset in range(expert_count):
            expert = lax.bitwise_xor(lax.axis_index("expert"), offset).astype(jnp.float32)
            wanted = jnp.where(name == expert, slot, -1.0)
            picked = picked + jnp.where(
                slots == wanted, table[:capacity, offset : offset + 1], 0.0
            )
        out_ref[k : k + 1, :] = jnp.sum(picked, axis=0, keepdims=True) / prob


def route_back(meta, near, far, expert_count, top_count, capacity):
    token_count = meta.shape[1]
    return pl.pallas_call(
        functools.partial(route_kernel, capacity),
        in_specs=[VMEM] * 3,
        out_shape=jax.ShapeDtypeStruct((top_count, token_count), jnp.float32),
        scratch_shapes=[pltpu.VMEM((expert_count, LANES), jnp.float32)],
        compiler_params=params(),
        cost_estimate=cost(1000000, 100000),
    )(meta, near, far)


def after_kernel(*refs):
    pass


def after(value, *earlier):
    return pl.pallas_call(
        after_kernel,
        in_specs=[ANY] * (1 + len(earlier)),
        out_specs=ANY,
        out_shape=jax.ShapeDtypeStruct(value.shape, value.dtype),
        input_output_aliases={0: 0},
        compiler_params=params(),
        cost_estimate=cost(64, 64),
    )(value, *earlier)


def swap(value, offset):
    size = lax.axis_size("expert")
    return lax.ppermute(value, "expert", [(place, place ^ offset) for place in range(size)])


def swap_far(value):
    size = lax.axis_size("expert")
    pairs = [(place, place ^ (4 + 2 * (place & 1))) for place in range(size)]
    return lax.ppermute(value, "expert", pairs)


def swap_groups(value, later):
    groups, places = lax.axis_size("dp"), lax.axis_size("expert")
    pairs = []
    for group in range(groups):
        for place in range(places):
            other = group ^ (1 + (place & 1) ^ (3 if later else 0))
            pairs.append((group * places + place, other * places + place))
    return lax.ppermute(value, ("dp", "expert"), pairs)


def line_shards(grad_out, probs, routes, saved_gate, saved_up, w_down):
    expert_count = lax.axis_size("expert")
    capacity = saved_gate.shape[3]
    hidden_width = saved_gate.shape[4]
    token_count, model_width = grad_out.shape
    top_count = routes.shape[1]
    row_count = expert_count * capacity

    meta = token_lines(routes.T, probs.T, expert_count)
    metas = [meta, swap(meta, 1)]
    near_rows = [grad_out, swap(grad_out, 1)]
    weight = w_down[0]
    turned, hidden, up_scale, gate_scale = hidden_parts(
        saved_gate.reshape(row_count, hidden_width), saved_up.reshape(row_count, hidden_width)
    )
    held, start = None, 0
    owns, arrived = [], []
    for chunk, width in enumerate(WIDTHS):
        far = swap_far(dispatch(metas, near_rows, capacity, top_count, start, width, True)[0])
        if chunk == 0:
            local, near = dispatch(metas, near_rows, capacity, top_count, 0, model_width, False)
            near = swap(near, 2)
        far = after(far, near, *owns)
        earlier = [] if held is None else [held, *arrived]
        rows, own, later, half = panel_parts(
            turned, [local, near, far, swap(far, 1)], capacity, start, earlier
        )
        earlier = arrived[-1:]
        if chunk + 1 < len(WIDTHS):
            held = grad_hidden_step(held, rows, weight, start)
        else:
            grad_hidden, lines = grad_hidden_last(held, rows, weight, start, hidden, capacity)
            lines = jnp.concatenate([lines, swap(lines, 1)], axis=0)
            grad_gate, grad_up = scaled_grads(grad_hidden, up_scale, gate_scale, [lines])
            lines = jnp.concatenate([lines, swap(lines, 2)], axis=0)
            earlier = earlier + [lines]
        own, half = halve(own, later, swap_groups(half, False), earlier)
        owns.append(own)
        arrived.append(swap_groups(half, True))
        start += width
    far_lines = swap(lines, 4)
    panel = total(owns, arrived, [far_lines])
    route_grad = route_back(meta, lines, far_lines, expert_count, top_count, capacity)
    return (
        grad_gate.reshape(saved_gate.shape),
        grad_up.reshape(saved_up.shape),
        panel[None],
        route_grad.T,
    )


def plain_shards(grad_out, probs, routes, saved_gate, saved_up, w_down):
    expert_count = lax.axis_size("expert")
    capacity = saved_gate.shape[3]
    hidden_width = saved_gate.shape[4]
    token_count, top_count = routes.shape
    model_width = grad_out.shape[1]
    row_count = expert_count * capacity
    flat_routes = routes.reshape(-1)
    onehot = (flat_routes[:, None] == jnp.arange(expert_count)[None, :]).astype(jnp.int32)
    before = jnp.cumsum(onehot, axis=0) - onehot
    position = flat_routes * capacity + jnp.sum(before * onehot, axis=1)
    selector = jnp.arange(row_count)[:, None] == position[None, :]
    selector = jnp.where(selector, probs.reshape(-1)[None], 0).reshape(
        row_count, token_count, top_count
    )
    sent = jnp.dot(jnp.sum(selector, axis=2), grad_out, preferred_element_type=jnp.float32)
    rows = lax.all_to_all(
        sent.astype(jnp.bfloat16).reshape(expert_count, capacity, model_width),
        "expert",
        split_axis=0,
        concat_axis=0,
        tiled=True,
    ).reshape(row_count, model_width)
    up_value = saved_up.reshape(row_count, hidden_width).astype(jnp.float32)
    activation, gate_slope = silu_parts(
        saved_gate.reshape(row_count, hidden_width).astype(jnp.float32)
    )
    hidden = (activation * up_value).astype(jnp.bfloat16)
    grad_hidden = lax.dot_general(
        rows, w_down[0], (((1,), (1,)), ((), ())), preferred_element_type=jnp.float32
    )
    slot_grad = jnp.sum(hidden.astype(jnp.float32) * grad_hidden, axis=1)
    grad_up = (grad_hidden * activation).astype(jnp.bfloat16)
    grad_gate = (grad_hidden * up_value * gate_slope).astype(jnp.bfloat16)
    whole_panel = lax.dot_general(
        hidden, rows, (((0,), (0,)), ((), ())), preferred_element_type=jnp.float32
    )
    panel = lax.psum_scatter(whole_panel, "dp", scatter_dimension=0, tiled=True)
    returned = lax.all_to_all(
        slot_grad.reshape(expert_count, capacity), "expert", split_axis=0, concat_axis=0, tiled=True
    )
    route_grad = jnp.take(returned.reshape(-1), position, axis=0).reshape(token_count, top_count)
    return (
        grad_gate.reshape(saved_gate.shape),
        grad_up.reshape(saved_up.shape),
        panel[None],
        route_grad / probs.astype(jnp.float32),
    )


def shards(grad_out, probs, routes, saved_gate, saved_up, w_down):
    expert_count = lax.axis_size("expert")
    group_count = lax.axis_size("dp")
    capacity, hidden_width = saved_gate.shape[3:]
    aligned = (
        expert_count == 8
        and group_count == 4
        and capacity % 16 == 0
        and capacity <= LANES
        and hidden_width % (16 * group_count) == 0
        and routes.shape[0] == LANES
        and grad_out.shape[1] == sum(WIDTHS)
    )
    run = line_shards if aligned else plain_shards
    return run(grad_out, probs, routes, saved_gate, saved_up, w_down)


def solution(mesh):
    return jax.shard_map(
        shards,
        mesh=mesh,
        in_specs=(
            P(("dp", "expert"), None),
            P(("dp", "expert"), None),
            P(("dp", "expert"), None),
            P("dp", "expert", None, None, None),
            P("dp", "expert", None, None, None),
            P("expert", None, None),
        ),
        out_specs=(
            P("dp", "expert", None, None, None),
            P("dp", "expert", None, None, None),
            P("expert", "dp", None),
            P(("dp", "expert"), None),
        ),
        check_vma=False,
    )
```

```python
import functools

import jax
import jax.numpy as jnp
from jax import lax
from jax.experimental import pallas as pl
from jax.experimental.pallas import tpu as pltpu
from jax.sharding import PartitionSpec as P

LANES = 128
META = 16
WIDTHS = (1152, 896)
VMEM_LIMIT = 10 * 1024 * 1024
VMEM = pl.BlockSpec(memory_space=pltpu.VMEM)
ANY = pl.BlockSpec(memory_space=pl.ANY)


def params():
    return pltpu.CompilerParams(vmem_limit_bytes=VMEM_LIMIT)


def cost(flops, moved):
    return pl.CostEstimate(flops=flops // 64, bytes_accessed=moved // 64, transcendentals=0)


def silu_parts(gate_value):
    sigmoid = jax.nn.sigmoid(gate_value)
    return (gate_value * sigmoid, sigmoid * (1.0 + gate_value * (1.0 - sigmoid)))


def tokens_kernel(expert_count, routes_ref, probs_ref, meta_ref):
    top_count, token_count = routes_ref.shape
    names = [routes_ref[k : k + 1, :] for k in range(top_count)]
    experts = lax.broadcasted_iota(jnp.int32, (expert_count, token_count), 0)
    onehots = [(experts == name).astype(jnp.float32) for name in names]
    earlier = (
        lax.broadcasted_iota(jnp.int32, (token_count, token_count), 0)
        < lax.broadcasted_iota(jnp.int32, (token_count, token_count), 1)
    ).astype(jnp.bfloat16)
    before = jnp.dot(
        sum(onehots).astype(jnp.bfloat16), earlier, preferred_element_type=jnp.float32
    )
    lines = [name.astype(jnp.float32) for name in names]
    for onehot in onehots:
        lines.append(jnp.sum(before * onehot, axis=0, keepdims=True))
        before = before + onehot
    for k in range(top_count):
        lines.append(probs_ref[k : k + 1, :].astype(jnp.float32))
    lines.append(jnp.zeros((META - len(lines), token_count), jnp.float32))
    meta_ref[...] = jnp.concatenate(lines, axis=0).astype(jnp.bfloat16)


def token_lines(routes, probs, expert_count):
    token_count = routes.shape[1]
    return pl.pallas_call(
        functools.partial(tokens_kernel, expert_count),
        in_specs=[VMEM] * 2,
        out_shape=jax.ShapeDtypeStruct((META, token_count), jnp.bfloat16),
        compiler_params=params(),
        cost_estimate=cost(100 * token_count * token_count, 4 * token_count * META),
    )(routes, probs)


def far_offset():
    return 4 + 2 * lax.bitwise_and(lax.axis_index("expert"), 1)


def chosen_rows(meta, top_count, capacity, offsets):
    token_count = meta.shape[1]
    slots = lax.broadcasted_iota(jnp.int32, (capacity, token_count), 0).astype(jnp.float32)
    parts = []
    for offset in offsets:
        target = lax.bitwise_xor(lax.axis_index("expert"), offset).astype(jnp.float32)
        part = jnp.zeros((capacity, token_count), jnp.float32)
        for k in range(top_count):
            name, slot, prob = (meta[k + top_count * i :][:1, :] for i in range(3))
            slot = jnp.where(name == target, slot, -1.0)
            part = part + jnp.where(slots == slot, prob, 0.0)
        parts.append(part)
    return jnp.concatenate(parts, axis=0).astype(jnp.bfloat16)


def dispatch_kernel(capacity, top_count, start, far, *refs):
    meta_refs, row_refs, block_refs = refs[:2], refs[2:4], refs[4:]
    if far:
        offsets = (far_offset(), far_offset() + 1)
        block_refs = refs[-1:] * 2
    else:
        offsets = (0, 2)
        block_refs = refs[-2:]
    width = block_refs[0].shape[1]
    for source in range(2):
        meta = meta_refs[source][...].astype(jnp.float32)
        rows = jnp.dot(
            chosen_rows(meta, top_count, capacity, offsets),
            row_refs[source][:, start : start + width],
            preferred_element_type=jnp.float32,
        ).astype(jnp.bfloat16)
        for step, block_ref in enumerate(block_refs):
            place = source + (2 * step if far else 0)
            block_ref[place * capacity : (place + 1) * capacity, :] = rows[
                step * capacity : (step + 1) * capacity, :
            ]


def dispatch(metas, rows, capacity, top_count, start, width, far):
    counts = (4,) if far else (2, 2)
    return pl.pallas_call(
        functools.partial(dispatch_kernel, capacity, top_count, start, far),
        in_specs=[VMEM] * 4,
        out_shape=[
            jax.ShapeDtypeStruct((count * capacity, width), jnp.bfloat16) for count in counts
        ],
        compiler_params=params(),
        cost_estimate=cost(8 * capacity * LANES * width, 8 * capacity * width),
    )(*metas, *rows)


def hidden_kernel(gate_ref, up_ref, turned_ref, hidden_ref, up_scale_ref, gate_scale_ref):
    activation, gate_slope = silu_parts(gate_ref[...].astype(jnp.float32))
    up_value = up_ref[...].astype(jnp.float32)
    hidden = activation * up_value
    turned_ref[...] = hidden.T.astype(jnp.bfloat16)
    hidden_ref[...] = hidden.astype(jnp.bfloat16)
    up_scale_ref[...] = activation
    gate_scale_ref[...] = up_value * gate_slope


def hidden_parts(gate, up):
    row_count, hidden_width = gate.shape
    step = 2 * LANES
    block = pl.BlockSpec((row_count, step), lambda i: (0, i))
    return pl.pallas_call(
        hidden_kernel,
        grid=(hidden_width // step,),
        in_specs=[block] * 2,
        out_specs=[pl.BlockSpec((step, row_count), lambda i: (i, 0))] + [block] * 3,
        out_shape=[
            jax.ShapeDtypeStruct((hidden_width, row_count), jnp.bfloat16),
            jax.ShapeDtypeStruct((row_count, hidden_width), jnp.bfloat16),
            jax.ShapeDtypeStruct((row_count, hidden_width), jnp.float32),
            jax.ShapeDtypeStruct((row_count, hidden_width), jnp.float32),
        ],
        compiler_params=params(),
        cost_estimate=cost(20 * row_count * hidden_width, 16 * row_count * hidden_width),
    )(gate, up)


def panel_kernel(capacity, start, turned_ref, *refs):
    block_refs, (rows_ref, own_ref, later_ref, sent_ref) = refs[:4], refs[-4:]
    share, width = own_ref.shape
    device = lax.axis_index("expert")
    far = far_offset()
    offsets = ((0, 1), (2, 3), (far, far + 1), (11 - far, 10 - far))
    for block, block_ref in enumerate(block_refs):
        first = 2 * capacity if block == 3 else 0
        column = start if block < 2 else 0
        for half in range(2):
            place = lax.bitwise_xor(device, offsets[block][half])
            row = pl.multiple_of(place * capacity, capacity)
            rows_ref[pl.ds(row, capacity), :] = block_ref[
                first + half * capacity : first + (half + 1) * capacity, column : column + width
            ]
    rows = rows_ref[...]

    def part(offset):
        owner = lax.bitwise_xor(lax.axis_index("dp"), offset)
        row = pl.multiple_of(owner * share, share)
        return jnp.dot(turned_ref[pl.ds(row, share), :], rows, preferred_element_type=jnp.float32)

    step = 1 + lax.bitwise_and(device, 1)
    sent_ref[:share, :] = part(step).astype(jnp.bfloat16)
    sent_ref[share:, :] = part(3).astype(jnp.bfloat16)
    later_ref[...] = part(3 - step)
    own_ref[...] = part(0)


def panel_parts(turned, blocks, capacity, start, earlier):
    hidden_width, row_count = turned.shape
    width = blocks[-1].shape[1]
    share = hidden_width // 4
    return pl.pallas_call(
        functools.partial(panel_kernel, capacity, start),
        in_specs=[VMEM] * 5 + [ANY] * len(earlier),
        out_shape=[
            jax.ShapeDtypeStruct((row_count, width), jnp.bfloat16),
            jax.ShapeDtypeStruct((share, width), jnp.float32),
            jax.ShapeDtypeStruct((share, width), jnp.float32),
            jax.ShapeDtypeStruct((2 * share, width), jnp.bfloat16),
        ],
        compiler_params=params(),
        cost_estimate=cost(
            2 * hidden_width * row_count * width, 2 * hidden_width * (row_count + width)
        ),
    )(turned, *blocks, *earlier)


def halve_kernel(own_ref, later_ref, arrived_ref, *refs):
    sum_ref, sent_ref = refs[-2:]
    share = own_ref.shape[0]
    sent_ref[...] = (later_ref[...] + arrived_ref[share:, :].astype(jnp.float32)).astype(
        jnp.bfloat16
    )
    sum_ref[...] = own_ref[...] + arrived_ref[:share, :].astype(jnp.float32)


def halve(own, later, arrived, earlier):
    return pl.pallas_call(
        halve_kernel,
        in_specs=[VMEM] * 3 + [ANY] * len(earlier),
        out_shape=[
            jax.ShapeDtypeStruct(own.shape, jnp.float32),
            jax.ShapeDtypeStruct(own.shape, jnp.bfloat16),
        ],
        compiler_params=params(),
        cost_estimate=cost(4 * own.size, 18 * own.size),
    )(own, later, arrived, *earlier)


def total_kernel(count, *refs):
    own_refs, arrived_refs = refs[:count], refs[count : 2 * count]
    total_ref, *sum_refs, semaphores = refs[-2 - count :]
    copies = []
    start = 0
    for place, (own_ref, arrived_ref) in enumerate(zip(own_refs, arrived_refs)):
        width = own_ref.shape[1]
        sum_refs[place][...] = own_ref[...] + arrived_ref[...].astype(jnp.float32)
        copies.append(
            pltpu.make_async_copy(
                sum_refs[place], total_ref.at[:, start : start + width], semaphores.at[place]
            )
        )
        copies[-1].start()
        start += width
    for copy in copies:
        copy.wait()


def total(owns, arrived, earlier):
    share = owns[0].shape[0]
    size = share * sum(own.shape[1] for own in owns)
    return pl.pallas_call(
        functools.partial(total_kernel, len(owns)),
        in_specs=[VMEM] * (2 * len(owns)) + [ANY] * len(earlier),
        out_specs=ANY,
        out_shape=jax.ShapeDtypeStruct((share, size // share), jnp.float32),
        scratch_shapes=[pltpu.VMEM(own.shape, jnp.float32) for own in owns]
        + [pltpu.SemaphoreType.DMA((len(owns),))],
        compiler_params=params(),
        cost_estimate=cost(2 * size, 10 * size),
    )(*owns, *arrived, *earlier)


def rows_times_weight(start, rows_ref, weight_ref):
    return lax.dot_general(
        rows_ref[...],
        weight_ref[:, start : start + rows_ref.shape[1]],
        (((1,), (1,)), ((), ())),
        preferred_element_type=jnp.float32,
    )


def first_kernel(start, rows_ref, weight_ref, sum_ref):
    sum_ref[...] = rows_times_weight(start, rows_ref, weight_ref)


def middle_kernel(start, held_ref, rows_ref, weight_ref, sum_ref):
    sum_ref[...] = held_ref[...] + rows_times_weight(start, rows_ref, weight_ref)


def grad_hidden_step(held, rows, weight, start):
    row_count, width = rows.shape
    hidden_width = weight.shape[0]
    step = 2 * LANES
    block = pl.BlockSpec((row_count, step), lambda i: (0, i))
    specs = [
        pl.BlockSpec((row_count, width), lambda i: (0, 0)),
        pl.BlockSpec((step, weight.shape[1]), lambda i: (i, 0)),
    ]
    return pl.pallas_call(
        functools.partial(first_kernel if held is None else middle_kernel, start),
        grid=(hidden_width // step,),
        in_specs=specs if held is None else [block] + specs,
        out_specs=block,
        out_shape=jax.ShapeDtypeStruct((row_count, hidden_width), jnp.float32),
        compiler_params=params(),
        cost_estimate=cost(2 * row_count * hidden_width * width, 8 * row_count * hidden_width),
    )(*([rows, weight] if held is None else [held, rows, weight]))


def last_kernel(
    capacity, start, held_ref, rows_ref, weight_ref, hidden_ref, grad_ref, slot_ref, sum_ref
):
    grid_place = pl.program_id(0)
    grad_hidden = held_ref[...] + rows_times_weight(start, rows_ref, weight_ref)
    grad_ref[...] = grad_hidden
    product = hidden_ref[...].astype(jnp.float32) * grad_hidden
    folded = product[:, :LANES]
    for column in range(LANES, product.shape[1], LANES):
        folded = folded + product[:, column : column + LANES]

    @pl.when(grid_place == 0)
    def _():
        sum_ref[...] = folded

    @pl.when(grid_place > 0)
    def _():
        sum_ref[...] = sum_ref[...] + folded

    @pl.when(grid_place == pl.num_programs(0) - 1)
    def _():
        line = jnp.sum(sum_ref[...].T, axis=0, keepdims=True)
        slot_ref[...] = jnp.zeros_like(slot_ref)
        for source in range(slot_ref.shape[0]):
            slot_ref[source : source + 1, 0:capacity] = line[
                :, source * capacity : (source + 1) * capacity
            ]


def grad_hidden_last(held, rows, weight, start, hidden, capacity):
    row_count, width = rows.shape
    hidden_width = weight.shape[0]
    step = 2 * LANES
    block = pl.BlockSpec((row_count, step), lambda i: (0, i))
    expert_count = row_count // capacity
    return pl.pallas_call(
        functools.partial(last_kernel, capacity, start),
        grid=(hidden_width // step,),
        in_specs=[
            block,
            pl.BlockSpec((row_count, width), lambda i: (0, 0)),
            pl.BlockSpec((step, weight.shape[1]), lambda i: (i, 0)),
            block,
        ],
        out_specs=[block, pl.BlockSpec((expert_count, LANES), lambda i: (0, 0))],
        out_shape=[
            jax.ShapeDtypeStruct((row_count, hidden_width), jnp.float32),
            jax.ShapeDtypeStruct((expert_count, LANES), jnp.float32),
        ],
        scratch_shapes=[pltpu.VMEM((row_count, LANES), jnp.float32)],
        compiler_params=params(),
        cost_estimate=cost(2 * row_count * hidden_width * width, 12 * row_count * hidden_width),
    )(held, rows, weight, hidden)


def scale_kernel(grad_ref, up_scale_ref, gate_scale_ref, *refs):
    grad_gate_ref, grad_up_ref = refs[-2:]
    grad_up_ref[...] = (grad_ref[...] * up_scale_ref[...]).astype(jnp.bfloat16)
    grad_gate_ref[...] = (grad_ref[...] * gate_scale_ref[...]).astype(jnp.bfloat16)


def scaled_grads(grad_hidden, up_scale, gate_scale, earlier):
    row_count, hidden_width = grad_hidden.shape
    step = 2 * LANES
    block = pl.BlockSpec((row_count, step), lambda i: (0, i))
    return pl.pallas_call(
        scale_kernel,
        grid=(hidden_width // step,),
        in_specs=[block] * 3 + [ANY] * len(earlier),
        out_specs=[block, block],
        out_shape=[jax.ShapeDtypeStruct((row_count, hidden_width), jnp.bfloat16)] * 2,
        compiler_params=params(),
        cost_estimate=cost(2 * row_count * hidden_width, 16 * row_count * hidden_width),
    )(grad_hidden, up_scale, gate_scale, *earlier)


def route_kernel(capacity, meta_ref, near_ref, far_ref, out_ref, table_ref):
    top_count, token_count = out_ref.shape
    expert_count = table_ref.shape[0]
    half = expert_count // 2
    for offset in range(expert_count):
        block_ref = near_ref if offset < half else far_ref
        row = offset % half * expert_count + lax.axis_index("expert")
        table_ref[offset : offset + 1, :] = block_ref[pl.ds(row, 1), :]
    table = table_ref[...].T
    meta = meta_ref[...].astype(jnp.float32)
    slots = lax.broadcasted_iota(jnp.int32, (capacity, token_count), 0).astype(jnp.float32)
    for k in range(top_count):
        name, slot, prob = (meta[k + top_count * i :][:1, :] for i in range(3))
        picked = jnp.zeros((capacity, token_count), jnp.float32)
        for offset in range(expert_count):
            expert = lax.bitwise_xor(lax.axis_index("expert"), offset).astype(jnp.float32)
            wanted = jnp.where(name == expert, slot, -1.0)
            picked = picked + jnp.where(
                slots == wanted, table[:capacity, offset : offset + 1], 0.0
            )
        out_ref[k : k + 1, :] = jnp.sum(picked, axis=0, keepdims=True) / prob


def route_back(meta, near, far, expert_count, top_count, capacity):
    token_count = meta.shape[1]
    return pl.pallas_call(
        functools.partial(route_kernel, capacity),
        in_specs=[VMEM] * 3,
        out_shape=jax.ShapeDtypeStruct((top_count, token_count), jnp.float32),
        scratch_shapes=[pltpu.VMEM((expert_count, LANES), jnp.float32)],
        compiler_params=params(),
        cost_estimate=cost(1000000, 100000),
    )(meta, near, far)


def after_kernel(*refs):
    pass


def after(value, *earlier):
    return pl.pallas_call(
        after_kernel,
        in_specs=[ANY] * (1 + len(earlier)),
        out_specs=ANY,
        out_shape=jax.ShapeDtypeStruct(value.shape, value.dtype),
        input_output_aliases={0: 0},
        compiler_params=params(),
        cost_estimate=cost(64, 64),
    )(value, *earlier)


def swap(value, offset):
    size = lax.axis_size("expert")
    return lax.ppermute(value, "expert", [(place, place ^ offset) for place in range(size)])


def swap_far(value):
    size = lax.axis_size("expert")
    pairs = [(place, place ^ (4 + 2 * (place & 1))) for place in range(size)]
    return lax.ppermute(value, "expert", pairs)


def swap_groups(value, later):
    groups, places = lax.axis_size("dp"), lax.axis_size("expert")
    pairs = []
    for group in range(groups):
        for place in range(places):
            other = group ^ (1 + (place & 1) ^ (3 if later else 0))
            pairs.append((group * places + place, other * places + place))
    return lax.ppermute(value, ("dp", "expert"), pairs)


def line_shards(grad_out, probs, routes, saved_gate, saved_up, w_down):
    expert_count = lax.axis_size("expert")
    capacity = saved_gate.shape[3]
    hidden_width = saved_gate.shape[4]
    token_count, model_width = grad_out.shape
    top_count = routes.shape[1]
    row_count = expert_count * capacity

    near_rows = [grad_out, swap(grad_out, 1)]
    routes, probs = routes.T, probs.T
    meta = token_lines(routes, probs, expert_count)
    metas = [meta, token_lines(swap(routes, 1), swap(probs, 1), expert_count)]
    weight = w_down[0]
    turned, hidden, up_scale, gate_scale = hidden_parts(
        saved_gate.reshape(row_count, hidden_width), saved_up.reshape(row_count, hidden_width)
    )
    held, start = None, 0
    owns, arrived = [], []
    for chunk, width in enumerate(WIDTHS):
        far = swap_far(dispatch(metas, near_rows, capacity, top_count, start, width, True)[0])
        if chunk == 0:
            local, near = dispatch(metas, near_rows, capacity, top_count, 0, model_width, False)
            near = swap(near, 2)
        far = after(far, near, *owns)
        earlier = [] if held is None else [held, *arrived]
        rows, own, later, half = panel_parts(
            turned, [local, near, far, swap(far, 1)], capacity, start, earlier
        )
        earlier = arrived[-1:]
        if chunk + 1 < len(WIDTHS):
            held = grad_hidden_step(held, rows, weight, start)
        else:
            grad_hidden, lines = grad_hidden_last(held, rows, weight, start, hidden, capacity)
            lines = jnp.concatenate([lines, swap(lines, 1)], axis=0)
            grad_gate, grad_up = scaled_grads(grad_hidden, up_scale, gate_scale, [lines])
            lines = jnp.concatenate([lines, swap(lines, 2)], axis=0)
            earlier = earlier + [lines]
        own, half = halve(own, later, swap_groups(half, False), earlier)
        owns.append(own)
        arrived.append(swap_groups(half, True))
        start += width
    far_lines = swap(lines, 4)
    panel = total(owns, arrived, [far_lines])
    route_grad = route_back(meta, lines, far_lines, expert_count, top_count, capacity)
    return (
        grad_gate.reshape(saved_gate.shape),
        grad_up.reshape(saved_up.shape),
        panel[None],
        route_grad.T,
    )


def plain_shards(grad_out, probs, routes, saved_gate, saved_up, w_down):
    expert_count = lax.axis_size("expert")
    capacity = saved_gate.shape[3]
    hidden_width = saved_gate.shape[4]
    token_count, top_count = routes.shape
    model_width = grad_out.shape[1]
    row_count = expert_count * capacity
    flat_routes = routes.reshape(-1)
    onehot = (flat_routes[:, None] == jnp.arange(expert_count)[None, :]).astype(jnp.int32)
    before = jnp.cumsum(onehot, axis=0) - onehot
    position = flat_routes * capacity + jnp.sum(before * onehot, axis=1)
    selector = jnp.arange(row_count)[:, None] == position[None, :]
    selector = jnp.where(selector, probs.reshape(-1)[None], 0).reshape(
        row_count, token_count, top_count
    )
    sent = jnp.dot(jnp.sum(selector, axis=2), grad_out, preferred_element_type=jnp.float32)
    rows = lax.all_to_all(
        sent.astype(jnp.bfloat16).reshape(expert_count, capacity, model_width),
        "expert",
        split_axis=0,
        concat_axis=0,
        tiled=True,
    ).reshape(row_count, model_width)
    up_value = saved_up.reshape(row_count, hidden_width).astype(jnp.float32)
    activation, gate_slope = silu_parts(
        saved_gate.reshape(row_count, hidden_width).astype(jnp.float32)
    )
    hidden = (activation * up_value).astype(jnp.bfloat16)
    grad_hidden = lax.dot_general(
        rows, w_down[0], (((1,), (1,)), ((), ())), preferred_element_type=jnp.float32
    )
    slot_grad = jnp.sum(hidden.astype(jnp.float32) * grad_hidden, axis=1)
    grad_up = (grad_hidden * activation).astype(jnp.bfloat16)
    grad_gate = (grad_hidden * up_value * gate_slope).astype(jnp.bfloat16)
    whole_panel = lax.dot_general(
        hidden, rows, (((0,), (0,)), ((), ())), preferred_element_type=jnp.float32
    )
    panel = lax.psum_scatter(whole_panel, "dp", scatter_dimension=0, tiled=True)
    returned = lax.all_to_all(
        slot_grad.reshape(expert_count, capacity), "expert", split_axis=0, concat_axis=0, tiled=True
    )
    route_grad = jnp.take(returned.reshape(-1), position, axis=0).reshape(token_count, top_count)
    return (
        grad_gate.reshape(saved_gate.shape),
        grad_up.reshape(saved_up.shape),
        panel[None],
        route_grad / probs.astype(jnp.float32),
    )


def shards(grad_out, probs, routes, saved_gate, saved_up, w_down):
    expert_count = lax.axis_size("expert")
    group_count = lax.axis_size("dp")
    capacity, hidden_width = saved_gate.shape[3:]
    aligned = (
        expert_count == 8
        and group_count == 4
        and capacity % 16 == 0
        and capacity <= LANES
        and hidden_width % (16 * group_count) == 0
        and routes.shape[0] == LANES
        and grad_out.shape[1] == sum(WIDTHS)
    )
    run = line_shards if aligned else plain_shards
    return run(grad_out, probs, routes, saved_gate, saved_up, w_down)


def solution(mesh):
    return jax.shard_map(
        shards,
        mesh=mesh,
        in_specs=(
            P(("dp", "expert"), None),
            P(("dp", "expert"), None),
            P(("dp", "expert"), None),
            P("dp", "expert", None, None, None),
            P("dp", "expert", None, None, None),
            P("expert", None, None),
        ),
        out_specs=(
            P("dp", "expert", None, None, None),
            P("dp", "expert", None, None, None),
            P("expert", "dp", None),
            P(("dp", "expert"), None),
        ),
        check_vma=False,
    )
```

```python
import functools

import jax
import jax.numpy as jnp
from jax import lax
from jax.experimental import pallas as pl
from jax.experimental.pallas import tpu as pltpu
from jax.sharding import PartitionSpec as P

LANES = 128
META = 16
WIDTHS = (1152, 896)
VMEM_LIMIT = 10 * 1024 * 1024
VMEM = pl.BlockSpec(memory_space=pltpu.VMEM)
ANY = pl.BlockSpec(memory_space=pl.ANY)


def params():
    return pltpu.CompilerParams(vmem_limit_bytes=VMEM_LIMIT)


def cost(flops, moved):
    return pl.CostEstimate(flops=flops // 64, bytes_accessed=moved // 64, transcendentals=0)


def silu_parts(gate_value):
    sigmoid = jax.nn.sigmoid(gate_value)
    return (gate_value * sigmoid, sigmoid * (1.0 + gate_value * (1.0 - sigmoid)))


def tokens_kernel(expert_count, routes_ref, probs_ref, meta_ref):
    top_count, token_count = routes_ref.shape
    names = [routes_ref[k : k + 1, :] for k in range(top_count)]
    experts = lax.broadcasted_iota(jnp.int32, (expert_count, token_count), 0)
    onehots = [(experts == name).astype(jnp.float32) for name in names]
    earlier = (
        lax.broadcasted_iota(jnp.int32, (token_count, token_count), 0)
        < lax.broadcasted_iota(jnp.int32, (token_count, token_count), 1)
    ).astype(jnp.bfloat16)
    before = jnp.dot(
        sum(onehots).astype(jnp.bfloat16), earlier, preferred_element_type=jnp.float32
    )
    lines = [name.astype(jnp.float32) for name in names]
    for onehot in onehots:
        lines.append(jnp.sum(before * onehot, axis=0, keepdims=True))
        before = before + onehot
    for k in range(top_count):
        lines.append(probs_ref[k : k + 1, :].astype(jnp.float32))
    lines.append(jnp.zeros((META - len(lines), token_count), jnp.float32))
    meta_ref[...] = jnp.concatenate(lines, axis=0).astype(jnp.bfloat16)


def token_lines(routes, probs, expert_count):
    token_count = routes.shape[1]
    return pl.pallas_call(
        functools.partial(tokens_kernel, expert_count),
        in_specs=[VMEM] * 2,
        out_shape=jax.ShapeDtypeStruct((META, token_count), jnp.bfloat16),
        compiler_params=params(),
        cost_estimate=cost(100 * token_count * token_count, 4 * token_count * META),
    )(routes, probs)


def far_offset():
    return 4 + 2 * lax.bitwise_and(lax.axis_index("expert"), 1)


def chosen_rows(meta, top_count, capacity, offsets):
    token_count = meta.shape[1]
    slots = lax.broadcasted_iota(jnp.int32, (capacity, token_count), 0).astype(jnp.float32)
    parts = []
    for offset in offsets:
        target = lax.bitwise_xor(lax.axis_index("expert"), offset).astype(jnp.float32)
        part = jnp.zeros((capacity, token_count), jnp.float32)
        for k in range(top_count):
            name, slot, prob = (meta[k + top_count * i :][:1, :] for i in range(3))
            slot = jnp.where(name == target, slot, -1.0)
            part = part + jnp.where(slots == slot, prob, 0.0)
        parts.append(part)
    return jnp.concatenate(parts, axis=0).astype(jnp.bfloat16)


def dispatch_kernel(capacity, top_count, start, far, *refs):
    meta_refs, row_refs, block_refs = refs[:2], refs[2:4], refs[4:]
    if far:
        offsets = (far_offset(), far_offset() + 1)
        block_refs = refs[-1:] * 2
    else:
        offsets = (0, 2)
        block_refs = refs[-2:]
    width = block_refs[0].shape[1]
    for source in range(2):
        meta = meta_refs[source][...].astype(jnp.float32)
        rows = jnp.dot(
            chosen_rows(meta, top_count, capacity, offsets),
            row_refs[source][:, start : start + width],
            preferred_element_type=jnp.float32,
        ).astype(jnp.bfloat16)
        for step, block_ref in enumerate(block_refs):
            place = source + (2 * step if far else 0)
            block_ref[place * capacity : (place + 1) * capacity, :] = rows[
                step * capacity : (step + 1) * capacity, :
            ]


def dispatch(metas, rows, capacity, top_count, start, width, far):
    counts = (4,) if far else (2, 2)
    return pl.pallas_call(
        functools.partial(dispatch_kernel, capacity, top_count, start, far),
        in_specs=[VMEM] * 4,
        out_shape=[
            jax.ShapeDtypeStruct((count * capacity, width), jnp.bfloat16) for count in counts
        ],
        compiler_params=params(),
        cost_estimate=cost(8 * capacity * LANES * width, 8 * capacity * width),
    )(*metas, *rows)


def hidden_kernel(gate_ref, up_ref, turned_ref, hidden_ref, up_scale_ref, gate_scale_ref):
    activation, gate_slope = silu_parts(gate_ref[...].astype(jnp.float32))
    up_value = up_ref[...].astype(jnp.float32)
    hidden = activation * up_value
    turned_ref[...] = hidden.T.astype(jnp.bfloat16)
    hidden_ref[...] = hidden.astype(jnp.bfloat16)
    up_scale_ref[...] = activation
    gate_scale_ref[...] = up_value * gate_slope


def hidden_parts(gate, up):
    row_count, hidden_width = gate.shape
    step = 2 * LANES
    block = pl.BlockSpec((row_count, step), lambda i: (0, i))
    return pl.pallas_call(
        hidden_kernel,
        grid=(hidden_width // step,),
        in_specs=[block] * 2,
        out_specs=[pl.BlockSpec((step, row_count), lambda i: (i, 0))] + [block] * 3,
        out_shape=[
            jax.ShapeDtypeStruct((hidden_width, row_count), jnp.bfloat16),
            jax.ShapeDtypeStruct((row_count, hidden_width), jnp.bfloat16),
            jax.ShapeDtypeStruct((row_count, hidden_width), jnp.float32),
            jax.ShapeDtypeStruct((row_count, hidden_width), jnp.float32),
        ],
        compiler_params=params(),
        cost_estimate=cost(20 * row_count * hidden_width, 16 * row_count * hidden_width),
    )(gate, up)


def panel_kernel(capacity, start, turned_ref, *refs):
    block_refs, (rows_ref, own_ref, later_ref, sent_ref) = refs[:4], refs[-4:]
    share, width = own_ref.shape
    device = lax.axis_index("expert")
    far = far_offset()
    offsets = ((0, 1), (2, 3), (far, far + 1), (11 - far, 10 - far))
    for block, block_ref in enumerate(block_refs):
        first = 2 * capacity if block == 3 else 0
        column = start if block < 2 else 0
        for half in range(2):
            place = lax.bitwise_xor(device, offsets[block][half])
            row = pl.multiple_of(place * capacity, capacity)
            rows_ref[pl.ds(row, capacity), :] = block_ref[
                first + half * capacity : first + (half + 1) * capacity, column : column + width
            ]
    rows = rows_ref[...]

    def part(offset):
        owner = lax.bitwise_xor(lax.axis_index("dp"), offset)
        row = pl.multiple_of(owner * share, share)
        return jnp.dot(turned_ref[pl.ds(row, share), :], rows, preferred_element_type=jnp.float32)

    step = 1 + lax.bitwise_and(device, 1)
    sent_ref[:share, :] = part(step).astype(jnp.bfloat16)
    sent_ref[share:, :] = part(3).astype(jnp.bfloat16)
    later_ref[...] = part(3 - step)
    own_ref[...] = part(0)


def panel_parts(turned, blocks, capacity, start, earlier):
    hidden_width, row_count = turned.shape
    width = blocks[-1].shape[1]
    share = hidden_width // 4
    return pl.pallas_call(
        functools.partial(panel_kernel, capacity, start),
        in_specs=[VMEM] * 5 + [ANY] * len(earlier),
        out_shape=[
            jax.ShapeDtypeStruct((row_count, width), jnp.bfloat16),
            jax.ShapeDtypeStruct((share, width), jnp.float32),
            jax.ShapeDtypeStruct((share, width), jnp.float32),
            jax.ShapeDtypeStruct((2 * share, width), jnp.bfloat16),
        ],
        compiler_params=params(),
        cost_estimate=cost(
            2 * hidden_width * row_count * width, 2 * hidden_width * (row_count + width)
        ),
    )(turned, *blocks, *earlier)


def halve_kernel(own_ref, later_ref, arrived_ref, *refs):
    sum_ref, sent_ref = refs[-2:]
    share = own_ref.shape[0]
    sent_ref[...] = (later_ref[...] + arrived_ref[share:, :].astype(jnp.float32)).astype(
        jnp.bfloat16
    )
    sum_ref[...] = own_ref[...] + arrived_ref[:share, :].astype(jnp.float32)


def halve(own, later, arrived, earlier):
    return pl.pallas_call(
        halve_kernel,
        in_specs=[VMEM] * 3 + [ANY] * len(earlier),
        out_shape=[
            jax.ShapeDtypeStruct(own.shape, jnp.float32),
            jax.ShapeDtypeStruct(own.shape, jnp.bfloat16),
        ],
        compiler_params=params(),
        cost_estimate=cost(4 * own.size, 18 * own.size),
    )(own, later, arrived, *earlier)


def total_kernel(start, *refs):
    own_ref, arrived_ref = refs[:2]
    total_ref, sum_ref, semaphore = refs[-3:]
    sum_ref[...] = own_ref[...] + arrived_ref[...].astype(jnp.float32)
    copy = pltpu.make_async_copy(
        sum_ref, total_ref.at[:, start : start + sum_ref.shape[1]], semaphore
    )
    copy.start()
    copy.wait()


def total(held, own, arrived, start, model_width, earlier):
    share, width = own.shape
    extra = ([] if held is None else [held]) + list(earlier)
    return pl.pallas_call(
        functools.partial(total_kernel, start),
        in_specs=[VMEM] * 2 + [ANY] * len(extra),
        out_specs=ANY,
        out_shape=jax.ShapeDtypeStruct((share, model_width), jnp.float32),
        scratch_shapes=[pltpu.VMEM((share, width), jnp.float32), pltpu.SemaphoreType.DMA],
        input_output_aliases={} if held is None else {2: 0},
        compiler_params=params(),
        cost_estimate=cost(2 * share * width, 10 * share * width),
    )(own, arrived, *extra)


def rows_times_weight(start, rows_ref, weight_ref):
    return lax.dot_general(
        rows_ref[...],
        weight_ref[:, start : start + rows_ref.shape[1]],
        (((1,), (1,)), ((), ())),
        preferred_element_type=jnp.float32,
    )


def first_kernel(start, rows_ref, weight_ref, sum_ref):
    sum_ref[...] = rows_times_weight(start, rows_ref, weight_ref)


def middle_kernel(start, held_ref, rows_ref, weight_ref, sum_ref):
    sum_ref[...] = held_ref[...] + rows_times_weight(start, rows_ref, weight_ref)


def grad_hidden_step(held, rows, weight, start):
    row_count, width = rows.shape
    hidden_width = weight.shape[0]
    step = 2 * LANES
    block = pl.BlockSpec((row_count, step), lambda i: (0, i))
    specs = [
        pl.BlockSpec((row_count, width), lambda i: (0, 0)),
        pl.BlockSpec((step, weight.shape[1]), lambda i: (i, 0)),
    ]
    return pl.pallas_call(
        functools.partial(first_kernel if held is None else middle_kernel, start),
        grid=(hidden_width // step,),
        in_specs=specs if held is None else [block] + specs,
        out_specs=block,
        out_shape=jax.ShapeDtypeStruct((row_count, hidden_width), jnp.float32),
        compiler_params=params(),
        cost_estimate=cost(2 * row_count * hidden_width * width, 8 * row_count * hidden_width),
    )(*([rows, weight] if held is None else [held, rows, weight]))


def last_kernel(
    capacity, start, held_ref, rows_ref, weight_ref, hidden_ref, grad_ref, slot_ref, sum_ref
):
    grid_place = pl.program_id(0)
    grad_hidden = held_ref[...] + rows_times_weight(start, rows_ref, weight_ref)
    grad_ref[...] = grad_hidden
    product = hidden_ref[...].astype(jnp.float32) * grad_hidden
    folded = product[:, :LANES]
    for column in range(LANES, product.shape[1], LANES):
        folded = folded + product[:, column : column + LANES]

    @pl.when(grid_place == 0)
    def _():
        sum_ref[...] = folded

    @pl.when(grid_place > 0)
    def _():
        sum_ref[...] = sum_ref[...] + folded

    @pl.when(grid_place == pl.num_programs(0) - 1)
    def _():
        line = jnp.sum(sum_ref[...].T, axis=0, keepdims=True)
        slot_ref[...] = jnp.zeros_like(slot_ref)
        for source in range(slot_ref.shape[0]):
            slot_ref[source : source + 1, 0:capacity] = line[
                :, source * capacity : (source + 1) * capacity
            ]


def grad_hidden_last(held, rows, weight, start, hidden, capacity):
    row_count, width = rows.shape
    hidden_width = weight.shape[0]
    step = 2 * LANES
    block = pl.BlockSpec((row_count, step), lambda i: (0, i))
    expert_count = row_count // capacity
    return pl.pallas_call(
        functools.partial(last_kernel, capacity, start),
        grid=(hidden_width // step,),
        in_specs=[
            block,
            pl.BlockSpec((row_count, width), lambda i: (0, 0)),
            pl.BlockSpec((step, weight.shape[1]), lambda i: (i, 0)),
            block,
        ],
        out_specs=[block, pl.BlockSpec((expert_count, LANES), lambda i: (0, 0))],
        out_shape=[
            jax.ShapeDtypeStruct((row_count, hidden_width), jnp.float32),
            jax.ShapeDtypeStruct((expert_count, LANES), jnp.float32),
        ],
        scratch_shapes=[pltpu.VMEM((row_count, LANES), jnp.float32)],
        compiler_params=params(),
        cost_estimate=cost(2 * row_count * hidden_width * width, 12 * row_count * hidden_width),
    )(held, rows, weight, hidden)


def scale_kernel(grad_ref, up_scale_ref, gate_scale_ref, *refs):
    grad_gate_ref, grad_up_ref = refs[-2:]
    grad_up_ref[...] = (grad_ref[...] * up_scale_ref[...]).astype(jnp.bfloat16)
    grad_gate_ref[...] = (grad_ref[...] * gate_scale_ref[...]).astype(jnp.bfloat16)


def scaled_grads(grad_hidden, up_scale, gate_scale, earlier):
    row_count, hidden_width = grad_hidden.shape
    step = 2 * LANES
    block = pl.BlockSpec((row_count, step), lambda i: (0, i))
    return pl.pallas_call(
        scale_kernel,
        grid=(hidden_width // step,),
        in_specs=[block] * 3 + [ANY] * len(earlier),
        out_specs=[block, block],
        out_shape=[jax.ShapeDtypeStruct((row_count, hidden_width), jnp.bfloat16)] * 2,
        compiler_params=params(),
        cost_estimate=cost(2 * row_count * hidden_width, 16 * row_count * hidden_width),
    )(grad_hidden, up_scale, gate_scale, *earlier)


def route_kernel(capacity, meta_ref, near_ref, far_ref, out_ref, table_ref):
    top_count, token_count = out_ref.shape
    expert_count = table_ref.shape[0]
    half = expert_count // 2
    for offset in range(expert_count):
        block_ref = near_ref if offset < half else far_ref
        row = offset % half * expert_count + lax.axis_index("expert")
        table_ref[offset : offset + 1, :] = block_ref[pl.ds(row, 1), :]
    table = table_ref[...].T
    meta = meta_ref[...].astype(jnp.float32)
    slots = lax.broadcasted_iota(jnp.int32, (capacity, token_count), 0).astype(jnp.float32)
    for k in range(top_count):
        name, slot, prob = (meta[k + top_count * i :][:1, :] for i in range(3))
        picked = jnp.zeros((capacity, token_count), jnp.float32)
        for offset in range(expert_count):
            expert = lax.bitwise_xor(lax.axis_index("expert"), offset).astype(jnp.float32)
            wanted = jnp.where(name == expert, slot, -1.0)
            picked = picked + jnp.where(
                slots == wanted, table[:capacity, offset : offset + 1], 0.0
            )
        out_ref[k : k + 1, :] = jnp.sum(picked, axis=0, keepdims=True) / prob


def route_back(meta, near, far, expert_count, top_count, capacity):
    token_count = meta.shape[1]
    return pl.pallas_call(
        functools.partial(route_kernel, capacity),
        in_specs=[VMEM] * 3,
        out_shape=jax.ShapeDtypeStruct((top_count, token_count), jnp.float32),
        scratch_shapes=[pltpu.VMEM((expert_count, LANES), jnp.float32)],
        compiler_params=params(),
        cost_estimate=cost(1000000, 100000),
    )(meta, near, far)


def after_kernel(*refs):
    pass


def after(value, *earlier):
    return pl.pallas_call(
        after_kernel,
        in_specs=[ANY] * (1 + len(earlier)),
        out_specs=ANY,
        out_shape=jax.ShapeDtypeStruct(value.shape, value.dtype),
        input_output_aliases={0: 0},
        compiler_params=params(),
        cost_estimate=cost(64, 64),
    )(value, *earlier)


def swap(value, offset):
    size = lax.axis_size("expert")
    return lax.ppermute(value, "expert", [(place, place ^ offset) for place in range(size)])


def swap_far(value):
    size = lax.axis_size("expert")
    pairs = [(place, place ^ (4 + 2 * (place & 1))) for place in range(size)]
    return lax.ppermute(value, "expert", pairs)


def swap_groups(value, later):
    groups, places = lax.axis_size("dp"), lax.axis_size("expert")
    pairs = []
    for group in range(groups):
        for place in range(places):
            other = group ^ (1 + (place & 1) ^ (3 if later else 0))
            pairs.append((group * places + place, other * places + place))
    return lax.ppermute(value, ("dp", "expert"), pairs)


def line_shards(grad_out, probs, routes, saved_gate, saved_up, w_down):
    expert_count = lax.axis_size("expert")
    capacity = saved_gate.shape[3]
    hidden_width = saved_gate.shape[4]
    token_count, model_width = grad_out.shape
    top_count = routes.shape[1]
    row_count = expert_count * capacity

    near_rows = [grad_out, swap(grad_out, 1)]
    routes, probs = routes.T, probs.T
    meta = token_lines(routes, probs, expert_count)
    metas = [meta, token_lines(swap(routes, 1), swap(probs, 1), expert_count)]
    weight = w_down[0]
    turned, hidden, up_scale, gate_scale = hidden_parts(
        saved_gate.reshape(row_count, hidden_width), saved_up.reshape(row_count, hidden_width)
    )
    held, start = None, 0
    owns, arrived = [], []
    for chunk, width in enumerate(WIDTHS):
        far = swap_far(dispatch(metas, near_rows, capacity, top_count, start, width, True)[0])
        if chunk == 0:
            local, near = dispatch(metas, near_rows, capacity, top_count, 0, model_width, False)
            near = swap(near, 2)
        far = after(far, near, *owns)
        earlier = [] if held is None else [held, *arrived]
        rows, own, later, half = panel_parts(
            turned, [local, near, far, swap(far, 1)], capacity, start, earlier
        )
        earlier = arrived[-1:]
        if chunk + 1 < len(WIDTHS):
            held = grad_hidden_step(held, rows, weight, start)
        else:
            grad_hidden, lines = grad_hidden_last(held, rows, weight, start, hidden, capacity)
            lines = jnp.concatenate([lines, swap(lines, 1)], axis=0)
            grad_gate, grad_up = scaled_grads(grad_hidden, up_scale, gate_scale, [lines])
            lines = jnp.concatenate([lines, swap(lines, 2)], axis=0)
            earlier = earlier + [lines]
        own, half = halve(own, later, swap_groups(half, False), earlier)
        owns.append(own)
        arrived.append(swap_groups(half, True))
        start += width
    far_lines = swap(lines, 4)
    panel, start = None, 0
    for own, half in zip(owns, arrived):
        last = start + own.shape[1] == model_width
        panel = total(panel, own, half, start, model_width, [far_lines] if last else [])
        start += own.shape[1]
    route_grad = route_back(meta, lines, far_lines, expert_count, top_count, capacity)
    return (
        grad_gate.reshape(saved_gate.shape),
        grad_up.reshape(saved_up.shape),
        panel[None],
        route_grad.T,
    )


def plain_shards(grad_out, probs, routes, saved_gate, saved_up, w_down):
    expert_count = lax.axis_size("expert")
    capacity = saved_gate.shape[3]
    hidden_width = saved_gate.shape[4]
    token_count, top_count = routes.shape
    model_width = grad_out.shape[1]
    row_count = expert_count * capacity
    flat_routes = routes.reshape(-1)
    onehot = (flat_routes[:, None] == jnp.arange(expert_count)[None, :]).astype(jnp.int32)
    before = jnp.cumsum(onehot, axis=0) - onehot
    position = flat_routes * capacity + jnp.sum(before * onehot, axis=1)
    selector = jnp.arange(row_count)[:, None] == position[None, :]
    selector = jnp.where(selector, probs.reshape(-1)[None], 0).reshape(
        row_count, token_count, top_count
    )
    sent = jnp.dot(jnp.sum(selector, axis=2), grad_out, preferred_element_type=jnp.float32)
    rows = lax.all_to_all(
        sent.astype(jnp.bfloat16).reshape(expert_count, capacity, model_width),
        "expert",
        split_axis=0,
        concat_axis=0,
        tiled=True,
    ).reshape(row_count, model_width)
    up_value = saved_up.reshape(row_count, hidden_width).astype(jnp.float32)
    activation, gate_slope = silu_parts(
        saved_gate.reshape(row_count, hidden_width).astype(jnp.float32)
    )
    hidden = (activation * up_value).astype(jnp.bfloat16)
    grad_hidden = lax.dot_general(
        rows, w_down[0], (((1,), (1,)), ((), ())), preferred_element_type=jnp.float32
    )
    slot_grad = jnp.sum(hidden.astype(jnp.float32) * grad_hidden, axis=1)
    grad_up = (grad_hidden * activation).astype(jnp.bfloat16)
    grad_gate = (grad_hidden * up_value * gate_slope).astype(jnp.bfloat16)
    whole_panel = lax.dot_general(
        hidden, rows, (((0,), (0,)), ((), ())), preferred_element_type=jnp.float32
    )
    panel = lax.psum_scatter(whole_panel, "dp", scatter_dimension=0, tiled=True)
    returned = lax.all_to_all(
        slot_grad.reshape(expert_count, capacity), "expert", split_axis=0, concat_axis=0, tiled=True
    )
    route_grad = jnp.take(returned.reshape(-1), position, axis=0).reshape(token_count, top_count)
    return (
        grad_gate.reshape(saved_gate.shape),
        grad_up.reshape(saved_up.shape),
        panel[None],
        route_grad / probs.astype(jnp.float32),
    )


def shards(grad_out, probs, routes, saved_gate, saved_up, w_down):
    expert_count = lax.axis_size("expert")
    group_count = lax.axis_size("dp")
    capacity, hidden_width = saved_gate.shape[3:]
    aligned = (
        expert_count == 8
        and group_count == 4
        and capacity % 16 == 0
        and capacity <= LANES
        and hidden_width % (16 * group_count) == 0
        and routes.shape[0] == LANES
        and grad_out.shape[1] == sum(WIDTHS)
    )
    run = line_shards if aligned else plain_shards
    return run(grad_out, probs, routes, saved_gate, saved_up, w_down)


def solution(mesh):
    return jax.shard_map(
        shards,
        mesh=mesh,
        in_specs=(
            P(("dp", "expert"), None),
            P(("dp", "expert"), None),
            P(("dp", "expert"), None),
            P("dp", "expert", None, None, None),
            P("dp", "expert", None, None, None),
            P("expert", None, None),
        ),
        out_specs=(
            P("dp", "expert", None, None, None),
            P("dp", "expert", None, None, None),
            P("expert", "dp", None),
            P(("dp", "expert"), None),
        ),
        check_vma=False,
    )
```
